32 devices in a mesh: layer: 8 (over y, x, core), feat: 4 (over z).
Axes of the slice: x: 2, y: 2, z: 4, core: 2. Of those that a mesh axis runs over, the one named last changes fastest.
Arguments:
- tokens_in: bfloat16 [512, 4096], P('feat', 'layer'), may hold values from -6 to 6
- targets: bfloat16 [512, 4096], P('feat', 'layer'), may hold values from -6 to 6
- enc_weight: bfloat16 [2048, 32768], P(None, ('layer', 'feat')), may hold values from -0.125 to 0.125
- enc_bias: float32 [32768], P(('layer', 'feat')), may hold values from -1 to 0.5
- dec_weight: bfloat16 [2, 32768, 2048], P(None, ('layer', 'feat')), may hold values from -0.046875 to 0.046875
Outputs:
- recon_error: float32 [512, 4096], P('feat', 'layer')
- mean_square: float32 [], replicated
- enc_grad: bfloat16 [2048, 32768], P(None, ('layer', 'feat'))
- bias_grad: float32 [32768], P(('layer', 'feat'))
- dec_grad: bfloat16 [2, 32768, 2048], P(None, ('layer', 'feat'))
The draws below stay inside these ranges and needn't reach their ends.
All inputs are finite; a program needn't handle non-finite values.
Results may differ from the reference program's by a relative error of at most 0.02.
Values may be sent and summed in bfloat16 or wider, within the bound.
No kernel may reach another device: no remote copies, remote signals or barrier semaphores. Data moves between devices by JAX's collectives and lax.ppermute only.
A program may use at most 128 MiB of HBM per device.

```python
import jax
import jax.numpy as jnp

D = 2048
LAYERS = 2
TOK = 512
FEATS = 16384


def block_levels(key, dims, pieces, least, top_value):
    def one(axis_at, blocks):
        draws = jax.random.uniform(jax.random.fold_in(jax.random.fold_in(key, 6), axis_at), (blocks,), jnp.float32, least / len(pieces), top_value / len(pieces))
        return jnp.repeat(jnp.exp(draws), dims[axis_at] // blocks).reshape((-1,) + (1,) * (len(dims) - axis_at - 1))

    gain = one(*pieces[0])
    for cut in pieces[1:]:
        gain = gain * one(*cut)
    return gain


def bell_draw(own_key, dims, deviation, reach, split=(), dtype=jnp.bfloat16):
    values = jax.random.normal(own_key, dims, jnp.float32) * deviation
    if len(split) > 0:
        values = block_levels(own_key, dims, split, -0.22, 0.18) * values
    return jnp.clip(values, min=-reach, max=reach).astype(dtype)


def setup_inputs(seed: int = 0) -> dict:
    keys = jax.random.split(jax.random.key(seed), 6)
    tokens_in = bell_draw(keys[0], (TOK, LAYERS * D), 1.0, 6.0, ((0, 4), (1, 8)))
    targets = bell_draw(keys[1], (TOK, LAYERS * D), 1.0, 6.0, ((0, 4), (1, 8)))
    enc_weight = bell_draw(keys[2], (D, LAYERS * FEATS), D ** -0.5, 0.125, ((1, 32),))
    enc_bias = jnp.clip(-1.0 + 1.5 * jax.random.uniform(keys[3], (LAYERS * FEATS,), jnp.float32) ** block_levels(keys[3], (LAYERS * FEATS,), ((0, 32),), -0.2, 0.2), -1.0, 0.5)
    dec_weight = bell_draw(keys[4], (LAYERS, LAYERS * FEATS, D), FEATS ** -0.5, 0.046875, ((1, 32),))
    return {"tokens_in": tokens_in, "targets": targets, "enc_weight": enc_weight, "enc_bias": enc_bias, "dec_weight": dec_weight}


loss_scale = 64.0


def reference(tokens_in, targets, enc_weight, enc_bias, dec_weight):
    layer_inputs, pre_acts, features = [], [], []
    for source in range(LAYERS):
        cols_in = tokens_in[:, source * D:(source + 1) * D]
        weights = enc_weight[:, source * FEATS:(source + 1) * FEATS]
        pre_act = jnp.dot(cols_in, weights, preferred_element_type=jnp.float32) + enc_bias[source * FEATS:(source + 1) * FEATS]
        layer_inputs.append(cols_in)
        pre_acts.append(pre_act)
        features.append(jnp.maximum(pre_act, 0.0).astype(jnp.bfloat16))
    errors = []
    for target in range(LAYERS):
        rebuilt = jnp.zeros((TOK, D), jnp.float32)
        for source in range(target + 1):
            rows = dec_weight[target - source, source * FEATS:(source + 1) * FEATS]
            rebuilt = rebuilt + jnp.dot(features[source], rows, preferred_element_type=jnp.float32)
        errors.append(rebuilt - targets[:, target * D:(target + 1) * D].astype(jnp.float32))
    recon_error = jnp.concatenate(errors, 1)
    mean_square = jnp.sum(recon_error * recon_error) / (LAYERS * TOK * D)
    scaled = ((loss_scale / TOK) * recon_error).astype(jnp.bfloat16)
    enc_parts, bias_parts = [], []
    dec_parts = [[] for offset in range(LAYERS)]
    for source in range(LAYERS):
        feature_grad = jnp.zeros((TOK, FEATS), jnp.float32)
        for offset in range(LAYERS):
            target = source + offset
            if target < LAYERS:
                grad_block = scaled[:, target * D:(target + 1) * D]
                rows = dec_weight[offset, source * FEATS:(source + 1) * FEATS]
                dec_parts[offset].append(jnp.dot(features[source].T, grad_block, preferred_element_type=jnp.float32).astype(jnp.bfloat16))
                feature_grad = feature_grad + jnp.dot(grad_block, rows.T, preferred_element_type=jnp.float32)
            else:
                dec_parts[offset].append(jnp.zeros((FEATS, D), jnp.bfloat16))
        preact_grad = jnp.where(pre_acts[source] > 0.0, feature_grad, 0.0).astype(jnp.bfloat16)
        enc_parts.append(jnp.dot(layer_inputs[source].T, preact_grad, preferred_element_type=jnp.float32).astype(jnp.bfloat16))
        bias_parts.append(jnp.sum(preact_grad.astype(jnp.float32), 0))
    enc_grad = jnp.concatenate(enc_parts, 1)
    bias_grad = jnp.concatenate(bias_parts, 0)
    dec_grad = jnp.stack([jnp.concatenate(dec_parts[offset], 0) for offset in range(LAYERS)], 0)
    return recon_error, mean_square, enc_grad, bias_grad, dec_grad
```

```python
import jax
import jax.numpy as jnp
from jax import lax
from jax.experimental import pallas as pl
from jax.experimental.pallas import tpu as pltpu
from jax.sharding import PartitionSpec as P

loss_scale = 64.0
vmem_limit = 50 * 1024 * 1024


def over_feat(value, mask):
    pairs = [(source, source ^ mask) for source in range(lax.axis_size("feat"))]
    return lax.ppermute(value, "feat", pairs)


def over_members(value, bit_level):
    mask = 2**bit_level
    pairs = [(source, source ^ mask) for source in range(lax.axis_size("layer"))]
    return lax.ppermute(value, "layer", pairs)


def to_layer(value, offset, sub_count):
    count = lax.axis_size("layer")
    shift = offset * sub_count
    pairs = [(p, p + shift) for p in range(count) if 0 <= p + shift < count]
    return lax.ppermute(value, "layer", pairs)


def params(flops, bytes_accessed):
    return dict(
        compiler_params=pltpu.CompilerParams(vmem_limit_bytes=vmem_limit),
        cost_estimate=pl.CostEstimate(
            flops=flops, bytes_accessed=bytes_accessed, transcendentals=0
        ),
    )


def whole(shape):
    return pl.BlockSpec(shape, lambda *_: (0,) * len(shape))


def encode_first(indices, pieces, enc_weight):
    count, feat_count, rows, cols = pieces.shape
    tok = feat_count * rows
    width = enc_weight.shape[1]

    def kernel(index_ref, piece_ref, weight_ref, out_ref):
        product = jnp.dot(
            piece_ref[0].reshape(tok, cols), weight_ref[...], preferred_element_type=jnp.float32
        )

        @pl.when(pl.program_id(0) == 0)
        def _():
            out_ref[...] = product

        @pl.when(pl.program_id(0) > 0)
        def _():
            out_ref[...] += product

    return pl.pallas_call(
        kernel,
        grid_spec=pltpu.PrefetchScalarGridSpec(
            num_scalar_prefetch=1,
            grid=(count,),
            in_specs=[
                pl.BlockSpec((1, feat_count, rows, cols), lambda i, idx: (i, 0, 0, 0)),
                pl.BlockSpec((cols, width), lambda i, idx: (idx[i], 0)),
            ],
            out_specs=whole((tok, width)),
        ),
        out_shape=jax.ShapeDtypeStruct((tok, width), jnp.float32),
        name="encode_first",
        **params(2 * count * tok * cols * width, 2 * count * cols * (tok + width) + 4 * tok * width),
    )(indices, pieces, enc_weight)


def encode_last(indices, pieces, enc_weight, partial, bias):
    count, feat_count, rows, cols = pieces.shape
    tok = feat_count * rows
    width = enc_weight.shape[1]

    def kernel(index_ref, piece_ref, weight_ref, partial_ref, bias_ref, feat_ref, mask_ref, total):
        step = pl.program_id(0)
        product = jnp.dot(
            piece_ref[0].reshape(tok, cols), weight_ref[...], preferred_element_type=jnp.float32
        )

        @pl.when(step == 0)
        def _():
            total[...] = partial_ref[...] + product

        @pl.when(step > 0)
        def _():
            total[...] += product

        @pl.when(step == count - 1)
        def _():
            pre_act = total[...] + bias_ref[...]
            feat_ref[...] = jnp.maximum(pre_act, 0.0).astype(jnp.bfloat16)
            mask_ref[...] = jnp.where(pre_act > 0.0, 1.0, 0.0).astype(jnp.bfloat16)

    return pl.pallas_call(
        kernel,
        grid_spec=pltpu.PrefetchScalarGridSpec(
            num_scalar_prefetch=1,
            grid=(count,),
            in_specs=[
                pl.BlockSpec((1, feat_count, rows, cols), lambda i, idx: (i, 0, 0, 0)),
                pl.BlockSpec((cols, width), lambda i, idx: (idx[i], 0)),
                whole((tok, width)),
                whole((1, width)),
            ],
            out_specs=[whole((tok, width)), whole((tok, width))],
            scratch_shapes=[pltpu.VMEM((tok, width), jnp.float32)],
        ),
        out_shape=[
            jax.ShapeDtypeStruct((tok, width), jnp.bfloat16),
            jax.ShapeDtypeStruct((tok, width), jnp.bfloat16),
        ],
        name="encode_last",
        **params(2 * count * tok * cols * width, 2 * count * cols * (tok + width) + 8 * tok * width),
    )(indices, pieces, enc_weight, partial, bias)


def decode(indices, features, dec_weight, offset, groups, rows, cols):
    tok, width = features.shape
    count = indices.shape[0]

    def kernel(index_ref, feat_ref, weight_ref, *out_refs):
        product = jnp.dot(feat_ref[...], weight_ref[0], preferred_element_type=jnp.float32)
        product = product.astype(jnp.bfloat16)
        for group, out_ref in zip(groups, out_refs):
            for place, block in enumerate(group):
                out_ref[0, place] = product[block * rows : (block + 1) * rows]

    return pl.pallas_call(
        kernel,
        grid_spec=pltpu.PrefetchScalarGridSpec(
            num_scalar_prefetch=1,
            grid=(count,),
            in_specs=[
                whole((tok, width)),
                pl.BlockSpec((1, width, cols), lambda i, idx: (offset, 0, idx[i])),
            ],
            out_specs=[
                pl.BlockSpec((1, len(group), rows, cols), lambda i, idx: (i, 0, 0, 0))
                for group in groups
            ],
        ),
        out_shape=[
            jax.ShapeDtypeStruct((count, len(group), rows, cols), jnp.bfloat16) for group in groups
        ],
        name="decode",
        **params(
            2 * count * tok * cols * width, 2 * count * cols * (tok + width) + 2 * tok * width
        ),
    )(indices, features, dec_weight)


def backward_piece(indices, grads, features, dec_weight, feature_grad, dec_grad):
    layers, width, depth = dec_weight.shape
    tok = features.shape[0]
    cols = grads[0][0].shape[2]
    per_layer = len(grads[0])
    flat = [piece for layer in grads for piece in layer]
    first = feature_grad is None

    def kernel(index_ref, *refs):
        grad_refs = refs[: len(flat)]
        feat_ref, weight_ref = refs[len(flat) : len(flat) + 2]
        out_ref, dec_ref = refs[-2:]
        step = pl.program_id(0)
        for k in range(layers):

            @pl.when(step == k)
            def _():
                parts = [
                    ref[...].reshape(-1, cols)
                    for ref in grad_refs[k * per_layer : (k + 1) * per_layer]
                ]
                grad = jnp.concatenate(parts, 0) if len(parts) > 1 else parts[0]
                product = lax.dot_general(
                    grad,
                    weight_ref[0],
                    (((1,), (1,)), ((), ())),
                    preferred_element_type=jnp.float32,
                )
                if k > 0:
                    out_ref[...] += product
                elif first:
                    out_ref[...] = product
                else:
                    out_ref[...] = refs[len(flat) + 2][...] + product
                dec_ref[0] = lax.dot_general(
                    feat_ref[...],
                    grad,
                    (((0,), (0,)), ((), ())),
                    preferred_element_type=jnp.float32,
                ).astype(jnp.bfloat16)

    extra_specs, extra, aliases = [], [], {}
    if not first:
        extra_specs = [whole((tok, width)), pl.BlockSpec(memory_space=pl.ANY)]
        extra = [feature_grad, dec_grad]
        aliases = {1 + len(flat) + 3: 1}
    return pl.pallas_call(
        kernel,
        grid_spec=pltpu.PrefetchScalarGridSpec(
            num_scalar_prefetch=1,
            grid=(layers,),
            in_specs=[whole(piece.shape) for piece in flat]
            + [
                whole((tok, width)),
                pl.BlockSpec((1, width, cols), lambda k, idx: (k, 0, idx[0])),
            ]
            + extra_specs,
            out_specs=[
                whole((tok, width)),
                pl.BlockSpec((1, width, cols), lambda k, idx: (k, 0, idx[0])),
            ],
        ),
        out_shape=[
            jax.ShapeDtypeStruct((tok, width), jnp.float32),
            jax.ShapeDtypeStruct((layers, width, depth), jnp.bfloat16),
        ],
        input_output_aliases=aliases,
        name="backward_piece",
        **params(
            4 * layers * tok * cols * width,
            4 * layers * cols * (tok + width) + 10 * tok * width,
        ),
    )(indices, *flat, features, dec_weight, *extra)


def encoder_grad(indices, halves, mask, feature_grad):
    count, feat_count, rows, cols = halves[0].shape
    tok, width = mask.shape

    def kernel(index_ref, low_ref, high_ref, mask_ref, grad_ref, enc_ref, bias_ref, preact):
        step = pl.program_id(0)

        @pl.when(step == 0)
        def _():
            kept = jnp.where(mask_ref[...] > 0.0, grad_ref[...], 0.0).astype(jnp.bfloat16)
            preact[...] = kept
            bias_ref[...] = jnp.sum(kept.astype(jnp.float32), 0, keepdims=True)

        for half, ref in enumerate((low_ref, high_ref)):

            @pl.when(step // count == half)
            def _():
                enc_ref[...] = lax.dot_general(
                    ref[0].reshape(tok, cols),
                    preact[...],
                    (((0,), (0,)), ((), ())),
                    preferred_element_type=jnp.float32,
                ).astype(jnp.bfloat16)

    return pl.pallas_call(
        kernel,
        grid_spec=pltpu.PrefetchScalarGridSpec(
            num_scalar_prefetch=1,
            grid=(2 * count,),
            in_specs=[
                pl.BlockSpec(
                    (1, feat_count, rows, cols),
                    lambda i, idx: (jnp.minimum(i, count - 1), 0, 0, 0),
                ),
                pl.BlockSpec(
                    (1, feat_count, rows, cols),
                    lambda i, idx: (jnp.maximum(i - count, 0), 0, 0, 0),
                ),
                whole((tok, width)),
                whole((tok, width)),
            ],
            out_specs=[
                pl.BlockSpec((cols, width), lambda i, idx: (idx[i], 0)),
                whole((1, width)),
            ],
            scratch_shapes=[pltpu.VMEM((tok, width), jnp.bfloat16)],
        ),
        out_shape=[
            jax.ShapeDtypeStruct((2 * count * cols, width), jnp.bfloat16),
            jax.ShapeDtypeStruct((1, width), jnp.float32),
        ],
        name="encoder_grad",
        **params(
            4 * count * tok * cols * width, 4 * count * cols * (tok + width) + 6 * tok * width
        ),
    )(indices, halves[0], halves[1], mask, feature_grad)


def add_pair(left, right):
    return (left.astype(jnp.float32) + right.astype(jnp.float32)).astype(jnp.bfloat16)


def on_device(tokens_in, targets, enc_weight, enc_bias, dec_weight):
    layers, width, depth = dec_weight.shape
    feat_count = lax.axis_size("feat")
    sub_count = lax.axis_size("layer") // layers
    member = lax.axis_index("layer") % sub_count
    rows, cols = tokens_in.shape
    bit_count = sub_count.bit_length() - 1
    pairs = sub_count // 2
    near = member ^ (2 * jnp.arange(pairs, dtype=jnp.int32))
    far = near ^ 1
    groups = [list(range(feat_count))]

    held = {0: [tokens_in] + [over_feat(tokens_in, s) for s in range(1, feat_count)]}
    for bit_level in range(bit_count - 1, 0, -1):
        for rel in list(held):
            held[rel ^ 2**bit_level] = [over_members(block, bit_level) for block in held[rel]]
    half = jnp.stack([jnp.stack(held[rel], 0) for rel in sorted(held)], 0)
    other = over_members(half, 0)
    partial = encode_first(near, half, enc_weight)
    features, mask = encode_last(far, other, enc_weight, partial, enc_bias[None])

    totals = [None] * layers
    for k in reversed(range(layers)):
        sent = decode(far, features, dec_weight, k, groups, rows, cols)
        kept = decode(near, features, dec_weight, k, groups, rows, cols)
        blocks = [None] * feat_count
        for place in reversed(range(len(groups))):
            current = add_pair(kept[place], over_members(sent[place], 0))
            for bit_level in range(1, bit_count):
                split = current.reshape((current.shape[0] // 2, 2) + current.shape[1:])
                current = add_pair(split[:, 0], over_members(split[:, 1], bit_level))
            for index, block in enumerate(groups[place]):
                blocks[block] = current[0, index]
        total = blocks[0].astype(jnp.float32)
        for s in range(1, feat_count):
            total = total + over_feat(blocks[s], s).astype(jnp.float32)
        totals[k] = total
    rebuilt = totals[0]
    for k in range(1, layers):
        rebuilt = rebuilt + to_layer(totals[k].astype(jnp.bfloat16), k, sub_count).astype(
            jnp.float32
        )
    recon_error = rebuilt - targets.astype(jnp.float32)
    scaled = (loss_scale / (feat_count * rows) * recon_error).astype(jnp.bfloat16)

    pieces = {}
    for k in range(layers):
        own = scaled if k == 0 else to_layer(scaled, -k, sub_count)
        blocks = [own] + [over_feat(own, s) for s in range(1, feat_count)]
        got = {0: [jnp.stack([blocks[s] for s in group], 0) for group in groups]}
        for bit_level in range(bit_count - 1, -1, -1):
            for rel in list(got):
                got[rel ^ 2**bit_level] = [over_members(part, bit_level) for part in got[rel]]
        for rel, parts in got.items():
            pieces.setdefault(rel, []).append(parts)

    squares = jnp.sum(recon_error * recon_error).reshape(1, 1)
    for s in range(feat_count.bit_length() - 1):
        squares = squares + over_feat(squares, 2**s)
    for s in range(lax.axis_size("layer").bit_length() - 1):
        squares = squares + over_members(squares, s)
    mean_square = squares[0, 0] / (layers * feat_count * rows * depth)

    feature_grad, dec_grad = None, None
    order = [rel for rel in sorted(pieces) if rel % 2 == 0]
    order += [rel for rel in sorted(pieces) if rel % 2 == 1]
    for rel in order:
        feature_grad, dec_grad = backward_piece(
            (member ^ rel).reshape(1), pieces[rel], features, dec_weight, feature_grad, dec_grad
        )
    enc_grad, bias_grad = encoder_grad(
        jnp.concatenate([near, far]), (half, other), mask, feature_grad
    )
    return (recon_error, mean_square, enc_grad, bias_grad[0], dec_grad)


def solution(mesh):
    placed = (
        P("feat", "layer"),
        P("feat", "layer"),
        P(None, ("layer", "feat")),
        P(("layer", "feat")),
        P(None, ("layer", "feat"), None),
    )
    return jax.shard_map(
        on_device,
        mesh=mesh,
        in_specs=placed,
        out_specs=(
            P("feat", "layer"),
            P(),
            P(None, ("layer", "feat")),
            P(("layer", "feat")),
            P(None, ("layer", "feat"), None),
        ),
        check_vma=False,
    )
```

```python
import jax
import jax.numpy as jnp
from jax import lax
from jax.experimental import pallas as pl
from jax.experimental.pallas import tpu as pltpu
from jax.sharding import PartitionSpec as P

loss_scale = 64.0
tile = 256
in_vmem = pl.BlockSpec(memory_space=pltpu.VMEM)
in_smem = pl.BlockSpec(memory_space=pltpu.SMEM)
anywhere = pl.BlockSpec(memory_space=pl.ANY)


def over_feat(value, mask):
    pairs = [(source, source ^ mask) for source in range(lax.axis_size("feat"))]
    return lax.ppermute(value, "feat", pairs)


def over_members(value, bit_level):
    mask = 2**bit_level
    pairs = [(source, source ^ mask) for source in range(lax.axis_size("layer"))]
    return lax.ppermute(value, "layer", pairs)


def to_layer(value, offset, sub_count):
    count = lax.axis_size("layer")
    shift = offset * sub_count
    pairs = [(p, p + shift) for p in range(count - shift)]
    return lax.ppermute(value, "layer", pairs)


def from_layer(value, offset, sub_count):
    count = lax.axis_size("layer")
    pairs = [(p, (p - offset * sub_count) % count) for p in range(count)]
    return lax.ppermute(value, "layer", pairs)


def after(value, *others):
    return lax.optimization_barrier((value, *others))[0]


def params(flops, bytes_accessed, scratch_mib):
    return dict(
        compiler_params=pltpu.CompilerParams(vmem_limit_bytes=scratch_mib * 1024 * 1024),
        cost_estimate=pl.CostEstimate(
            flops=flops, bytes_accessed=bytes_accessed, transcendentals=0
        ),
    )


def dot(left, right, contract):
    return lax.dot_general(
        left, right, ((contract[:1], contract[1:]), ((), ())), preferred_element_type=jnp.float32
    )


def span(index, size):
    return pl.ds(pl.multiple_of(index * size, size), size)


def encode(indices, pieces, enc_weight, partial, bias):
    feat_count, rows, cols = pieces[0].shape
    tok = feat_count * rows
    width = enc_weight.shape[1]
    extra = [value for value in (partial, bias) if value is not None]

    def kernel(index_ref, *refs):
        piece_refs = refs[: len(pieces)]
        weight_ref = refs[len(pieces)]
        extra_refs = list(refs[len(pieces) + 1 : len(pieces) + 1 + len(extra)])
        out_refs = refs[len(pieces) + 1 + len(extra) :]
        left = jnp.concatenate([ref[...].reshape(tok, cols) for ref in piece_refs], 1)
        for start in range(0, width, tile):
            here = slice(start, start + tile)
            right = jnp.concatenate(
                [weight_ref[span(index_ref[i], cols), here] for i in range(len(pieces))], 0
            )
            total = dot(left, right, (1, 0))
            if partial is not None:
                total += extra_refs[0][:, here]
            if bias is None:
                out_refs[0][:, here] = total
            else:
                pre_act = total + extra_refs[-1][:, here]
                out_refs[0][:, here] = jnp.maximum(pre_act, 0.0).astype(jnp.bfloat16)
                out_refs[1][:, here] = jnp.where(pre_act > 0.0, 1.0, 0.0).astype(jnp.bfloat16)

    if bias is None:
        out_shape = [jax.ShapeDtypeStruct((tok, width), jnp.float32)]
    else:
        out_shape = [jax.ShapeDtypeStruct((tok, width), jnp.bfloat16)] * 2
    return pl.pallas_call(
        kernel,
        in_specs=[in_smem] + [in_vmem] * (len(pieces) + 1 + len(extra)),
        out_specs=[in_vmem] * len(out_shape),
        out_shape=out_shape,
        name="encode",
        **params(
            2 * len(pieces) * tok * cols * width,
            2 * len(pieces) * cols * (tok + width) + 8 * tok * width,
            12,
        ),
    )(indices, *pieces, enc_weight, *extra)


def decode(indices, features, dec_weight, offset, groups, rows, cols):
    tok, width = features.shape
    count = indices.shape[0]

    def kernel(index_ref, feat_ref, weight_ref, *out_refs):
        left = feat_ref[...]
        for piece in range(count):
            for start in range(0, cols, tile):
                right = weight_ref[
                    offset,
                    :,
                    pl.ds(pl.multiple_of(index_ref[piece] * cols + start, tile), tile),
                ]
                product = dot(left, right, (1, 0)).astype(jnp.bfloat16)
                for group, out_ref in zip(groups, out_refs):
                    for place, block in enumerate(group):
                        out_ref[piece, place, :, start : start + tile] = product[
                            block * rows : (block + 1) * rows
                        ]

    return pl.pallas_call(
        kernel,
        in_specs=[in_smem, in_vmem, in_vmem],
        out_specs=[in_vmem] * len(groups),
        out_shape=[
            jax.ShapeDtypeStruct((count, len(group), rows, cols), jnp.bfloat16) for group in groups
        ],
        name="decode",
        **params(
            2 * count * tok * cols * width,
            2 * count * cols * (tok + width) + 2 * tok * width,
            12,
        ),
    )(indices, features, dec_weight)


def turned(value):
    count, tok, width = value.shape

    def kernel(in_ref, out_ref):
        for piece in range(count):
            for start in range(0, width, tile):
                out_ref[piece, start : start + tile, :] = in_ref[
                    piece, :, start : start + tile
                ].T

    return pl.pallas_call(
        kernel,
        in_specs=[in_vmem],
        out_specs=in_vmem,
        out_shape=jax.ShapeDtypeStruct((count, width, tok), value.dtype),
        name="turned",
        **params(0, 4 * count * tok * width, 12),
    )(value)


def tree_sum(values):
    while len(values) > 1:
        values = [values[i] + values[i + 1] for i in range(0, len(values), 2)]
    return values[0]


def backward_piece(info, offset, grads, turned_features, dec_weight, feature_grad, dec_grad):
    layers, width, depth = dec_weight.shape
    tok = turned_features.shape[1]
    cols = grads[0].shape[2]
    first = feature_grad is None
    extra = [] if first else [feature_grad, dec_grad]

    def kernel(info_ref, *refs):
        grad_refs = refs[: len(grads)]
        feat_ref, weight_ref = refs[len(grads) : len(grads) + 2]
        out_ref, dec_ref, square_ref, held, sems = refs[-5:]
        blocks = [ref[i] for ref in grad_refs for i in range(ref.shape[0])]
        sums = []
        for block in blocks:
            total = jnp.zeros((8, 128), jnp.float32)
            for row in range(0, block.shape[0], 8):
                for col in range(0, cols, 128):
                    part = block[row : row + 8, col : col + 128].astype(jnp.float32)
                    total += part * part
            sums.append(total)
        square_ref[...] = tree_sum(sums)
        grad = jnp.concatenate(blocks, 0)
        if offset > 0:
            grad = jnp.where(info_ref[1] > 0, grad, jnp.zeros_like(grad))
        columns = span(info_ref[0], cols)
        copies = []
        for place, start in enumerate(range(0, width, tile)):
            here = slice(start, start + tile)
            held[here] = dot(feat_ref[here], grad, (1, 0)).astype(jnp.bfloat16)
            copy = pltpu.make_async_copy(
                held.at[here], dec_ref.at[offset, here, columns], sems.at[place]
            )
            copy.start()
            copies.append(copy)
        for start in range(0, width, tile):
            here = slice(start, start + tile)
            product = dot(grad, weight_ref[offset, here, columns], (1, 1))
            if not first:
                product += refs[len(grads) + 2][:, here]
            out_ref[:, here] = product
        for copy in copies:
            copy.wait()

    return pl.pallas_call(
        kernel,
        in_specs=[in_smem]
        + [in_vmem] * (len(grads) + 2)
        + ([] if first else [in_vmem, anywhere]),
        out_specs=[in_vmem, anywhere, in_vmem],
        out_shape=[
            jax.ShapeDtypeStruct((tok, width), jnp.float32),
            jax.ShapeDtypeStruct((layers, width, depth), jnp.bfloat16),
            jax.ShapeDtypeStruct((8, 128), jnp.float32),
        ],
        scratch_shapes=[
            pltpu.VMEM((width, cols), jnp.bfloat16),
            pltpu.SemaphoreType.DMA((width // tile,)),
        ],
        input_output_aliases={} if first else {len(grads) + 3: 0, len(grads) + 4: 1},
        name="backward_piece",
        **params(tok * cols, tok * cols, 12),
    )(info, *grads, turned_features, dec_weight, *extra)


def encoder_grad(indices, turned_tokens, mask, feature_grad, squares, scale):
    count, cols, tok = turned_tokens[0].shape
    width = mask.shape[1]
    pieces = len(turned_tokens) * count

    def kernel(index_ref, *refs):
        token_refs = refs[: len(turned_tokens)]
        mask_ref, grad_ref = refs[len(turned_tokens) : len(turned_tokens) + 2]
        square_refs = refs[len(turned_tokens) + 2 : -6]
        enc_ref, bias_ref, mean_ref, preact, held, sems = refs[-6:]
        mean_ref[...] = scale * jnp.sum(
            tree_sum([ref[...] for ref in square_refs]), (0, 1), keepdims=True
        )
        for start in range(0, width, tile):
            here = slice(start, start + tile)
            kept = jnp.where(mask_ref[:, here] > 0.0, grad_ref[:, here], 0.0).astype(jnp.bfloat16)
            preact[:, here] = kept
            bias_ref[:, here] = jnp.sum(kept.astype(jnp.float32), 0, keepdims=True)
        copies = []
        for piece in range(pieces):
            held[piece] = dot(
                token_refs[piece // count][piece % count], preact[...], (1, 0)
            ).astype(jnp.bfloat16)
            copy = pltpu.make_async_copy(
                held.at[piece], enc_ref.at[span(index_ref[piece], cols)], sems.at[piece]
            )
            copy.start()
            copies.append(copy)
        for copy in copies:
            copy.wait()

    return pl.pallas_call(
        kernel,
        in_specs=[in_smem] + [in_vmem] * (len(turned_tokens) + 2 + len(squares)),
        out_specs=[anywhere, in_vmem, in_vmem],
        out_shape=[
            jax.ShapeDtypeStruct((pieces * cols, width), jnp.bfloat16),
            jax.ShapeDtypeStruct((1, width), jnp.float32),
            jax.ShapeDtypeStruct((1, 1), jnp.float32),
        ],
        scratch_shapes=[
            pltpu.VMEM((tok, width), jnp.bfloat16),
            pltpu.VMEM((pieces, cols, width), jnp.bfloat16),
            pltpu.SemaphoreType.DMA((pieces,)),
        ],
        name="encoder_grad",
        **params(
            2 * pieces * tok * cols * width, 2 * pieces * cols * (tok + width) + 6 * tok * width, 16
        ),
    )(indices, *turned_tokens, mask, feature_grad, *squares)


def add_pair(left, right):
    return (left.astype(jnp.float32) + right.astype(jnp.float32)).astype(jnp.bfloat16)


def on_device(tokens_in, targets, enc_weight, enc_bias, dec_weight):
    layers, width, depth = dec_weight.shape
    feat_count = lax.axis_size("feat")
    sub_count = lax.axis_size("layer") // layers
    member = lax.axis_index("layer") % sub_count
    rows, cols = tokens_in.shape
    tok = feat_count * rows
    bit_count = sub_count.bit_length() - 1
    near = member ^ (2 * jnp.arange(sub_count // 2, dtype=jnp.int32))
    far = near ^ 1
    groups = [list(range(feat_count // 2)), list(range(feat_count // 2, feat_count))]

    held = {0: [tokens_in] + [over_feat(tokens_in, s) for s in range(1, feat_count)]}
    for bit_level in range(bit_count - 1, 0, -1):
        for rel in list(held):
            held[rel ^ 2**bit_level] = [over_members(block, bit_level) for block in held[rel]]
    tokens, order = {}, []
    for rel in sorted(held):
        tokens[rel] = jnp.stack(held[rel], 0)
        tokens[rel ^ 1] = over_members(tokens[rel], 0)
        order += [rel, rel ^ 1]
    partial = encode(
        jnp.stack([member, member ^ 1]), [tokens[0], tokens[1]], enc_weight, None, None
    )[0]
    for rel in order[2:-1]:
        partial = encode((member ^ rel).reshape(1), [tokens[rel]], enc_weight, partial, None)[0]
    features, mask = encode(
        (member ^ order[-1]).reshape(1), [tokens[order[-1]]], enc_weight, partial, enc_bias[None]
    )

    totals = [None] * layers
    source = features
    for k in reversed(range(layers)):
        sent = decode(far, source, dec_weight, k, groups, rows, cols)
        kept = decode(near, source, dec_weight, k, groups, rows, cols)
        blocks = [None] * feat_count
        for place in reversed(range(len(groups))):
            current = add_pair(kept[place], over_members(sent[place], 0))
            for bit_level in range(1, bit_count):
                split = current.reshape((current.shape[0] // 2, 2) + current.shape[1:])
                if bit_level == 1:
                    source = after(features, current)
                current = add_pair(split[:, 0], over_members(split[:, 1], bit_level))
            for index, block in enumerate(groups[place]):
                blocks[block] = current[0, index]
        total = blocks[0].astype(jnp.float32)
        for s in range(1, feat_count):
            total = total + over_feat(blocks[s], s).astype(jnp.float32)
        totals[k] = total
    turned_features = turned(source[None])[0]
    turned_tokens = [
        turned(after(tokens[rel], turned_features).reshape(1, tok, cols)) for rel in order
    ]
    rebuilt = totals[0]
    for k in range(1, layers):
        rebuilt = rebuilt + to_layer(totals[k].astype(jnp.bfloat16), k, sub_count).astype(
            jnp.float32
        )
    recon_error = rebuilt - after(targets, turned_features, *turned_tokens).astype(jnp.float32)
    scaled = (loss_scale / tok * recon_error).astype(jnp.bfloat16)

    layer = lax.axis_index("layer") // sub_count
    there = [(layer + k < layers).astype(jnp.int32) for k in range(layers)]
    groups_of = {}
    for k in range(layers):
        own = scaled if k == 0 else from_layer(scaled, k, sub_count)
        blocks = [own] + [over_feat(own, s) for s in range(1, feat_count)]
        groups_of[0, k] = [jnp.stack([blocks[s] for s in group], 0) for group in groups]
    stages = [[0]]
    for level in range(bit_count - 1, 0, -1):
        known = [rel for stage in stages for rel in stage]
        stages.append([rel ^ 2**level for rel in known])
        for k in range(layers):
            for rel in known:
                groups_of[rel ^ 2**level, k] = [
                    over_members(part, level) for part in groups_of[rel, k]
                ]

    feature_grad, dec_grad, squares = None, None, {}
    for number, stage in enumerate(stages):
        for k in range(layers):
            guard = []
            if k > 0 and number + 1 < len(stages):
                guard = [part for rel in stages[number + 1] for part in groups_of[rel, k - 1]]
            elif k == 0 and number > 0:
                guard = [groups_of[rel, layers - 1][0] for rel in stage]
            if feature_grad is not None and guard:
                feature_grad = after(feature_grad, *guard)
            for rel in stage:
                parts = groups_of[rel, k]
                if feature_grad is not None:
                    parts = [after(part, feature_grad) for part in parts]
                groups_of[rel ^ 1, k] = [over_members(part, 0) for part in parts]
                for half in (rel, rel ^ 1):
                    feature_grad, dec_grad, squares[k, half] = backward_piece(
                        jnp.stack([member ^ half, there[k]]),
                        k,
                        groups_of[half, k],
                        turned_features,
                        dec_weight,
                        feature_grad,
                        dec_grad,
                    )
    scale = (tok / loss_scale) ** 2 / (layers * tok * depth)
    enc_grad, bias_grad, mean_square = encoder_grad(
        jnp.stack([member ^ rel for rel in order]),
        turned_tokens,
        mask,
        feature_grad,
        [squares[key] for key in sorted(squares)],
        scale,
    )
    return (recon_error, mean_square[0, 0], enc_grad, bias_grad[0], dec_grad)


def solution(mesh):
    placed = (
        P("feat", "layer"),
        P("feat", "layer"),
        P(None, ("layer", "feat")),
        P(("layer", "feat")),
        P(None, ("layer", "feat"), None),
    )
    return jax.shard_map(
        on_device,
        mesh=mesh,
        in_specs=placed,
        out_specs=(
            P("feat", "layer"),
            P(),
            P(None, ("layer", "feat")),
            P(("layer", "feat")),
            P(None, ("layer", "feat"), None),
        ),
        check_vma=False,
    )
```

```python
import jax
import jax.numpy as jnp
from jax import lax
from jax.experimental import pallas as pl
from jax.experimental.pallas import tpu as pltpu
from jax.sharding import PartitionSpec as P

loss_scale = 64.0
tile = 256
in_vmem = pl.BlockSpec(memory_space=pltpu.VMEM)
in_smem = pl.BlockSpec(memory_space=pltpu.SMEM)
in_hbm = pl.BlockSpec(memory_space=pltpu.HBM)


def over_feat(value, mask):
    pairs = [(source, source ^ mask) for source in range(lax.axis_size("feat"))]
    return lax.ppermute(value, "feat", pairs)


def over_members(value, bit_level):
    mask = 2**bit_level
    pairs = [(source, source ^ mask) for source in range(lax.axis_size("layer"))]
    return lax.ppermute(value, "layer", pairs)


def to_layer(value, offset, sub_count):
    count = lax.axis_size("layer")
    shift = offset * sub_count
    pairs = [(p, p + shift) for p in range(count - shift)]
    return lax.ppermute(value, "layer", pairs)


def from_layer(value, offset, sub_count):
    count = lax.axis_size("layer")
    pairs = [(p, (p - offset * sub_count) % count) for p in range(count)]
    return lax.ppermute(value, "layer", pairs)


def after(value, *others):
    return lax.optimization_barrier((value, *others))[0]


def all_over_feat(value):
    blocks = [value, over_feat(value, 1)]
    for s in range(2, lax.axis_size("feat")):
        blocks.append(over_feat(after(value, blocks[1]) if s > 2 else value, s))
    return blocks


def params(flops, bytes_accessed, scratch_mib):
    return dict(
        compiler_params=pltpu.CompilerParams(vmem_limit_bytes=scratch_mib * 1024 * 1024),
        cost_estimate=pl.CostEstimate(
            flops=flops, bytes_accessed=bytes_accessed, transcendentals=0
        ),
    )


def dot(left, right, contract):
    return lax.dot_general(
        left, right, ((contract[:1], contract[1:]), ((), ())), preferred_element_type=jnp.float32
    )


def span(index, size):
    return pl.ds(pl.multiple_of(index * size, size), size)


def encode_first(indices, pieces, enc_weight, dec_weight, offset, late, ahead):
    feat_count, rows, cols = pieces[0].shape
    tok = feat_count * rows
    width = enc_weight.shape[1]
    now = len(pieces)

    def kernel(index_ref, *refs):
        piece_refs = refs[:now]
        weight_ref, next_ref, out_ref, late_ref, ahead_ref, held, sems = refs[now:]
        copies = []
        for i in range(now + late):
            copies.append(
                pltpu.make_async_copy(
                    weight_ref.at[span(index_ref[i], cols)],
                    held.at[i] if i < now else late_ref.at[i - now],
                    sems.at[i],
                )
            )
        for i in range(ahead):
            copies.append(
                pltpu.make_async_copy(
                    next_ref.at[offset, :, span(index_ref[now + late + i], cols)],
                    ahead_ref.at[i],
                    sems.at[now + late + i],
                )
            )
        for copy in copies:
            copy.start()
        for copy in copies[:now]:
            copy.wait()
        left = jnp.concatenate([ref[...].reshape(tok, cols) for ref in piece_refs], 1)
        for start in range(0, width, tile):
            here = slice(start, start + tile)
            right = jnp.concatenate([held[i, :, here] for i in range(now)], 0)
            out_ref[:, here] = dot(left, right, (1, 0))
        for copy in copies[now:]:
            copy.wait()

    return pl.pallas_call(
        kernel,
        in_specs=[in_smem] + [in_vmem] * now + [in_hbm] * 2,
        out_specs=[in_vmem] * 3,
        out_shape=[
            jax.ShapeDtypeStruct((tok, width), jnp.float32),
            jax.ShapeDtypeStruct((late, cols, width), jnp.bfloat16),
            jax.ShapeDtypeStruct((ahead, width, cols), jnp.bfloat16),
        ],
        scratch_shapes=[
            pltpu.VMEM((now, cols, width), jnp.bfloat16),
            pltpu.SemaphoreType.DMA((now + late + ahead,)),
        ],
        name="encode_first",
        **params(2 * now * tok * cols * width, 2 * (now + late + 2 * ahead) * cols * width, 12),
    )(indices, *pieces, enc_weight, dec_weight)


def encode_next(piece, weights, place, partial, bias):
    feat_count, rows, cols = piece.shape
    tok = feat_count * rows
    width = weights.shape[2]
    extra = [partial] if bias is None else [partial, bias]

    def kernel(piece_ref, weight_ref, partial_ref, *refs):
        left = piece_ref[...].reshape(tok, cols)
        for start in range(0, width, tile):
            here = slice(start, start + tile)
            total = partial_ref[:, here] + dot(left, weight_ref[place, :, here], (1, 0))
            if bias is None:
                refs[0][:, here] = total
            else:
                pre_act = total + refs[0][:, here]
                refs[1][:, here] = jnp.maximum(pre_act, 0.0).astype(jnp.bfloat16)
                refs[2][:, here] = jnp.where(pre_act > 0.0, 1.0, 0.0).astype(jnp.bfloat16)

    if bias is None:
        out_shape = [jax.ShapeDtypeStruct((tok, width), jnp.float32)]
    else:
        out_shape = [jax.ShapeDtypeStruct((tok, width), jnp.bfloat16)] * 2
    return pl.pallas_call(
        kernel,
        in_specs=[in_vmem] * (2 + len(extra)),
        out_specs=[in_vmem] * len(out_shape),
        out_shape=out_shape,
        name="encode_next",
        **params(2 * tok * cols * width, 2 * cols * width, 8),
    )(piece, weights, *extra)


def decode(features, weights, groups, rows, indices=None, dec_weight=None, offset=None):
    tok, width = features.shape
    count, _, cols = weights.shape
    ahead = indices is not None

    def kernel(feat_ref, weight_ref, *refs):
        if ahead:
            index_ref, next_ref = refs[:2]
            out_refs, next_out, sems = refs[2:-2], refs[-2], refs[-1]
            copies = [
                pltpu.make_async_copy(
                    next_ref.at[offset, :, span(index_ref[i], cols)], next_out.at[i], sems.at[i]
                )
                for i in range(count)
            ]
            for copy in copies:
                copy.start()
        else:
            out_refs = refs
        left = feat_ref[...]
        for piece in range(count):
            for start in range(0, cols, tile):
                here = slice(start, start + tile)
                product = dot(left, weight_ref[piece, :, here], (1, 0)).astype(jnp.bfloat16)
                for group, out_ref in zip(groups, out_refs):
                    for place, block in enumerate(group):
                        out_ref[piece, place, :, here] = product[block * rows : (block + 1) * rows]
        if ahead:
            for copy in copies:
                copy.wait()

    out_shape = [
        jax.ShapeDtypeStruct((count, len(group), rows, cols), jnp.bfloat16) for group in groups
    ]
    if ahead:
        out_shape.append(jax.ShapeDtypeStruct((count, width, cols), jnp.bfloat16))
    result = pl.pallas_call(
        kernel,
        in_specs=[in_vmem] * 2 + ([in_smem, in_hbm] if ahead else []),
        out_specs=[in_vmem] * len(out_shape),
        out_shape=out_shape,
        scratch_shapes=[pltpu.SemaphoreType.DMA((count,))] if ahead else [],
        name="decode",
        **params(2 * count * tok * cols * width, 2 * count * cols * width, 8),
    )(features, weights, *([indices, dec_weight] if ahead else []))
    return result[: len(groups)], (result[-1] if ahead else None)


def turned(value):
    count, tok, width = value.shape

    def kernel(in_ref, out_ref):
        for piece in range(count):
            for start in range(0, width, tile):
                out_ref[piece, start : start + tile, :] = in_ref[
                    piece, :, start : start + tile
                ].T

    return pl.pallas_call(
        kernel,
        in_specs=[in_vmem],
        out_specs=in_vmem,
        out_shape=jax.ShapeDtypeStruct((count, width, tok), value.dtype),
        name="turned",
        **params(0, 4 * count * tok * width, 12),
    )(value)


def tree_sum(values):
    while len(values) > 1:
        values = [values[i] + values[i + 1] for i in range(0, len(values), 2)]
    return values[0]


def backward_piece(info, offset, grads, turned_features, dec_weight, feature_grad, dec_grad):
    layers, width, depth = dec_weight.shape
    tok = turned_features.shape[1]
    cols = grads[0].shape[2]
    first = feature_grad is None
    extra = [] if first else [feature_grad, dec_grad]

    def kernel(info_ref, *refs):
        grad_refs = refs[: len(grads)]
        feat_ref, weight_ref = refs[len(grads) : len(grads) + 2]
        out_ref, dec_ref, square_ref, held, weights, sems = refs[-6:]
        columns = span(info_ref[0], cols)
        fetch = pltpu.make_async_copy(
            weight_ref.at[offset, :, columns], weights, sems.at[width // tile]
        )
        fetch.start()
        blocks = [ref[i] for ref in grad_refs for i in range(ref.shape[0])]
        sums = []
        for block in blocks:
            total = jnp.zeros((8, 128), jnp.float32)
            for row in range(0, block.shape[0], 8):
                for col in range(0, cols, 128):
                    part = block[row : row + 8, col : col + 128].astype(jnp.float32)
                    total += part * part
            sums.append(total)
        square_ref[...] = tree_sum(sums)
        grad = jnp.concatenate(blocks, 0)
        if offset > 0:
            grad = jnp.where(info_ref[1] > 0, grad, jnp.zeros_like(grad))
        copies = []
        for place, start in enumerate(range(0, width, tile)):
            here = slice(start, start + tile)
            held[here] = dot(feat_ref[here], grad, (1, 0)).astype(jnp.bfloat16)
            copy = pltpu.make_async_copy(
                held.at[here], dec_ref.at[offset, here, columns], sems.at[place]
            )
            copy.start()
            copies.append(copy)
        fetch.wait()
        for start in range(0, width, tile):
            here = slice(start, start + tile)
            product = dot(grad, weights[here], (1, 1))
            if not first:
                product += refs[len(grads) + 2][:, here]
            out_ref[:, here] = product
        for copy in copies:
            copy.wait()

    return pl.pallas_call(
        kernel,
        in_specs=[in_smem]
        + [in_vmem] * (len(grads) + 1)
        + [in_hbm]
        + ([] if first else [in_vmem, in_hbm]),
        out_specs=[in_vmem, in_hbm, in_vmem],
        out_shape=[
            jax.ShapeDtypeStruct((tok, width), jnp.float32),
            jax.ShapeDtypeStruct((layers, width, depth), jnp.bfloat16),
            jax.ShapeDtypeStruct((8, 128), jnp.float32),
        ],
        scratch_shapes=[
            pltpu.VMEM((width, cols), jnp.bfloat16),
            pltpu.VMEM((width, cols), jnp.bfloat16),
            pltpu.SemaphoreType.DMA((width // tile + 1,)),
        ],
        input_output_aliases={} if first else {len(grads) + 3: 0, len(grads) + 4: 1},
        name="backward_piece",
        **params(tok * cols, tok * cols, 12),
    )(info, *grads, turned_features, dec_weight, *extra)


def encoder_grad(indices, turned_tokens, mask, feature_grad, squares, scale):
    count, cols, tok = turned_tokens[0].shape
    width = mask.shape[1]
    pieces = len(turned_tokens) * count

    def kernel(index_ref, *refs):
        token_refs = refs[: len(turned_tokens)]
        mask_ref, grad_ref = refs[len(turned_tokens) : len(turned_tokens) + 2]
        square_refs = refs[len(turned_tokens) + 2 : -6]
        enc_ref, bias_ref, mean_ref, preact, held, sems = refs[-6:]
        mean_ref[...] = scale * jnp.sum(
            tree_sum([ref[...] for ref in square_refs]), (0, 1), keepdims=True
        )
        for start in range(0, width, tile):
            here = slice(start, start + tile)
            kept = jnp.where(mask_ref[:, here] > 0.0, grad_ref[:, here], 0.0).astype(jnp.bfloat16)
            preact[:, here] = kept
            bias_ref[:, here] = jnp.sum(kept.astype(jnp.float32), 0, keepdims=True)
        copies = []
        for piece in range(pieces):
            held[piece] = dot(
                token_refs[piece // count][piece % count], preact[...], (1, 0)
            ).astype(jnp.bfloat16)
            copy = pltpu.make_async_copy(
                held.at[piece], enc_ref.at[span(index_ref[piece], cols)], sems.at[piece]
            )
            copy.start()
            copies.append(copy)
        for copy in copies:
            copy.wait()

    return pl.pallas_call(
        kernel,
        in_specs=[in_smem] + [in_vmem] * (len(turned_tokens) + 2 + len(squares)),
        out_specs=[in_hbm, in_vmem, in_vmem],
        out_shape=[
            jax.ShapeDtypeStruct((pieces * cols, width), jnp.bfloat16),
            jax.ShapeDtypeStruct((1, width), jnp.float32),
            jax.ShapeDtypeStruct((1, 1), jnp.float32),
        ],
        scratch_shapes=[
            pltpu.VMEM((tok, width), jnp.bfloat16),
            pltpu.VMEM((pieces, cols, width), jnp.bfloat16),
            pltpu.SemaphoreType.DMA((pieces,)),
        ],
        name="encoder_grad",
        **params(
            2 * pieces * tok * cols * width, 2 * pieces * cols * (tok + width) + 6 * tok * width, 16
        ),
    )(indices, *turned_tokens, mask, feature_grad, *squares)


def add_pair(left, right):
    return (left.astype(jnp.float32) + right.astype(jnp.float32)).astype(jnp.bfloat16)


def on_device(tokens_in, targets, enc_weight, enc_bias, dec_weight):
    layers, width, depth = dec_weight.shape
    feat_count = lax.axis_size("feat")
    sub_count = lax.axis_size("layer") // layers
    member = lax.axis_index("layer") % sub_count
    rows, cols = tokens_in.shape
    tok = feat_count * rows
    bit_count = sub_count.bit_length() - 1
    near = member ^ (2 * jnp.arange(sub_count // 2, dtype=jnp.int32))
    far = near ^ 1
    groups = [list(range(feat_count // 2)), list(range(feat_count // 2, feat_count))]

    enc_weight = pltpu.with_memory_space_constraint(enc_weight, pltpu.HBM)
    dec_weight = pltpu.with_memory_space_constraint(dec_weight, pltpu.HBM)

    held = {0: all_over_feat(tokens_in)}
    for bit_level in range(bit_count - 1, 0, -1):
        for rel in list(held):
            held[rel ^ 2**bit_level] = [None] * feat_count
    for s in range(feat_count):
        known = [0]
        for bit_level in range(bit_count - 1, 0, -1):
            for rel in known:
                held[rel ^ 2**bit_level][s] = over_members(held[rel][s], bit_level)
            known += [rel ^ 2**bit_level for rel in known]
    order = [rel for pair in sorted(held) for rel in (pair, pair ^ 1)]
    early = [held[rel][s] for rel in order[2::2] for s in range(feat_count - 1)]
    tokens = {0: after(jnp.stack(held[0], 0), *early)}
    tokens[1] = over_members(tokens[0], 0)
    partial, late_weights, weights = encode_first(
        jnp.concatenate([jnp.stack([member ^ rel for rel in order]), far]),
        [tokens[0], tokens[1]],
        enc_weight,
        dec_weight,
        layers - 1,
        len(order) - 2,
        len(order) // 2,
    )
    for rel in order[2::2]:
        tokens[rel] = jnp.stack([after(block, partial) for block in held[rel]], 0)
        tokens[rel ^ 1] = over_members(tokens[rel], 0)
    for place, rel in enumerate(order[2:-1]):
        partial = encode_next(tokens[rel], late_weights, place, partial, None)[0]
    features, mask = encode_next(
        tokens[order[-1]], late_weights, len(order) - 3, partial, enc_bias[None]
    )

    current, source = {}, features
    for k in reversed(range(layers)):
        sent, weights = decode(source, weights, groups, rows, near, dec_weight, k)
        if k > 0:
            kept, weights = decode(source, weights, groups, rows, far, dec_weight, k - 1)
        else:
            kept, weights = decode(source, weights, groups, rows)
        for place in reversed(range(len(groups))):
            current[place, k] = add_pair(kept[place], over_members(sent[place], 0))
        source = after(features, current[len(groups) - 1, k])
    turns = sorted(current, reverse=True)
    joined = {}
    for bit_level in range(1, bit_count):
        halves = {}
        for turn, value in current.items():
            split = value.reshape((value.shape[0] // 2, 2) + value.shape[1:])
            halves[turn] = (split[:, 0], split[:, 1])
        if bit_level == bit_count - 1:
            for k in range(1, layers):
                kept, sent = halves.pop((0, k))
                sent = to_layer(sent, k, sub_count)
                halves[0, 0] = (halves[0, 0][0], add_pair(halves[0, 0][1], sent))
                joined[0, k] = kept
            turns = [turn for turn in turns if turn in halves]
        received, operands = [], []
        for turn in turns:
            operand = halves[turn][1]
            if len(received) > 1:
                operand = after(operand, received[-2], operands[-1])
            operands.append(operand)
            received.append(over_members(operand, bit_level))
        for place, turn in enumerate(turns):
            arrived = after(received[place], *operands[place + 1 :][:1])
            if bit_level < bit_count - 1:
                current[turn] = add_pair(halves[turn][0], arrived)
            else:
                current[turn] = (halves[turn][0], arrived)
    blocks = [None] * feat_count
    for place in reversed(range(len(groups))):
        total = sum(part.astype(jnp.float32) for part in current[place, 0])
        for k in range(1, layers):
            if (place, k) in joined:
                moved = to_layer(after(joined[place, k], moved), k, sub_count)
            else:
                moved = to_layer(add_pair(*current[place, k]), k, sub_count)
            total = total + moved.astype(jnp.float32)
        for index, block in enumerate(groups[place]):
            blocks[block] = total[0, index]
    rebuilt = blocks[0]
    for s in reversed(range(1, feat_count)):
        rebuilt = rebuilt + over_feat(blocks[s].astype(jnp.bfloat16), s).astype(jnp.float32)
    turned_features = turned(source[None])[0]
    turned_tokens = [
        turned(after(tokens[rel], turned_features).reshape(1, tok, cols)) for rel in order
    ]
    recon_error = rebuilt - after(targets, turned_features, *turned_tokens).astype(jnp.float32)
    scaled = (loss_scale / tok * recon_error).astype(jnp.bfloat16)

    layer = lax.axis_index("layer") // sub_count
    there = [(layer + k < layers).astype(jnp.int32) for k in range(layers)]
    blocks = all_over_feat(scaled)
    stages = [[0]]
    for level in range(bit_count - 1, 0, -1):
        known = [rel for stage in stages for rel in stage]
        stages.append([rel ^ 2**level for rel in known])
    spans = [[s] for s in range(min(2, feat_count))]
    spans += [list(range(2, feat_count))] if feat_count > 2 else []
    groups_of = {(0, k): [None] * len(spans) for k in range(layers)}
    early, last = [], len(spans) - 1
    for place, group in enumerate(spans):
        stacked = jnp.stack([after(blocks[s], *early) for s in group], 0)
        groups_of[0, 0][place] = stacked
        for k in range(1, layers):
            groups_of[0, k][place] = from_layer(stacked, k, sub_count)
        known = [0]
        for level in range(bit_count - 1, 0, -1):
            for rel in known:
                other = rel ^ 2**level
                for k in range(layers):
                    if k == 0 or place < last:
                        part = over_members(groups_of[rel, k][place], level)
                    else:
                        part = from_layer(groups_of[other, 0][place], k, sub_count)
                    groups_of.setdefault((other, k), [None] * len(spans))[place] = part
            known += [rel ^ 2**level for rel in known]
        if place == last - 1:
            early = [part for parts in groups_of.values() for part in parts if part is not None]
            later = early.pop()

    feature_grad, dec_grad, squares = None, None, {}
    for number, stage in enumerate(stages):
        for k in range(layers):
            if k > 0 and number + 1 < len(stages):
                guard = [part for rel in stages[number + 1] for part in groups_of[rel, k - 1]]
                feature_grad = after(feature_grad, *guard)
            for rel in stage:
                parts = groups_of[rel, k]
                if feature_grad is not None:
                    parts = [after(part, feature_grad) for part in parts]
                groups_of[rel ^ 1, k] = [over_members(part, 0) for part in parts]
                for half in (rel, rel ^ 1):
                    if k == 0 and number > 0:
                        coming = groups_of[rel, layers - 1][-(half % 2)]
                        feature_grad = after(feature_grad, coming)
                    elif (half, k) == (1, 0):
                        feature_grad = after(feature_grad, later)
                    feature_grad, dec_grad, squares[k, half] = backward_piece(
                        jnp.stack([member ^ half, there[k]]),
                        k,
                        groups_of[half, k],
                        turned_features,
                        dec_weight,
                        feature_grad,
                        dec_grad,
                    )
    scale = (tok / loss_scale) ** 2 / (layers * tok * depth)
    enc_grad, bias_grad, mean_square = encoder_grad(
        jnp.stack([member ^ rel for rel in order]),
        turned_tokens,
        mask,
        feature_grad,
        [squares[key] for key in sorted(squares)],
        scale,
    )
    return (recon_error, mean_square[0, 0], enc_grad, bias_grad[0], dec_grad)


def solution(mesh):
    placed = (
        P("feat", "layer"),
        P("feat", "layer"),
        P(None, ("layer", "feat")),
        P(("layer", "feat")),
        P(None, ("layer", "feat"), None),
    )
    return jax.shard_map(
        on_device,
        mesh=mesh,
        in_specs=placed,
        out_specs=(
            P("feat", "layer"),
            P(),
            P(None, ("layer", "feat")),
            P(("layer", "feat")),
            P(None, ("layer", "feat"), None),
        ),
        check_vma=False,
    )
```

```python
import jax
import jax.numpy as jnp
from jax import lax
from jax.experimental import pallas as pl
from jax.experimental.pallas import tpu as pltpu
from jax.sharding import PartitionSpec as P

loss_scale = 64.0
tile = 256
in_vmem = pl.BlockSpec(memory_space=pltpu.VMEM)
in_smem = pl.BlockSpec(memory_space=pltpu.SMEM)
in_hbm = pl.BlockSpec(memory_space=pltpu.HBM)


def over_feat(value, mask):
    pairs = [(source, source ^ mask) for source in range(lax.axis_size("feat"))]
    return lax.ppermute(value, "feat", pairs)


def over_members(value, bit_level):
    mask = 2**bit_level
    pairs = [(source, source ^ mask) for source in range(lax.axis_size("layer"))]
    return lax.ppermute(value, "layer", pairs)


def to_layer(value, offset, sub_count):
    count = lax.axis_size("layer")
    shift = offset * sub_count
    pairs = [(p, p + shift) for p in range(count - shift)]
    return lax.ppermute(value, "layer", pairs)


def from_layer(value, offset, sub_count):
    count = lax.axis_size("layer")
    pairs = [(p, (p - offset * sub_count) % count) for p in range(count)]
    return lax.ppermute(value, "layer", pairs)


def after(value, *others):
    return lax.optimization_barrier((value, *others))[0]


def all_over_feat(value):
    blocks = [value, over_feat(value, 1)]
    for s in range(2, lax.axis_size("feat")):
        blocks.append(over_feat(after(value, blocks[1]) if s > 2 else value, s))
    return blocks


def params(flops, bytes_accessed, scratch_mib):
    return dict(
        compiler_params=pltpu.CompilerParams(vmem_limit_bytes=scratch_mib * 1024 * 1024),
        cost_estimate=pl.CostEstimate(
            flops=flops, bytes_accessed=bytes_accessed, transcendentals=0
        ),
    )


def dot(left, right, contract):
    return lax.dot_general(
        left, right, ((contract[:1], contract[1:]), ((), ())), preferred_element_type=jnp.float32
    )


def span(index, size):
    return pl.ds(pl.multiple_of(index * size, size), size)


def fetch(*arrays):
    parts = [(number, start) for number, array in enumerate(arrays) for start in range(4)]

    def kernel(*refs):
        copies = []
        for place, (number, start) in enumerate(parts):
            source, target = refs[number], refs[len(arrays) + number]
            size = source.shape[-2] // 4
            here = (slice(None),) * (len(source.shape) - 2) + (pl.ds(start * size, size),)
            copies.append(
                pltpu.make_async_copy(source.at[here], target.at[here], refs[-1].at[place])
            )
        for copy in copies:
            copy.start()
        for copy in copies:
            copy.wait()

    total = sum(2 * array.size for array in arrays)
    return pl.pallas_call(
        kernel,
        in_specs=[in_hbm] * len(arrays),
        out_specs=[in_vmem] * len(arrays),
        out_shape=[jax.ShapeDtypeStruct(array.shape, array.dtype) for array in arrays],
        scratch_shapes=[pltpu.SemaphoreType.DMA((len(parts),))],
        name="fetch",
        **params(0, total, 14),
    )(*arrays)


def encode(indices, pieces, weights, partial, bias):
    feat_count, rows, cols = pieces[0].shape
    tok = feat_count * rows
    width = weights.shape[1]
    extra = [value for value in (partial, bias) if value is not None]

    def kernel(index_ref, *refs):
        piece_refs, weight_ref = refs[: len(pieces)], refs[len(pieces)]
        extra_refs, out_ref = refs[len(pieces) + 1 : -1], refs[-1]
        left = jnp.concatenate([ref[...].reshape(tok, cols) for ref in piece_refs], 1)
        for start in range(0, width, tile):
            here = slice(start, start + tile)
            right = jnp.concatenate(
                [weight_ref[span(index_ref[i], cols), here] for i in range(len(pieces))], 0
            )
            total = dot(left, right, (1, 0))
            if partial is not None:
                total += extra_refs[0][:, here]
            if bias is None:
                out_ref[:, here] = total
            else:
                pre_act = total + extra_refs[-1][:, here]
                out_ref[0, :, here] = jnp.maximum(pre_act, 0.0).astype(jnp.bfloat16)
                out_ref[1, :, here] = jnp.where(pre_act > 0.0, 1.0, 0.0).astype(jnp.bfloat16)

    if bias is None:
        out_shape = jax.ShapeDtypeStruct((tok, width), jnp.float32)
    else:
        out_shape = jax.ShapeDtypeStruct((2, tok, width), jnp.bfloat16)
    return pl.pallas_call(
        kernel,
        in_specs=[in_smem] + [in_vmem] * (len(pieces) + 1 + len(extra)),
        out_specs=in_vmem,
        out_shape=out_shape,
        name="encode",
        **params(
            2 * len(pieces) * tok * cols * width, 2 * len(pieces) * cols * (tok + width), 4
        ),
    )(indices, *pieces, weights, *extra)


def decode(indices, features, weights, offset, groups, rows, cols):
    _, tok, width = features.shape
    count = indices.shape[0]

    def kernel(index_ref, feat_ref, weight_ref, *out_refs):
        left = feat_ref[0]
        for piece in range(count):
            for start in range(0, cols, tile):
                columns = pl.ds(pl.multiple_of(index_ref[piece] * cols + start, tile), tile)
                product = dot(left, weight_ref[offset, :, columns], (1, 0)).astype(jnp.bfloat16)
                for group, out_ref in zip(groups, out_refs):
                    for place, block in enumerate(group):
                        out_ref[piece, place, :, start : start + tile] = product[
                            block * rows : (block + 1) * rows
                        ]

    return pl.pallas_call(
        kernel,
        in_specs=[in_smem, in_vmem, in_vmem],
        out_specs=[in_vmem] * len(groups),
        out_shape=[
            jax.ShapeDtypeStruct((count, len(group), rows, cols), jnp.bfloat16) for group in groups
        ],
        name="decode",
        **params(2 * count * tok * cols * width, 2 * count * cols * width, 4),
    )(indices, features, weights)


def turned(value):
    count, tok, width = value.shape

    def kernel(in_ref, out_ref):
        for piece in range(count):
            for start in range(0, width, tile):
                out_ref[piece, start : start + tile, :] = in_ref[
                    piece, :, start : start + tile
                ].T

    return pl.pallas_call(
        kernel,
        in_specs=[in_vmem],
        out_specs=in_vmem,
        out_shape=jax.ShapeDtypeStruct((count, width, tok), value.dtype),
        name="turned",
        **params(0, 4 * count * tok * width, 4),
    )(value)


def tree_sum(values):
    while len(values) > 1:
        values = [values[i] + values[i + 1] for i in range(0, len(values), 2)]
    return values[0]


def backward_piece(info, offset, grads, turned_features, dec_weight, feature_grad, dec_grad):
    layers, width, depth = dec_weight.shape
    tok = turned_features.shape[1]
    cols = grads[0].shape[2]
    first = feature_grad is None
    extra = [] if first else [feature_grad, dec_grad]

    def kernel(info_ref, *refs):
        grad_refs = refs[: len(grads)]
        feat_ref, weight_ref = refs[len(grads) : len(grads) + 2]
        out_ref, dec_ref, square_ref, held, sems = refs[-5:]
        columns = span(info_ref[0], cols)
        starts = range(0, width, tile)
        copies = [
            pltpu.make_async_copy(
                held.at[slice(start, start + tile)],
                dec_ref.at[offset, slice(start, start + tile), columns],
                sems.at[place],
            )
            for place, start in enumerate(starts)
        ]
        blocks = [ref[i] for ref in grad_refs for i in range(ref.shape[0])]
        sums = []
        for block in blocks:
            total = jnp.zeros((8, 128), jnp.float32)
            for row in range(0, block.shape[0], 8):
                for col in range(0, cols, 128):
                    part = block[row : row + 8, col : col + 128].astype(jnp.float32)
                    total += part * part
            sums.append(total)
        square_ref[...] = tree_sum(sums)

        def products():
            grad = jnp.concatenate(blocks, 0)
            for copy, start in zip(copies, starts):
                here = slice(start, start + tile)
                held[here] = dot(feat_ref[here], grad, (1, 0)).astype(jnp.bfloat16)
                copy.start()
            for start in starts:
                here = slice(start, start + tile)
                product = dot(grad, weight_ref[offset, here, columns], (1, 1))
                if not first:
                    product += refs[len(grads) + 2][:, here]
                out_ref[:, here] = product

        def nothing():
            held[...] = jnp.zeros_like(held)
            for copy in copies:
                copy.start()
            out_ref[...] = refs[len(grads) + 2][...]

        if offset == 0:
            products()
        else:
            pl.when(info_ref[1] > 0)(products)
            pl.when(info_ref[1] == 0)(nothing)
        for copy in copies:
            copy.wait()

    return pl.pallas_call(
        kernel,
        in_specs=[in_smem]
        + [in_vmem] * (len(grads) + 2)
        + ([] if first else [in_vmem, in_hbm]),
        out_specs=[in_vmem, in_hbm, in_vmem],
        out_shape=[
            jax.ShapeDtypeStruct((tok, width), jnp.float32),
            jax.ShapeDtypeStruct((layers, width, depth), jnp.bfloat16),
            jax.ShapeDtypeStruct((8, 128), jnp.float32),
        ],
        scratch_shapes=[
            pltpu.VMEM((width, cols), jnp.bfloat16),
            pltpu.SemaphoreType.DMA((width // tile,)),
        ],
        input_output_aliases={} if first else {len(grads) + 3: 0, len(grads) + 4: 1},
        name="backward_piece",
        **params(tok * cols, tok * cols, 6),
    )(info, *grads, turned_features, dec_weight, *extra)


def encoder_grad(indices, turned_tokens, features, feature_grad, squares, scale):
    count, cols, tok = turned_tokens[0].shape
    width = features.shape[2]
    pieces = len(turned_tokens) * count

    def kernel(index_ref, *refs):
        token_refs = refs[: len(turned_tokens)]
        mask_ref, grad_ref = refs[len(turned_tokens) : len(turned_tokens) + 2]
        square_refs = refs[len(turned_tokens) + 2 : -6]
        enc_ref, bias_ref, mean_ref, preact, held, sems = refs[-6:]
        mean_ref[...] = scale * jnp.sum(
            tree_sum([ref[...] for ref in square_refs]), (0, 1), keepdims=True
        )
        for start in range(0, width, tile):
            here = slice(start, start + tile)
            kept = jnp.where(mask_ref[1, :, here] > 0.0, grad_ref[:, here], 0.0).astype(jnp.bfloat16)
            preact[:, here] = kept
            bias_ref[:, here] = jnp.sum(kept.astype(jnp.float32), 0, keepdims=True)
        copies = []
        for piece in range(pieces):
            held[piece] = dot(
                token_refs[piece // count][piece % count], preact[...], (1, 0)
            ).astype(jnp.bfloat16)
            copy = pltpu.make_async_copy(
                held.at[piece], enc_ref.at[span(index_ref[piece], cols)], sems.at[piece]
            )
            copy.start()
            copies.append(copy)
        for copy in copies:
            copy.wait()

    return pl.pallas_call(
        kernel,
        in_specs=[in_smem] + [in_vmem] * (len(turned_tokens) + 2 + len(squares)),
        out_specs=[in_hbm, in_vmem, in_vmem],
        out_shape=[
            jax.ShapeDtypeStruct((pieces * cols, width), jnp.bfloat16),
            jax.ShapeDtypeStruct((1, width), jnp.float32),
            jax.ShapeDtypeStruct((1, 1), jnp.float32),
        ],
        scratch_shapes=[
            pltpu.VMEM((tok, width), jnp.bfloat16),
            pltpu.VMEM((pieces, cols, width), jnp.bfloat16),
            pltpu.SemaphoreType.DMA((pieces,)),
        ],
        name="encoder_grad",
        **params(
            2 * pieces * tok * cols * width, 2 * pieces * cols * (tok + width) + 6 * tok * width, 10
        ),
    )(indices, *turned_tokens, features, feature_grad, *squares)


def add_pair(left, right):
    return (left.astype(jnp.float32) + right.astype(jnp.float32)).astype(jnp.bfloat16)


def on_device(tokens_in, targets, enc_weight, enc_bias, dec_weight):
    layers, width, depth = dec_weight.shape
    feat_count = lax.axis_size("feat")
    sub_count = lax.axis_size("layer") // layers
    member = lax.axis_index("layer") % sub_count
    rows, cols = tokens_in.shape
    tok = feat_count * rows
    bit_count = sub_count.bit_length() - 1
    near = member ^ (2 * jnp.arange(sub_count // 2, dtype=jnp.int32))
    far = near ^ 1
    groups = [list(range(feat_count // 2)), list(range(feat_count // 2, feat_count))]

    enc_weight = pltpu.with_memory_space_constraint(enc_weight, pltpu.HBM)
    dec_weight = pltpu.with_memory_space_constraint(dec_weight, pltpu.HBM)

    held = {0: all_over_feat(tokens_in)}
    for bit_level in range(bit_count - 1, 0, -1):
        for rel in list(held):
            held[rel ^ 2**bit_level] = [None] * feat_count
    for s in range(feat_count):
        known = [0]
        for bit_level in range(bit_count - 1, 0, -1):
            for rel in known:
                held[rel ^ 2**bit_level][s] = over_members(held[rel][s], bit_level)
            known += [rel ^ 2**bit_level for rel in known]
    order = [rel for pair in sorted(held) for rel in (pair, pair ^ 1)]
    enc_held, dec_held = fetch(enc_weight, after(dec_weight, held[0][1]))
    early = [held[rel][s] for rel in order[2::2] for s in range(2)]
    tokens = {0: after(jnp.stack(held[0], 0), enc_held, *early)}
    tokens[1] = over_members(tokens[0], 0)
    index = {rel: (member ^ rel).reshape(1) for rel in order}
    partial = encode(
        jnp.concatenate([index[0], index[1]]), [tokens[0], tokens[1]], enc_held, None, None
    )
    for rel in order[2::2]:
        tokens[rel] = jnp.stack([after(block, partial) for block in held[rel]], 0)
        tokens[rel ^ 1] = over_members(tokens[rel], 0)
    for rel in order[2:-1]:
        partial = encode(index[rel], [tokens[rel]], enc_held, partial, None)
    features = encode(index[order[-1]], [tokens[order[-1]]], enc_held, partial, enc_bias[None])

    current, source = {}, features
    for k in reversed(range(layers)):
        sent = decode(far, source, dec_held, k, groups, rows, cols)
        kept = decode(near, source, dec_held, k, groups, rows, cols)
        for place in reversed(range(len(groups))):
            current[place, k] = add_pair(kept[place], over_members(sent[place], 0))
        source = after(features, current[len(groups) - 1, k])
    turns = sorted(current, reverse=True)
    joined = {}
    for bit_level in range(1, bit_count):
        halves = {}
        for turn, value in current.items():
            split = value.reshape((value.shape[0] // 2, 2) + value.shape[1:])
            halves[turn] = (split[:, 0], split[:, 1])
        if bit_level == bit_count - 1:
            for k in range(1, layers):
                joined[k], sent = halves.pop((0, k))
                sent = to_layer(sent, k, sub_count)
                halves[0, 0] = (halves[0, 0][0], add_pair(halves[0, 0][1], sent))
        turns = [turn for turn in turns if turn in halves]
        received, operands = [], []
        for turn in turns:
            operand = halves[turn][1]
            if len(received) > 1:
                operand = after(operand, received[-2], operands[-1])
            operands.append(operand)
            received.append(over_members(operand, bit_level))
        for place, turn in enumerate(turns):
            arrived = after(received[place], *operands[place + 1 :][:1])
            if bit_level < bit_count - 1:
                current[turn] = add_pair(halves[turn][0], arrived)
            else:
                current[turn] = (halves[turn][0], arrived)
    blocks, operands = [None] * feat_count, []
    for place in reversed(range(len(groups))):
        total = sum(part.astype(jnp.float32) for part in current[place, 0])
        for k in range(1, layers):
            if place > 0:
                moved = to_layer(add_pair(*current[place, k]), k, sub_count)
            else:
                moved = to_layer(after(joined[k], *operands), k, sub_count)
            total = total + moved.astype(jnp.float32)
        for spot, block in enumerate(groups[place]):
            if block == 0:
                rebuilt = total[0, spot]
            else:
                operands.append(total[0, spot].astype(jnp.bfloat16))
                blocks[block] = over_feat(operands[-1], block)
    for block in reversed(blocks[1:]):
        rebuilt = rebuilt + block.astype(jnp.float32)
    turned_features = turned(source[:1])[0]
    turned_tokens = [
        turned(after(tokens[rel], turned_features).reshape(1, tok, cols)) for rel in order
    ]
    (dec_held,) = fetch(after(dec_weight, turned_features))
    recon_error = rebuilt - after(targets, dec_held, *turned_tokens).astype(jnp.float32)
    scaled = (loss_scale / tok * recon_error).astype(jnp.bfloat16)

    layer = lax.axis_index("layer") // sub_count
    there = [(layer + k < layers).astype(jnp.int32) for k in range(layers)]
    blocks = all_over_feat(scaled)
    stages = [[0]]
    for level in range(bit_count - 1, 0, -1):
        known = [rel for stage in stages for rel in stage]
        stages.append([rel ^ 2**level for rel in known])
    spans = [[s] for s in range(min(2, feat_count))]
    spans += [list(range(2, feat_count))] if feat_count > 2 else []
    groups_of = {(0, k): [None] * len(spans) for k in range(layers)}
    early, last = [], len(spans) - 1
    for place, group in enumerate(spans):
        stacked = jnp.stack([after(blocks[s], *early) for s in group], 0)
        groups_of[0, 0][place] = stacked
        for k in range(1, layers):
            groups_of[0, k][place] = from_layer(stacked, k, sub_count)
        known = [0]
        for level in range(bit_count - 1, 0, -1):
            for rel in known:
                other = rel ^ 2**level
                for k in range(layers):
                    if k == 0 or place < last:
                        part = over_members(groups_of[rel, k][place], level)
                    else:
                        part = from_layer(groups_of[other, 0][place], k, sub_count)
                    groups_of.setdefault((other, k), [None] * len(spans))[place] = part
            known += [rel ^ 2**level for rel in known]
        if place == last - 1:
            early = [part for parts in groups_of.values() for part in parts if part is not None]
            early.pop()

    feature_grad, dec_grad, squares = None, None, {}
    for number, stage in enumerate(stages):
        for k in range(layers):
            if k > 0 and number + 1 < len(stages):
                guard = [part for rel in stages[number + 1] for part in groups_of[rel, k - 1]]
                feature_grad = after(feature_grad, *guard)
            for rel in stage:
                parts = groups_of[rel, k]
                if feature_grad is not None:
                    parts = [after(part, feature_grad) for part in parts]
                groups_of[rel ^ 1, k] = [over_members(part, 0) for part in parts]
                for half in (rel, rel ^ 1):
                    if k == 0 and number > 0:
                        coming = groups_of[rel, layers - 1][-(half % 2)]
                        feature_grad = after(feature_grad, coming)
                    feature_grad, dec_grad, squares[k, half] = backward_piece(
                        jnp.stack([member ^ half, there[k]]),
                        k,
                        groups_of[half, k],
                        turned_features,
                        dec_held,
                        feature_grad,
                        dec_grad,
                    )
    scale = (tok / loss_scale) ** 2 / (layers * tok * depth)
    enc_grad, bias_grad, mean_square = encoder_grad(
        jnp.stack([member ^ rel for rel in order]),
        turned_tokens,
        features,
        feature_grad,
        [squares[key] for key in sorted(squares)],
        scale,
    )
    return (recon_error, mean_square[0, 0], enc_grad, bias_grad[0], dec_grad)


def solution(mesh):
    placed = (
        P("feat", "layer"),
        P("feat", "layer"),
        P(None, ("layer", "feat")),
        P(("layer", "feat")),
        P(None, ("layer", "feat"), None),
    )
    return jax.shard_map(
        on_device,
        mesh=mesh,
        in_specs=placed,
        out_specs=(
            P("feat", "layer"),
            P(),
            P(None, ("layer", "feat")),
            P(("layer", "feat")),
            P(None, ("layer", "feat"), None),
        ),
        check_vma=False,
    )
```

```python
import jax
import jax.numpy as jnp
from jax import lax
from jax.experimental import pallas as pl
from jax.experimental.pallas import tpu as pltpu
from jax.sharding import PartitionSpec as P

loss_scale = 64.0
tile = 256
in_vmem = pl.BlockSpec(memory_space=pltpu.VMEM)
in_smem = pl.BlockSpec(memory_space=pltpu.SMEM)
in_hbm = pl.BlockSpec(memory_space=pltpu.HBM)


def over_feat(value, mask):
    pairs = [(source, source ^ mask) for source in range(lax.axis_size("feat"))]
    return lax.ppermute(value, "feat", pairs)


def over_members(value, bit_level):
    mask = 2**bit_level
    pairs = [(source, source ^ mask) for source in range(lax.axis_size("layer"))]
    return lax.ppermute(value, "layer", pairs)


def to_layer(value, offset, sub_count):
    count = lax.axis_size("layer")
    shift = offset * sub_count
    pairs = [(p, p + shift) for p in range(count - shift)]
    return lax.ppermute(value, "layer", pairs)


def from_layer(value, offset, sub_count):
    count = lax.axis_size("layer")
    pairs = [(p, (p - offset * sub_count) % count) for p in range(count)]
    return lax.ppermute(value, "layer", pairs)


def after(value, *others):
    return lax.optimization_barrier((value, *others))[0]


def all_over_feat(value):
    blocks = [value, over_feat(value, 1)]
    for s in range(2, lax.axis_size("feat")):
        blocks.append(over_feat(value, s))
    return blocks


def params(flops, bytes_accessed, scratch_mib):
    return dict(
        compiler_params=pltpu.CompilerParams(vmem_limit_bytes=scratch_mib * 1024 * 1024),
        cost_estimate=pl.CostEstimate(
            flops=flops, bytes_accessed=bytes_accessed, transcendentals=0
        ),
    )


def dot(left, right, contract):
    return lax.dot_general(
        left, right, ((contract[:1], contract[1:]), ((), ())), preferred_element_type=jnp.float32
    )


def span(index, size):
    return pl.ds(pl.multiple_of(index * size, size), size)


def in_parts(source, target, sems, first, count=8):
    size = target.shape[0] // count
    return [
        pltpu.make_async_copy(
            source.at[pl.ds(part * size, size)],
            target.at[pl.ds(part * size, size)],
            sems.at[first + part],
        )
        for part in range(count)
    ]


def encode_first(indices, pieces, enc_weight, dec_weight, offset, late, ahead):
    feat_count, rows, cols = pieces[0].shape
    tok = feat_count * rows
    width = enc_weight.shape[1]
    now = len(pieces)

    def kernel(index_ref, *refs):
        piece_refs = refs[:now]
        weight_ref, next_ref, out_ref, late_ref, ahead_ref, held, sems = refs[now:]
        copies = []
        for i in range(now + late):
            target = held.at[i] if i < now else late_ref.at[i - now]
            source = weight_ref.at[span(index_ref[i], cols)]
            copies += in_parts(source, target, sems, 8 * i)
        for i in range(ahead):
            source = next_ref.at[offset, :, span(index_ref[now + late + i], cols)]
            copies += in_parts(source, ahead_ref.at[i], sems, 8 * (now + late + i))
        for copy in copies:
            copy.start()
        for copy in copies[: 8 * now]:
            copy.wait()
        left = jnp.concatenate([ref[...].reshape(tok, cols) for ref in piece_refs], 1)
        for start in range(0, width, tile):
            here = slice(start, start + tile)
            right = jnp.concatenate([held[i, :, here] for i in range(now)], 0)
            out_ref[:, here] = dot(left, right, (1, 0))
        for copy in copies[8 * now :]:
            copy.wait()

    return pl.pallas_call(
        kernel,
        in_specs=[in_smem] + [in_vmem] * now + [in_hbm] * 2,
        out_specs=[in_vmem] * 3,
        out_shape=[
            jax.ShapeDtypeStruct((tok, width), jnp.float32),
            jax.ShapeDtypeStruct((late, cols, width), jnp.bfloat16),
            jax.ShapeDtypeStruct((ahead, width, cols), jnp.bfloat16),
        ],
        scratch_shapes=[
            pltpu.VMEM((now, cols, width), jnp.bfloat16),
            pltpu.SemaphoreType.DMA((8 * (now + late + ahead),)),
        ],
        name="encode_first",
        **params(2 * now * tok * cols * width, 2 * (now + late + 2 * ahead) * cols * width, 12),
    )(indices, *pieces, enc_weight, dec_weight)


def encode_next(piece, weights, place, partial, bias):
    feat_count, rows, cols = piece.shape
    tok = feat_count * rows
    width = weights.shape[2]
    extra = [partial] if bias is None else [partial, bias]

    def kernel(piece_ref, weight_ref, partial_ref, *refs):
        left = piece_ref[...].reshape(tok, cols)
        for start in range(0, width, tile):
            here = slice(start, start + tile)
            total = partial_ref[:, here] + dot(left, weight_ref[place, :, here], (1, 0))
            if bias is None:
                refs[0][:, here] = total
            else:
                pre_act = total + refs[0][:, here]
                refs[1][0, :, here] = jnp.maximum(pre_act, 0.0).astype(jnp.bfloat16)
                refs[1][1, :, here] = jnp.where(pre_act > 0.0, 1.0, 0.0).astype(jnp.bfloat16)

    if bias is None:
        out_shape = jax.ShapeDtypeStruct((tok, width), jnp.float32)
    else:
        out_shape = jax.ShapeDtypeStruct((2, tok, width), jnp.bfloat16)
    return pl.pallas_call(
        kernel,
        in_specs=[in_vmem] * (2 + len(extra)),
        out_specs=in_vmem,
        out_shape=out_shape,
        name="encode_next",
        **params(2 * tok * cols * width, 2 * cols * width, 8),
    )(piece, weights, *extra)


def decode(features, weights, groups, rows, indices=None, dec_weight=None, offset=None):
    _, tok, width = features.shape
    count, _, cols = weights.shape
    ahead = indices is not None

    def kernel(feat_ref, weight_ref, *refs):
        if ahead:
            index_ref, next_ref = refs[:2]
            out_refs, next_out, sems = refs[2:-2], refs[-2], refs[-1]
            copies = []
            for i in range(count):
                source = next_ref.at[offset, :, span(index_ref[i], cols)]
                copies += in_parts(source, next_out.at[i], sems, 8 * i)
            for copy in copies:
                copy.start()
        else:
            out_refs = refs
        left = feat_ref[0]
        for piece in range(count):
            for start in range(0, cols, tile):
                here = slice(start, start + tile)
                product = dot(left, weight_ref[piece, :, here], (1, 0)).astype(jnp.bfloat16)
                for group, out_ref in zip(groups, out_refs):
                    for place, block in enumerate(group):
                        out_ref[piece, place, :, here] = product[block * rows : (block + 1) * rows]
        if ahead:
            for copy in copies:
                copy.wait()

    out_shape = [
        jax.ShapeDtypeStruct((count, len(group), rows, cols), jnp.bfloat16) for group in groups
    ]
    if ahead:
        out_shape.append(jax.ShapeDtypeStruct((count, width, cols), jnp.bfloat16))
    result = pl.pallas_call(
        kernel,
        in_specs=[in_vmem] * 2 + ([in_smem, in_hbm] if ahead else []),
        out_specs=[in_vmem] * len(out_shape),
        out_shape=out_shape,
        scratch_shapes=[pltpu.SemaphoreType.DMA((8 * count,))] if ahead else [],
        name="decode",
        **params(2 * count * tok * cols * width, 2 * count * cols * width, 8),
    )(features, weights, *([indices, dec_weight] if ahead else []))
    return result[: len(groups)], (result[-1] if ahead else None)


def turned(value):
    count, tok, width = value.shape

    def kernel(in_ref, out_ref):
        for piece in range(count):
            for start in range(0, width, tile):
                out_ref[piece, start : start + tile, :] = in_ref[
                    piece, :, start : start + tile
                ].T

    return pl.pallas_call(
        kernel,
        in_specs=[in_vmem],
        out_specs=in_vmem,
        out_shape=jax.ShapeDtypeStruct((count, width, tok), value.dtype),
        name="turned",
        **params(0, 4 * count * tok * width, 4),
    )(value)


def tree_sum(values):
    while len(values) > 1:
        values = [values[i] + values[i + 1] for i in range(0, len(values), 2)]
    return values[0]


def backward_piece(info, offset, grads, turned_features, dec_weight, feature_grad, dec_grad):
    layers, width, depth = dec_weight.shape
    tok = turned_features.shape[1]
    cols = grads[0].shape[2]
    first = feature_grad is None
    extra = [] if first else [feature_grad, dec_grad]

    def kernel(info_ref, *refs):
        grad_refs = refs[: len(grads)]
        feat_ref, weight_ref = refs[len(grads) : len(grads) + 2]
        out_ref, dec_ref, square_ref, held, weights, sems = refs[-6:]
        columns = span(info_ref[0], cols)
        starts = range(0, width, tile)
        fetches = in_parts(weight_ref.at[offset, :, columns], weights, sems, len(starts))
        for fetch in fetches:
            fetch.start()
        copies = [
            pltpu.make_async_copy(
                held.at[slice(start, start + tile)],
                dec_ref.at[offset, slice(start, start + tile), columns],
                sems.at[place],
            )
            for place, start in enumerate(starts)
        ]
        blocks = [ref[i] for ref in grad_refs for i in range(ref.shape[0])]
        sums = []
        for block in blocks:
            total = jnp.zeros((8, 128), jnp.float32)
            for row in range(0, block.shape[0], 8):
                for col in range(0, cols, 128):
                    part = block[row : row + 8, col : col + 128].astype(jnp.float32)
                    total += part * part
            sums.append(total)
        square_ref[...] = tree_sum(sums)

        def products():
            grad = jnp.concatenate(blocks, 0)
            for copy, start in zip(copies, starts):
                here = slice(start, start + tile)
                held[here] = dot(feat_ref[here], grad, (1, 0)).astype(jnp.bfloat16)
                copy.start()
            for fetch in fetches:
                fetch.wait()
            for start in starts:
                here = slice(start, start + tile)
                product = dot(grad, weights[here], (1, 1))
                if not first:
                    product += refs[len(grads) + 2][:, here]
                out_ref[:, here] = product

        def nothing():
            held[...] = jnp.zeros_like(held)
            for copy in copies:
                copy.start()
            out_ref[...] = refs[len(grads) + 2][...]
            for fetch in fetches:
                fetch.wait()

        if offset == 0:
            products()
        else:
            pl.when(info_ref[1] > 0)(products)
            pl.when(info_ref[1] == 0)(nothing)
        for copy in copies:
            copy.wait()

    return pl.pallas_call(
        kernel,
        in_specs=[in_smem]
        + [in_vmem] * (len(grads) + 1)
        + [in_hbm]
        + ([] if first else [in_vmem, in_hbm]),
        out_specs=[in_vmem, in_hbm, in_vmem],
        out_shape=[
            jax.ShapeDtypeStruct((tok, width), jnp.float32),
            jax.ShapeDtypeStruct((layers, width, depth), jnp.bfloat16),
            jax.ShapeDtypeStruct((8, 128), jnp.float32),
        ],
        scratch_shapes=[
            pltpu.VMEM((width, cols), jnp.bfloat16),
            pltpu.VMEM((width, cols), jnp.bfloat16),
            pltpu.SemaphoreType.DMA((width // tile + 8,)),
        ],
        input_output_aliases={} if first else {len(grads) + 3: 0, len(grads) + 4: 1},
        name="backward_piece",
        **params(tok * cols, tok * cols, 6),
    )(info, *grads, turned_features, dec_weight, *extra)


def encoder_grad(indices, turned_tokens, features, feature_grad, squares, scale):
    count, cols, tok = turned_tokens[0].shape
    width = features.shape[2]
    pieces = len(turned_tokens) * count

    def kernel(index_ref, *refs):
        token_refs = refs[: len(turned_tokens)]
        mask_ref, grad_ref = refs[len(turned_tokens) : len(turned_tokens) + 2]
        square_refs = refs[len(turned_tokens) + 2 : -6]
        enc_ref, bias_ref, mean_ref, preact, held, sems = refs[-6:]
        mean_ref[...] = scale * jnp.sum(
            tree_sum([ref[...] for ref in square_refs]), (0, 1), keepdims=True
        )
        for start in range(0, width, tile):
            here = slice(start, start + tile)
            kept = jnp.where(mask_ref[1, :, here] > 0.0, grad_ref[:, here], 0.0).astype(jnp.bfloat16)
            preact[:, here] = kept
            bias_ref[:, here] = jnp.sum(kept.astype(jnp.float32), 0, keepdims=True)
        copies = []
        for piece in range(pieces):
            held[piece] = dot(
                token_refs[piece // count][piece % count], preact[...], (1, 0)
            ).astype(jnp.bfloat16)
            copy = pltpu.make_async_copy(
                held.at[piece], enc_ref.at[span(index_ref[piece], cols)], sems.at[piece]
            )
            copy.start()
            copies.append(copy)
        for copy in copies:
            copy.wait()

    return pl.pallas_call(
        kernel,
        in_specs=[in_smem] + [in_vmem] * (len(turned_tokens) + 2 + len(squares)),
        out_specs=[in_hbm, in_vmem, in_vmem],
        out_shape=[
            jax.ShapeDtypeStruct((pieces * cols, width), jnp.bfloat16),
            jax.ShapeDtypeStruct((1, width), jnp.float32),
            jax.ShapeDtypeStruct((1, 1), jnp.float32),
        ],
        scratch_shapes=[
            pltpu.VMEM((tok, width), jnp.bfloat16),
            pltpu.VMEM((pieces, cols, width), jnp.bfloat16),
            pltpu.SemaphoreType.DMA((pieces,)),
        ],
        name="encoder_grad",
        **params(
            2 * pieces * tok * cols * width, 2 * pieces * cols * (tok + width) + 6 * tok * width, 10
        ),
    )(indices, *turned_tokens, features, feature_grad, *squares)


def add_pair(left, right):
    return (left.astype(jnp.float32) + right.astype(jnp.float32)).astype(jnp.bfloat16)


def on_device(tokens_in, targets, enc_weight, enc_bias, dec_weight):
    layers, width, depth = dec_weight.shape
    feat_count = lax.axis_size("feat")
    sub_count = lax.axis_size("layer") // layers
    member = lax.axis_index("layer") % sub_count
    rows, cols = tokens_in.shape
    tok = feat_count * rows
    bit_count = sub_count.bit_length() - 1
    near = member ^ (2 * jnp.arange(sub_count // 2, dtype=jnp.int32))
    far = near ^ 1
    groups = [list(range(feat_count // 2))]
    groups += [[s] for s in range(feat_count // 2, feat_count)]

    enc_weight = pltpu.with_memory_space_constraint(enc_weight, pltpu.HBM)
    dec_weight = pltpu.with_memory_space_constraint(dec_weight, pltpu.HBM)

    held = {0: all_over_feat(tokens_in)}
    for bit_level in range(bit_count - 1, 0, -1):
        for rel in list(held):
            held[rel ^ 2**bit_level] = [None] * feat_count
    for s in range(feat_count):
        known = [0]
        for bit_level in range(bit_count - 1, 0, -1):
            for rel in known:
                held[rel ^ 2**bit_level][s] = over_members(held[rel][s], bit_level)
            known += [rel ^ 2**bit_level for rel in known]
    order = [rel for pair in sorted(held) for rel in (pair, pair ^ 1)]
    early = [held[rel][s] for rel in order[2::2] for s in range(2)]
    tokens = {0: after(jnp.stack(held[0], 0), *early)}
    tokens[1] = over_members(tokens[0], 0)
    partial, late_weights, weights = encode_first(
        jnp.concatenate([jnp.stack([member ^ rel for rel in order]), far]),
        [tokens[0], tokens[1]],
        enc_weight,
        dec_weight,
        layers - 1,
        len(order) - 2,
        len(order) // 2,
    )
    for rel in order[2::2]:
        tokens[rel] = jnp.stack([after(block, partial) for block in held[rel]], 0)
        tokens[rel ^ 1] = over_members(tokens[rel], 0)
    for place, rel in enumerate(order[2:-1]):
        partial = encode_next(tokens[rel], late_weights, place, partial, None)
    features = encode_next(
        tokens[order[-1]], late_weights, len(order) - 3, partial, enc_bias[None]
    )

    current, source = {}, features
    for k in reversed(range(layers)):
        sent, weights = decode(source, weights, groups, rows, near, dec_weight, k)
        if k > 0:
            kept, weights = decode(source, weights, groups, rows, far, dec_weight, k - 1)
        else:
            kept, weights = decode(source, weights, groups, rows)
        for place in reversed(range(len(groups))):
            current[place, k] = add_pair(kept[place], over_members(sent[place], 0))
        source = after(features, current[len(groups) - 1, k])
    turns = sorted(current, reverse=True)
    joined = {}
    for bit_level in range(1, bit_count):
        halves = {}
        for turn, value in current.items():
            split = value.reshape((value.shape[0] // 2, 2) + value.shape[1:])
            halves[turn] = (split[:, 0], split[:, 1])
        if bit_level == bit_count - 1:
            for k in range(1, layers):
                joined[k], sent = halves.pop((0, k))
                sent = to_layer(after(sent, halves[len(groups) - 1, 0][1]), k, sub_count)
                halves[0, 0] = (halves[0, 0][0], add_pair(halves[0, 0][1], sent))
        turns = [turn for turn in turns if turn in halves]
        received, operands = [], []
        for turn in turns:
            operand = halves[turn][1]
            if len(received) > 1:
                operand = after(operand, received[-2], operands[-1])
            operands.append(operand)
            received.append(over_members(operand, bit_level))
        for place, turn in enumerate(turns):
            arrived = after(received[place], *operands[place + 1 :][:1])
            if bit_level < bit_count - 1:
                current[turn] = add_pair(halves[turn][0], arrived)
            else:
                current[turn] = (halves[turn][0], arrived)
    blocks, operands = [None] * feat_count, []
    for place in reversed(range(len(groups))):
        total = sum(part.astype(jnp.float32) for part in current[place, 0])
        for k in range(1, layers):
            if place > 0:
                moved = to_layer(add_pair(*current[place, k]), k, sub_count)
            else:
                moved = to_layer(after(joined[k], *operands), k, sub_count)
            total = total + moved.astype(jnp.float32)
        for spot, block in enumerate(groups[place]):
            if block == 0:
                rebuilt = total[0, spot]
            else:
                operands.append(total[0, spot].astype(jnp.bfloat16))
                blocks[block] = over_feat(operands[-1], block)
    for block in reversed(blocks[1:]):
        rebuilt = rebuilt + block.astype(jnp.float32)
    turned_features = turned(source[:1])[0]
    turned_tokens = [
        turned(after(tokens[rel], turned_features).reshape(1, tok, cols)) for rel in order
    ]
    recon_error = rebuilt - after(targets, turned_features, *turned_tokens).astype(jnp.float32)
    scaled = (loss_scale / tok * recon_error).astype(jnp.bfloat16)

    layer = lax.axis_index("layer") // sub_count
    there = [(layer + k < layers).astype(jnp.int32) for k in range(layers)]
    blocks = all_over_feat(scaled)
    stages = [[0]]
    for level in range(bit_count - 1, 0, -1):
        known = [rel for stage in stages for rel in stage]
        stages.append([rel ^ 2**level for rel in known])
    spans = [[s] for s in range(min(2, feat_count))]
    spans += [list(range(2, feat_count))] if feat_count > 2 else []
    groups_of = {(0, k): [None] * len(spans) for k in range(layers)}
    early, last = [], len(spans) - 1
    for place, group in enumerate(spans):
        stacked = jnp.stack([blocks[s] for s in group], 0)
        groups_of[0, 0][place] = stacked
        for k in range(1, layers):
            groups_of[0, k][place] = from_layer(stacked, k, sub_count)
        known = [0]
        for level in range(bit_count - 1, 0, -1):
            for rel in known:
                other = rel ^ 2**level
                for k in range(layers):
                    if k == 0 or place < last:
                        part = over_members(groups_of[rel, k][place], level)
                    else:
                        part = from_layer(groups_of[other, 0][place], k, sub_count)
                    groups_of.setdefault((other, k), [None] * len(spans))[place] = part
            known += [rel ^ 2**level for rel in known]
        if place == last - 1:
            early = [part for parts in groups_of.values() for part in parts if part is not None]
            early.pop()

    feature_grad, dec_grad, squares = None, None, {}
    for number, stage in enumerate(stages):
        for k in range(layers):
            if k > 0 and number + 1 < len(stages):
                guard = [part for rel in stages[number + 1] for part in groups_of[rel, k - 1]]
                feature_grad = after(feature_grad, *guard)
            for rel in stage:
                parts = groups_of[rel, k]
                if feature_grad is not None:
                    parts = [after(part, feature_grad) for part in parts]
                groups_of[rel ^ 1, k] = [over_members(part, 0) for part in parts]
                if feature_grad is None:
                    groups_of[rel, k][0] = after(parts[0], *early)
                for half in (rel, rel ^ 1):
                    if k == 0 and number > 0:
                        coming = groups_of[rel, layers - 1][-(half % 2)]
                        feature_grad = after(feature_grad, coming)
                    feature_grad, dec_grad, squares[k, half] = backward_piece(
                        jnp.stack([member ^ half, there[k]]),
                        k,
                        groups_of[half, k],
                        turned_features,
                        dec_weight,
                        feature_grad,
                        dec_grad,
                    )
    scale = (tok / loss_scale) ** 2 / (layers * tok * depth)
    enc_grad, bias_grad, mean_square = encoder_grad(
        jnp.stack([member ^ rel for rel in order]),
        turned_tokens,
        features,
        feature_grad,
        [squares[key] for key in sorted(squares)],
        scale,
    )
    return (recon_error, mean_square[0, 0], enc_grad, bias_grad[0], dec_grad)


def solution(mesh):
    placed = (
        P("feat", "layer"),
        P("feat", "layer"),
        P(None, ("layer", "feat")),
        P(("layer", "feat")),
        P(None, ("layer", "feat"), None),
    )
    return jax.shard_map(
        on_device,
        mesh=mesh,
        in_specs=placed,
        out_specs=(
            P("feat", "layer"),
            P(),
            P(None, ("layer", "feat")),
            P(("layer", "feat")),
            P(None, ("layer", "feat"), None),
        ),
        check_vma=False,
    )
```

```python
import jax
import jax.numpy as jnp
from jax import lax
from jax.experimental import pallas as pl
from jax.experimental.pallas import tpu as pltpu
from jax.sharding import PartitionSpec as P

loss_scale = 64.0
tile = 256
in_vmem = pl.BlockSpec(memory_space=pltpu.VMEM)
in_smem = pl.BlockSpec(memory_space=pltpu.SMEM)
in_hbm = pl.BlockSpec(memory_space=pltpu.HBM)


def over_feat(value, mask):
    pairs = [(source, source ^ mask) for source in range(lax.axis_size("feat"))]
    return lax.ppermute(value, "feat", pairs)


def over_members(value, bit_level):
    mask = 2**bit_level
    pairs = [(source, source ^ mask) for source in range(lax.axis_size("layer"))]
    return lax.ppermute(value, "layer", pairs)


def to_layer(value, offset, sub_count):
    count = lax.axis_size("layer")
    pairs = [(p, (p + offset * sub_count) % count) for p in range(count)]
    moved = lax.ppermute(value, "layer", pairs)
    real = lax.axis_index("layer") >= offset * sub_count
    return jnp.where(real, moved, jnp.zeros_like(moved))


def from_layer(value, offset, sub_count):
    count = lax.axis_size("layer")
    pairs = [(p, (p - offset * sub_count) % count) for p in range(count)]
    return lax.ppermute(value, "layer", pairs)


def after(value, *others):
    return lax.optimization_barrier((value, *others))[0]


def all_over_feat(value):
    blocks = [value, over_feat(value, 1)]
    for s in range(2, lax.axis_size("feat")):
        blocks.append(over_feat(value, s))
    return blocks


def params(flops, bytes_accessed, scratch_mib):
    return dict(
        compiler_params=pltpu.CompilerParams(vmem_limit_bytes=scratch_mib * 1024 * 1024),
        cost_estimate=pl.CostEstimate(
            flops=flops, bytes_accessed=bytes_accessed, transcendentals=0
        ),
    )


def dot(left, right, contract):
    return lax.dot_general(
        left, right, ((contract[:1], contract[1:]), ((), ())), preferred_element_type=jnp.float32
    )


def span(index, size):
    return pl.ds(pl.multiple_of(index * size, size), size)


def in_parts(source, target, sems, first, count=4):
    size = target.shape[0] // count
    return [
        pltpu.make_async_copy(
            source.at[pl.ds(part * size, size)],
            target.at[pl.ds(part * size, size)],
            sems.at[first + part],
        )
        for part in range(count)
    ]


def encode_first(indices, pieces, enc_weight, dec_weight, offset, late):
    feat_count, rows, cols = pieces[0].shape
    tok = feat_count * rows
    width = enc_weight.shape[1]
    now = len(pieces)

    def kernel(index_ref, *refs):
        piece_refs = refs[:now]
        weight_ref, next_ref, out_ref, late_ref, ahead_ref, held, sems = refs[now:]
        copies = []
        for i in range(now + late):
            target = held.at[i] if i < now else late_ref.at[i - now]
            source = weight_ref.at[span(index_ref[i], cols)]
            copies += in_parts(source, target, sems, 4 * i)
        copies += in_parts(next_ref.at[offset], ahead_ref, sems, 4 * (now + late))
        for copy in copies:
            copy.start()
        for copy in copies[: 4 * now]:
            copy.wait()
        left = jnp.concatenate([ref[...].reshape(tok, cols) for ref in piece_refs], 1)
        for start in range(0, width, tile):
            here = slice(start, start + tile)
            right = jnp.concatenate([held[i, :, here] for i in range(now)], 0)
            out_ref[:, here] = dot(left, right, (1, 0))
        for copy in copies[4 * now :]:
            copy.wait()

    return pl.pallas_call(
        kernel,
        in_specs=[in_smem] + [in_vmem] * now + [in_hbm] * 2,
        out_specs=[in_vmem] * 3,
        out_shape=[
            jax.ShapeDtypeStruct((tok, width), jnp.float32),
            jax.ShapeDtypeStruct((late, cols, width), jnp.bfloat16),
            jax.ShapeDtypeStruct(dec_weight.shape[1:], jnp.bfloat16),
        ],
        scratch_shapes=[
            pltpu.VMEM((now, cols, width), jnp.bfloat16),
            pltpu.SemaphoreType.DMA((4 * (now + late + 1),)),
        ],
        name="encode_first",
        **params(2 * now * tok * cols * width, 4 * (now + late) * cols * width, 6),
    )(indices, *pieces, enc_weight, dec_weight)


def encode_next(piece, weights, place, partial, bias):
    feat_count, rows, cols = piece.shape
    tok = feat_count * rows
    width = weights.shape[2]
    extra = [partial] if bias is None else [partial, bias]

    def kernel(piece_ref, weight_ref, partial_ref, *refs):
        left = piece_ref[...].reshape(tok, cols)
        for start in range(0, width, tile):
            here = slice(start, start + tile)
            total = partial_ref[:, here] + dot(left, weight_ref[place, :, here], (1, 0))
            if bias is None:
                refs[0][:, here] = total
            else:
                pre_act = total + refs[0][:, here]
                refs[1][0, :, here] = jnp.maximum(pre_act, 0.0).astype(jnp.bfloat16)
                refs[1][1, :, here] = jnp.where(pre_act > 0.0, 1.0, 0.0).astype(jnp.bfloat16)

    if bias is None:
        out_shape = jax.ShapeDtypeStruct((tok, width), jnp.float32)
    else:
        out_shape = jax.ShapeDtypeStruct((2, tok, width), jnp.bfloat16)
    return pl.pallas_call(
        kernel,
        in_specs=[in_vmem] * (2 + len(extra)),
        out_specs=in_vmem,
        out_shape=out_shape,
        name="encode_next",
        **params(2 * tok * cols * width, 2 * cols * width, 8),
    )(piece, weights, *extra)


def decode(member, features, weights, groups, rows, cols, dec_weight=None, offset=None):
    _, tok, width = features.shape
    count = weights.shape[1] // cols // 2
    ahead = dec_weight is not None

    def kernel(member_ref, feat_ref, weight_ref, *refs):
        if ahead:
            copies = in_parts(refs[0].at[offset], refs[-2], refs[-1], 0)
            for copy in copies:
                copy.start()
            out_refs = refs[1:-2]
        else:
            out_refs = refs
        left = feat_ref[0]
        even = member_ref[0] % 2 == 0
        for pair in range(count):
            piece = pair ^ (member_ref[0] // 2)
            for start in range(0, cols, tile):
                low, high = (
                    dot(left, weight_ref[:, base + start : base + start + tile], (1, 0)).astype(
                        jnp.bfloat16
                    )
                    for base in (2 * pair * cols, (2 * pair + 1) * cols)
                )
                sides = (jnp.where(even, high, low), jnp.where(even, low, high))
                for side, product in enumerate(sides):
                    for number, group in enumerate(groups):
                        for place, block in enumerate(group):
                            out_refs[side * len(groups) + number][
                                piece, place, :, start : start + tile
                            ] = product[block * rows : (block + 1) * rows]
        if ahead:
            for copy in copies:
                copy.wait()

    out_shape = [
        jax.ShapeDtypeStruct((count, len(group), rows, cols), jnp.bfloat16) for group in groups
    ] * 2
    if ahead:
        out_shape.append(jax.ShapeDtypeStruct(weights.shape, jnp.bfloat16))
    result = pl.pallas_call(
        kernel,
        in_specs=[in_smem] + [in_vmem] * 2 + ([in_hbm] if ahead else []),
        out_specs=[in_vmem] * len(out_shape),
        out_shape=out_shape,
        scratch_shapes=[pltpu.SemaphoreType.DMA((4,))] if ahead else [],
        name="decode",
        **params(4 * count * tok * cols * width, 4 * count * cols * width, 4),
    )(member, features, weights, *([dec_weight] if ahead else []))
    return result[: len(groups)], result[len(groups) : 2 * len(groups)], result[-1]


def turned(value):
    count, tok, width = value.shape

    def kernel(in_ref, out_ref):
        for piece in range(count):
            for start in range(0, width, tile):
                out_ref[piece, start : start + tile, :] = in_ref[
                    piece, :, start : start + tile
                ].T

    return pl.pallas_call(
        kernel,
        in_specs=[in_vmem],
        out_specs=in_vmem,
        out_shape=jax.ShapeDtypeStruct((count, width, tok), value.dtype),
        name="turned",
        **params(0, 4 * count * tok * width, 4),
    )(value)


def tree_sum(values):
    while len(values) > 1:
        values = [values[i] + values[i + 1] for i in range(0, len(values), 2)]
    return values[0]


def backward_pair(info, offset, own, other, turned_features, dec_weight, feature_grad, dec_grad):
    layers, width, depth = dec_weight.shape
    tok = turned_features.shape[1]
    cols = own[0].shape[2]
    first = feature_grad is None
    extra = [] if first else [feature_grad, dec_grad]
    inputs = [*own, *other]

    def kernel(info_ref, *refs):
        grad_refs = refs[: len(inputs)]
        feat_ref, weight_ref = refs[len(inputs) : len(inputs) + 2]
        out_ref, dec_ref, square_ref, held, weights, sems = refs[-6:]
        columns = span(info_ref[1], 2 * cols)
        starts = range(0, width, tile)
        fetches = in_parts(weight_ref.at[offset, :, columns], weights, sems, len(starts))
        for fetch in fetches:
            fetch.start()
        copies = [
            pltpu.make_async_copy(
                held.at[slice(start, start + tile)],
                dec_ref.at[offset, slice(start, start + tile), columns],
                sems.at[place],
            )
            for place, start in enumerate(starts)
        ]
        sides, sums = [], []
        for side in (grad_refs[: len(own)], grad_refs[len(own) :]):
            blocks = [ref[i] for ref in side for i in range(ref.shape[0])]
            totals = []
            for block in blocks:
                total = jnp.zeros((8, 128), jnp.float32)
                for row in range(0, block.shape[0], 8):
                    for col in range(0, cols, 128):
                        part = block[row : row + 8, col : col + 128].astype(jnp.float32)
                        total += part * part
                totals.append(total)
            sums.append(tree_sum(totals))
            sides.append(jnp.concatenate(blocks, 0))
        square_ref[...] = tree_sum(sums)

        def products():
            second = info_ref[0] > 0
            grad = jnp.concatenate(
                [jnp.where(second, sides[1], sides[0]), jnp.where(second, sides[0], sides[1])], 1
            )
            for copy, start in zip(copies, starts):
                here = slice(start, start + tile)
                held[here] = dot(feat_ref[here], grad, (1, 0)).astype(jnp.bfloat16)
                copy.start()
            for fetch in fetches:
                fetch.wait()
            for start in starts:
                here = slice(start, start + tile)
                product = dot(grad, weights[here], (1, 1))
                if not first:
                    product += refs[len(inputs) + 2][:, here]
                out_ref[:, here] = product

        def nothing():
            held[...] = jnp.zeros_like(held)
            for copy in copies:
                copy.start()
            out_ref[...] = refs[len(inputs) + 2][...]
            for fetch in fetches:
                fetch.wait()

        if offset == 0:
            products()
        else:
            pl.when(info_ref[2] > 0)(products)
            pl.when(info_ref[2] == 0)(nothing)
        for copy in copies:
            copy.wait()

    return pl.pallas_call(
        kernel,
        in_specs=[in_smem]
        + [in_vmem] * (len(inputs) + 1)
        + [in_hbm]
        + ([] if first else [in_vmem, in_hbm]),
        out_specs=[in_vmem, in_hbm, in_vmem],
        out_shape=[
            jax.ShapeDtypeStruct((tok, width), jnp.float32),
            jax.ShapeDtypeStruct((layers, width, depth), jnp.bfloat16),
            jax.ShapeDtypeStruct((8, 128), jnp.float32),
        ],
        scratch_shapes=[
            pltpu.VMEM((width, 2 * cols), jnp.bfloat16),
            pltpu.VMEM((width, 2 * cols), jnp.bfloat16),
            pltpu.SemaphoreType.DMA((width // tile + 4,)),
        ],
        input_output_aliases={} if first else {len(inputs) + 3: 0, len(inputs) + 4: 1},
        name="backward_pair",
        **params(tok * cols, tok * cols, 10),
    )(info, *inputs, turned_features, dec_weight, *extra)


def encoder_grad(indices, turned_tokens, features, feature_grad, squares, scale):
    count, cols, tok = turned_tokens[0].shape
    width = features.shape[2]
    pieces = len(turned_tokens) * count

    def kernel(index_ref, *refs):
        token_refs = refs[: len(turned_tokens)]
        mask_ref, grad_ref = refs[len(turned_tokens) : len(turned_tokens) + 2]
        square_refs = refs[len(turned_tokens) + 2 : -6]
        enc_ref, bias_ref, mean_ref, preact, held, sems = refs[-6:]
        mean_ref[...] = scale * jnp.sum(
            tree_sum([ref[...] for ref in square_refs]), (0, 1), keepdims=True
        )
        for start in range(0, width, tile):
            here = slice(start, start + tile)
            kept = jnp.where(mask_ref[1, :, here] > 0.0, grad_ref[:, here], 0.0).astype(jnp.bfloat16)
            preact[:, here] = kept
            bias_ref[:, here] = jnp.sum(kept.astype(jnp.float32), 0, keepdims=True)
        copies = []
        for piece in range(pieces):
            held[piece] = dot(
                token_refs[piece // count][piece % count], preact[...], (1, 0)
            ).astype(jnp.bfloat16)
            copy = pltpu.make_async_copy(
                held.at[piece], enc_ref.at[span(index_ref[piece], cols)], sems.at[piece]
            )
            copy.start()
            copies.append(copy)
        for copy in copies:
            copy.wait()

    return pl.pallas_call(
        kernel,
        in_specs=[in_smem] + [in_vmem] * (len(turned_tokens) + 2 + len(squares)),
        out_specs=[in_hbm, in_vmem, in_vmem],
        out_shape=[
            jax.ShapeDtypeStruct((pieces * cols, width), jnp.bfloat16),
            jax.ShapeDtypeStruct((1, width), jnp.float32),
            jax.ShapeDtypeStruct((1, 1), jnp.float32),
        ],
        scratch_shapes=[
            pltpu.VMEM((tok, width), jnp.bfloat16),
            pltpu.VMEM((pieces, cols, width), jnp.bfloat16),
            pltpu.SemaphoreType.DMA((pieces,)),
        ],
        name="encoder_grad",
        **params(
            2 * pieces * tok * cols * width, 2 * pieces * cols * (tok + width) + 6 * tok * width, 10
        ),
    )(indices, *turned_tokens, features, feature_grad, *squares)


def add_pair(left, right):
    return (left.astype(jnp.float32) + right.astype(jnp.float32)).astype(jnp.bfloat16)


def on_device(tokens_in, targets, enc_weight, enc_bias, dec_weight):
    layers, width, depth = dec_weight.shape
    feat_count = lax.axis_size("feat")
    sub_count = lax.axis_size("layer") // layers
    member = lax.axis_index("layer") % sub_count
    rows, cols = tokens_in.shape
    tok = feat_count * rows
    bit_count = sub_count.bit_length() - 1
    groups = [list(range(feat_count // 2))]
    groups += [[s] for s in range(feat_count // 2, feat_count)]

    enc_weight = pltpu.with_memory_space_constraint(enc_weight, pltpu.HBM)
    dec_weight = pltpu.with_memory_space_constraint(dec_weight, pltpu.HBM)

    held = {0: all_over_feat(tokens_in)}
    for bit_level in range(bit_count - 1, 0, -1):
        for rel in list(held):
            held[rel ^ 2**bit_level] = [None] * feat_count
    for s in range(feat_count):
        known = [0]
        for bit_level in range(bit_count - 1, 0, -1):
            for rel in known:
                held[rel ^ 2**bit_level][s] = over_members(held[rel][s], bit_level)
            known += [rel ^ 2**bit_level for rel in known]
    order = [rel for pair in sorted(held) for rel in (pair, pair ^ 1)]
    early = [held[rel][s] for rel in order[2::2] for s in range(2)]
    tokens = {0: after(jnp.stack(held[0], 0), *early)}
    tokens[1] = over_members(tokens[0], 0)
    partial, late_weights, weights = encode_first(
        jnp.stack([member ^ rel for rel in order]),
        [tokens[0], tokens[1]],
        enc_weight,
        dec_weight,
        layers - 1,
        len(order) - 2,
    )
    for rel in order[2::2]:
        tokens[rel] = jnp.stack([after(block, partial) for block in held[rel]], 0)
        tokens[rel ^ 1] = over_members(tokens[rel], 0)
    for place, rel in enumerate(order[2:-1]):
        partial = encode_next(tokens[rel], late_weights, place, partial, None)
    features = encode_next(
        tokens[order[-1]], late_weights, len(order) - 3, partial, enc_bias[None]
    )

    current, source = {}, features
    for k in reversed(range(layers)):
        ahead = (dec_weight, k - 1) if k > 0 else ()
        sent, kept, weights = decode(
            member.reshape(1), source, weights, groups, rows, cols, *ahead
        )
        for place in reversed(range(len(groups))):
            current[place, k] = add_pair(kept[place], over_members(sent[place], 0))
        source = after(features, current[len(groups) - 1, k])
    turns = sorted(current, reverse=True)
    joined = {}
    for bit_level in range(1, bit_count):
        halves = {}
        for turn, value in current.items():
            split = value.reshape((value.shape[0] // 2, 2) + value.shape[1:])
            halves[turn] = (split[:, 0], split[:, 1])
        if bit_level == bit_count - 1:
            for k in range(1, layers):
                joined[k], sent = halves.pop((0, k))
                sent = to_layer(after(sent, halves[len(groups) - 1, 0][1]), k, sub_count)
                halves[0, 0] = (halves[0, 0][0], add_pair(halves[0, 0][1], sent))
        turns = [turn for turn in turns if turn in halves]
        received, operands = [], []
        for turn in turns:
            operand = halves[turn][1]
            if len(received) > 1:
                operand = after(operand, received[-2], operands[-1])
            operands.append(operand)
            received.append(over_members(operand, bit_level))
        for place, turn in enumerate(turns):
            arrived = after(received[place], *operands[place + 1 :][:1])
            if bit_level < bit_count - 1:
                current[turn] = add_pair(halves[turn][0], arrived)
            else:
                current[turn] = (halves[turn][0], arrived)
    blocks, operands = [None] * feat_count, []
    for place in reversed(range(len(groups))):
        total = sum(part.astype(jnp.float32) for part in current[place, 0])
        for k in range(1, layers):
            if place > 0:
                moved = to_layer(add_pair(*current[place, k]), k, sub_count)
            else:
                moved = to_layer(after(joined[k], *operands), k, sub_count)
            total = total + moved.astype(jnp.float32)
        for spot, block in enumerate(groups[place]):
            if block == 0:
                rebuilt = total[0, spot]
            else:
                operands.append(total[0, spot].astype(jnp.bfloat16))
                blocks[block] = over_feat(operands[-1], block)
    for block in reversed(blocks[1:]):
        rebuilt = rebuilt + block.astype(jnp.float32)
    turned_features = turned(source[:1])[0]
    turned_tokens = [
        turned(after(tokens[rel], turned_features).reshape(1, tok, cols)) for rel in order
    ]
    recon_error = rebuilt - after(targets, turned_features, *turned_tokens).astype(jnp.float32)
    scaled = (loss_scale / tok * recon_error).astype(jnp.bfloat16)

    layer = lax.axis_index("layer") // sub_count
    there = [(layer + k < layers).astype(jnp.int32) for k in range(layers)]
    blocks = all_over_feat(scaled)
    stages = [[0]]
    for level in range(bit_count - 1, 0, -1):
        known = [rel for stage in stages for rel in stage]
        stages.append([rel ^ 2**level for rel in known])
    spans = [[s] for s in range(min(2, feat_count))]
    spans += [list(range(2, feat_count))] if feat_count > 2 else []
    groups_of = {(0, k): [None] * len(spans) for k in range(layers)}
    early, last = [], len(spans) - 1
    for place, group in enumerate(spans):
        stacked = jnp.stack([blocks[s] for s in group], 0)
        groups_of[0, 0][place] = stacked
        for k in range(1, layers):
            groups_of[0, k][place] = from_layer(stacked, k, sub_count)
        known = [0]
        for level in range(bit_count - 1, 0, -1):
            for rel in known:
                other = rel ^ 2**level
                for k in range(layers):
                    if k == 0 or place < last:
                        part = over_members(groups_of[rel, k][place], level)
                    else:
                        part = from_layer(groups_of[other, 0][place], k, sub_count)
                    groups_of.setdefault((other, k), [None] * len(spans))[place] = part
            known += [rel ^ 2**level for rel in known]
        if place == last - 1:
            early = [part for parts in groups_of.values() for part in parts if part is not None]
            early.pop()

    feature_grad, dec_grad, squares = None, None, {}
    for number, stage in enumerate(stages):
        for k in range(layers):
            for rel in stage:
                parts = groups_of[rel, k]
                if feature_grad is None:
                    parts = [after(parts[0], *early)] + parts[1:]
                else:
                    parts = [after(part, feature_grad) for part in parts]
                if k == 0 and number > 0:
                    feature_grad = after(feature_grad, groups_of[rel, layers - 1][-1])
                elif k > 0 and number + 1 < len(stages):
                    coming = [groups_of[other, k - 1][-1] for other in stages[number + 1]]
                    feature_grad = after(feature_grad, *coming)
                feature_grad, dec_grad, squares[k, rel] = backward_pair(
                    jnp.stack([member % 2, (member ^ rel) // 2, there[k]]),
                    k,
                    parts,
                    [over_members(part, 0) for part in parts],
                    turned_features,
                    dec_weight,
                    feature_grad,
                    dec_grad,
                )
    scale = (tok / loss_scale) ** 2 / (layers * tok * depth)
    enc_grad, bias_grad, mean_square = encoder_grad(
        jnp.stack([member ^ rel for rel in order]),
        turned_tokens,
        features,
        feature_grad,
        [squares[key] for key in sorted(squares)],
        scale,
    )
    return (recon_error, mean_square[0, 0], enc_grad, bias_grad[0], dec_grad)


def solution(mesh):
    placed = (
        P("feat", "layer"),
        P("feat", "layer"),
        P(None, ("layer", "feat")),
        P(("layer", "feat")),
        P(None, ("layer", "feat"), None),
    )
    return jax.shard_map(
        on_device,
        mesh=mesh,
        in_specs=placed,
        out_specs=(
            P("feat", "layer"),
            P(),
            P(None, ("layer", "feat")),
            P(("layer", "feat")),
            P(None, ("layer", "feat"), None),
        ),
        check_vma=False,
    )
```

```python
import jax
import jax.numpy as jnp
from jax import lax
from jax.experimental import pallas as pl
from jax.experimental.pallas import tpu as pltpu
from jax.sharding import PartitionSpec as P

loss_scale = 64.0
tile = 256
in_vmem = pl.BlockSpec(memory_space=pltpu.VMEM)
in_smem = pl.BlockSpec(memory_space=pltpu.SMEM)
in_hbm = pl.BlockSpec(memory_space=pltpu.HBM)


def over_feat(value, mask):
    pairs = [(source, source ^ mask) for source in range(lax.axis_size("feat"))]
    return lax.ppermute(value, "feat", pairs)


def over_members(value, bit_level):
    mask = 2**bit_level
    pairs = [(source, source ^ mask) for source in range(lax.axis_size("layer"))]
    return lax.ppermute(value, "layer", pairs)


def to_layer(value, offset, sub_count, real):
    count = lax.axis_size("layer")
    pairs = [(p, (p + offset * sub_count) % count) for p in range(count)]
    moved = lax.ppermute(value, "layer", pairs)
    return jnp.where(real[offset], moved, jnp.zeros_like(moved))


def from_layer(value, offset, sub_count):
    count = lax.axis_size("layer")
    pairs = [(p, (p - offset * sub_count) % count) for p in range(count)]
    return lax.ppermute(value, "layer", pairs)


def after(value, *others):
    return lax.optimization_barrier((value, *others))[0]


def all_over_feat(value):
    blocks = [value, over_feat(value, 1)]
    for s in range(2, lax.axis_size("feat")):
        blocks.append(over_feat(value, s))
    return blocks


def params(flops, bytes_accessed, scratch_mib):
    return dict(
        compiler_params=pltpu.CompilerParams(vmem_limit_bytes=scratch_mib * 1024 * 1024),
        cost_estimate=pl.CostEstimate(
            flops=flops, bytes_accessed=bytes_accessed, transcendentals=0
        ),
    )


def dot(left, right, contract):
    return lax.dot_general(
        left, right, ((contract[:1], contract[1:]), ((), ())), preferred_element_type=jnp.float32
    )


def span(index, size):
    return pl.ds(pl.multiple_of(index * size, size), size)


def fetch(*arrays):
    parts = [(number, start) for number, array in enumerate(arrays) for start in range(4)]

    def kernel(*refs):
        copies = []
        for place, (number, start) in enumerate(parts):
            source, target = refs[number], refs[len(arrays) + number]
            size = source.shape[-2] // 4
            here = (slice(None),) * (len(source.shape) - 2) + (pl.ds(start * size, size),)
            copies.append(
                pltpu.make_async_copy(source.at[here], target.at[here], refs[-1].at[place])
            )
        for copy in copies:
            copy.start()
        for copy in copies:
            copy.wait()

    total = sum(2 * array.size for array in arrays)
    return pl.pallas_call(
        kernel,
        in_specs=[in_hbm] * len(arrays),
        out_specs=[in_vmem] * len(arrays),
        out_shape=[jax.ShapeDtypeStruct(array.shape, array.dtype) for array in arrays],
        scratch_shapes=[pltpu.SemaphoreType.DMA((len(parts),))],
        name="fetch",
        **params(0, total, 14),
    )(*arrays)


def encode(info, rels, pieces, weights, partial, bias):
    feat_count, rows, cols = pieces[0].shape
    tok = feat_count * rows
    width = weights.shape[1]
    extra = [value for value in (partial, bias) if value is not None]

    def kernel(info_ref, *refs):
        piece_refs, weight_ref = refs[: len(pieces)], refs[len(pieces)]
        extra_refs, out_ref = refs[len(pieces) + 1 : -1], refs[-1]
        left = jnp.concatenate([ref[...].reshape(tok, cols) for ref in piece_refs], 1)
        for start in range(0, width, tile):
            here = slice(start, start + tile)
            right = jnp.concatenate(
                [weight_ref[span(info_ref[0] ^ rel, cols), here] for rel in rels], 0
            )
            total = dot(left, right, (1, 0))
            if partial is not None:
                total += extra_refs[0][:, here]
            if bias is None:
                out_ref[:, here] = total
            else:
                pre_act = total + extra_refs[-1][:, here]
                out_ref[0, :, here] = jnp.maximum(pre_act, 0.0).astype(jnp.bfloat16)
                out_ref[1, :, here] = jnp.where(pre_act > 0.0, 1.0, 0.0).astype(jnp.bfloat16)

    if bias is None:
        out_shape = jax.ShapeDtypeStruct((tok, width), jnp.float32)
    else:
        out_shape = jax.ShapeDtypeStruct((2, tok, width), jnp.bfloat16)
    return pl.pallas_call(
        kernel,
        in_specs=[in_smem] + [in_vmem] * (len(pieces) + 1 + len(extra)),
        out_specs=in_vmem,
        out_shape=out_shape,
        name="encode",
        **params(
            2 * len(pieces) * tok * cols * width, 2 * len(pieces) * cols * (tok + width), 4
        ),
    )(info, *pieces, weights, *extra)


def decode(info, features, weights, offset, groups, rows, cols):
    _, tok, width = features.shape
    count = weights.shape[2] // cols // 2

    def kernel(info_ref, feat_ref, weight_ref, *out_refs):
        left = feat_ref[0]
        even = info_ref[0] % 2 == 0
        for pair in range(count):
            piece = pair ^ (info_ref[0] // 2)
            for start in range(0, cols, tile):
                low, high = (
                    dot(left, weight_ref[offset, :, base + start : base + start + tile], (1, 0)).astype(
                        jnp.bfloat16
                    )
                    for base in (2 * pair * cols, (2 * pair + 1) * cols)
                )
                sides = (jnp.where(even, high, low), jnp.where(even, low, high))
                for side, product in enumerate(sides):
                    for number, group in enumerate(groups):
                        for place, block in enumerate(group):
                            out_refs[side * len(groups) + number][
                                piece, place, :, start : start + tile
                            ] = product[block * rows : (block + 1) * rows]
    out_shape = [
        jax.ShapeDtypeStruct((count, len(group), rows, cols), jnp.bfloat16) for group in groups
    ] * 2
    result = pl.pallas_call(
        kernel,
        in_specs=[in_smem, in_vmem, in_vmem],
        out_specs=[in_vmem] * len(out_shape),
        out_shape=out_shape,
        name="decode",
        **params(4 * count * tok * cols * width, 4 * count * cols * width, 4),
    )(info, features, weights)
    return result[: len(groups)], result[len(groups) :]


def turned(value, count):
    _, tok, width = value.shape

    def kernel(in_ref, out_ref):
        for piece in range(count):
            for start in range(0, width, tile):
                out_ref[piece, start : start + tile, :] = in_ref[
                    piece, :, start : start + tile
                ].T

    return pl.pallas_call(
        kernel,
        in_specs=[in_vmem],
        out_specs=in_vmem,
        out_shape=jax.ShapeDtypeStruct((count, width, tok), value.dtype),
        name="turned",
        **params(0, 4 * count * tok * width, 4),
    )(value)


def tree_sum(values):
    while len(values) > 1:
        values = [values[i] + values[i + 1] for i in range(0, len(values), 2)]
    return values[0]


def backward_pair(info, rel, offset, own, other, turned_features, dec_weight, feature_grad, dec_grad):
    layers, width, depth = dec_weight.shape
    tok = turned_features.shape[1]
    cols = own[0].shape[2]
    first = feature_grad is None
    extra = [] if first else [feature_grad, dec_grad]
    inputs = [*own, *other]

    def kernel(info_ref, *refs):
        grad_refs = refs[: len(inputs)]
        feat_ref, weight_ref = refs[len(inputs) : len(inputs) + 2]
        out_ref, dec_ref, square_ref, held, sems = refs[-5:]
        columns = span((info_ref[0] ^ rel) // 2, 2 * cols)
        starts = range(0, width, tile)
        copies = [
            pltpu.make_async_copy(
                held.at[slice(start, start + tile)],
                dec_ref.at[offset, slice(start, start + tile), columns],
                sems.at[place],
            )
            for place, start in enumerate(starts)
        ]
        sides, sums = [], []
        for side in (grad_refs[: len(own)], grad_refs[len(own) :]):
            blocks = [ref[i] for ref in side for i in range(ref.shape[0])]
            totals = []
            for block in blocks:
                total = jnp.zeros((8, 128), jnp.float32)
                for row in range(0, block.shape[0], 8):
                    for col in range(0, cols, 128):
                        part = block[row : row + 8, col : col + 128].astype(jnp.float32)
                        total += part * part
                totals.append(total)
            sums.append(tree_sum(totals))
            sides.append(jnp.concatenate(blocks, 0))
        square_ref[...] = tree_sum(sums)

        def products():
            second = info_ref[0] % 2 > 0
            grad = jnp.concatenate(
                [jnp.where(second, sides[1], sides[0]), jnp.where(second, sides[0], sides[1])], 1
            )
            for copy, start in zip(copies, starts):
                here = slice(start, start + tile)
                held[here] = dot(feat_ref[here], grad, (1, 0)).astype(jnp.bfloat16)
                copy.start()
            for start in starts:
                here = slice(start, start + tile)
                product = dot(grad, weight_ref[offset, here, columns], (1, 1))
                if not first:
                    product += refs[len(inputs) + 2][:, here]
                out_ref[:, here] = product

        def nothing():
            held[...] = jnp.zeros_like(held)
            for copy in copies:
                copy.start()
            out_ref[...] = refs[len(inputs) + 2][...]

        if offset == 0:
            products()
        else:
            pl.when(info_ref[1] >= offset)(products)
            pl.when(info_ref[1] < offset)(nothing)
        for copy in copies:
            copy.wait()

    return pl.pallas_call(
        kernel,
        in_specs=[in_smem]
        + [in_vmem] * (len(inputs) + 2)
        + ([] if first else [in_vmem, in_hbm]),
        out_specs=[in_vmem, in_hbm, in_vmem],
        out_shape=[
            jax.ShapeDtypeStruct((tok, width), jnp.float32),
            jax.ShapeDtypeStruct((layers, width, depth), jnp.bfloat16),
            jax.ShapeDtypeStruct((8, 128), jnp.float32),
        ],
        scratch_shapes=[
            pltpu.VMEM((width, 2 * cols), jnp.bfloat16),
            pltpu.SemaphoreType.DMA((width // tile,)),
        ],
        input_output_aliases={} if first else {len(inputs) + 3: 0, len(inputs) + 4: 1},
        name="backward_pair",
        **params(tok * cols, tok * cols, 8),
    )(info, *inputs, turned_features, dec_weight, *extra)


def encoder_grad(info, rels, turned_tokens, features, feature_grad, squares, scale):
    count, cols, tok = turned_tokens[0].shape
    width = features.shape[2]
    pieces = len(turned_tokens) * count

    def kernel(info_ref, *refs):
        token_refs = refs[: len(turned_tokens)]
        mask_ref, grad_ref = refs[len(turned_tokens) : len(turned_tokens) + 2]
        square_refs = refs[len(turned_tokens) + 2 : -6]
        enc_ref, bias_ref, mean_ref, preact, held, sems = refs[-6:]
        mean_ref[...] = scale * jnp.sum(
            tree_sum([ref[...] for ref in square_refs]), (0, 1), keepdims=True
        )
        for start in range(0, width, tile):
            here = slice(start, start + tile)
            kept = jnp.where(mask_ref[1, :, here] > 0.0, grad_ref[:, here], 0.0).astype(jnp.bfloat16)
            preact[:, here] = kept
            bias_ref[:, here] = jnp.sum(kept.astype(jnp.float32), 0, keepdims=True)
        copies = []
        for piece in range(pieces):
            held[piece] = dot(
                token_refs[piece // count][piece % count], preact[...], (1, 0)
            ).astype(jnp.bfloat16)
            copy = pltpu.make_async_copy(
                held.at[piece], enc_ref.at[span(info_ref[0] ^ rels[piece], cols)], sems.at[piece]
            )
            copy.start()
            copies.append(copy)
        for copy in copies:
            copy.wait()

    return pl.pallas_call(
        kernel,
        in_specs=[in_smem] + [in_vmem] * (len(turned_tokens) + 2 + len(squares)),
        out_specs=[in_hbm, in_vmem, in_vmem],
        out_shape=[
            jax.ShapeDtypeStruct((pieces * cols, width), jnp.bfloat16),
            jax.ShapeDtypeStruct((1, width), jnp.float32),
            jax.ShapeDtypeStruct((1, 1), jnp.float32),
        ],
        scratch_shapes=[
            pltpu.VMEM((tok, width), jnp.bfloat16),
            pltpu.VMEM((pieces, cols, width), jnp.bfloat16),
            pltpu.SemaphoreType.DMA((pieces,)),
        ],
        name="encoder_grad",
        **params(
            2 * pieces * tok * cols * width, 2 * pieces * cols * (tok + width) + 6 * tok * width, 10
        ),
    )(info, *turned_tokens, features, feature_grad, *squares)


def add_pair(left, right):
    return (left.astype(jnp.float32) + right.astype(jnp.float32)).astype(jnp.bfloat16)


def on_device(tokens_in, targets, enc_weight, enc_bias, dec_weight):
    layers, width, depth = dec_weight.shape
    feat_count = lax.axis_size("feat")
    sub_count = lax.axis_size("layer") // layers
    position = lax.axis_index("layer")
    layer = position // sub_count
    rows, cols = tokens_in.shape
    tok = feat_count * rows
    bit_count = sub_count.bit_length() - 1
    groups = [list(range(feat_count // 2))]
    groups += [[s] for s in range(feat_count // 2, feat_count)]

    info = jnp.stack([position % sub_count, layers - 1 - layer]).astype(jnp.int32)
    real = [layer >= k for k in range(layers)]
    tokens_in, info, *real = lax.optimization_barrier((tokens_in, info, *real))
    enc_weight = pltpu.with_memory_space_constraint(enc_weight, pltpu.HBM)
    dec_weight = pltpu.with_memory_space_constraint(dec_weight, pltpu.HBM)

    held = {0: all_over_feat(tokens_in)}
    for bit_level in range(bit_count - 1, 0, -1):
        for rel in list(held):
            held[rel ^ 2**bit_level] = [None] * feat_count
    for s in range(feat_count):
        known = [0]
        for bit_level in range(bit_count - 1, 0, -1):
            for rel in known:
                held[rel ^ 2**bit_level][s] = over_members(held[rel][s], bit_level)
            known += [rel ^ 2**bit_level for rel in known]
    order = [rel for pair in sorted(held) for rel in (pair, pair ^ 1)]
    enc_held, dec_held = fetch(enc_weight, after(dec_weight, held[0][1]))
    early = [held[rel][s] for rel in order[2::2] for s in range(2)]
    tokens = {0: after(jnp.stack(held[0], 0), enc_held, *early)}
    tokens[1] = over_members(tokens[0], 0)
    partial = encode(info, [0, 1], [tokens[0], tokens[1]], enc_held, None, None)
    for rel in order[2::2]:
        tokens[rel] = jnp.stack([after(block, partial) for block in held[rel]], 0)
        tokens[rel ^ 1] = over_members(tokens[rel], 0)
    for rel in order[2:-1]:
        partial = encode(info, [rel], [tokens[rel]], enc_held, partial, None)
    features = encode(info, order[-1:], [tokens[order[-1]]], enc_held, partial, enc_bias[None])

    current, source = {}, features
    for k in reversed(range(layers)):
        sent, kept = decode(info, source, dec_held, k, groups, rows, cols)
        for place in reversed(range(len(groups))):
            current[place, k] = add_pair(kept[place], over_members(sent[place], 0))
        source = after(features, current[len(groups) - 1, k])
    turns = sorted(current, reverse=True)
    joined = {}
    for bit_level in range(1, bit_count):
        halves = {}
        for turn, value in current.items():
            split = value.reshape((value.shape[0] // 2, 2) + value.shape[1:])
            halves[turn] = (split[:, 0], split[:, 1])
        if bit_level == bit_count - 1:
            for k in range(1, layers):
                joined[k], sent = halves.pop((0, k))
                sent = to_layer(after(sent, halves[len(groups) - 1, 0][1]), k, sub_count, real)
                halves[0, 0] = (halves[0, 0][0], add_pair(halves[0, 0][1], sent))
        turns = [turn for turn in turns if turn in halves]
        received, operands = [], []
        for turn in turns:
            operand = halves[turn][1]
            if len(received) > 1:
                operand = after(operand, received[-2], operands[-1])
            operands.append(operand)
            received.append(over_members(operand, bit_level))
        for place, turn in enumerate(turns):
            arrived = after(received[place], *operands[place + 1 :][:1])
            if bit_level < bit_count - 1:
                current[turn] = add_pair(halves[turn][0], arrived)
            else:
                current[turn] = (halves[turn][0], arrived)
    blocks, operands = [None] * feat_count, []
    for place in reversed(range(len(groups))):
        total = sum(part.astype(jnp.float32) for part in current[place, 0])
        for k in range(1, layers):
            if place > 0:
                moved = to_layer(add_pair(*current[place, k]), k, sub_count, real)
            else:
                moved = to_layer(after(joined[k], *operands), k, sub_count, real)
            total = total + moved.astype(jnp.float32)
        for spot, block in enumerate(groups[place]):
            if block == 0:
                rebuilt = total[0, spot]
            else:
                operands.append(total[0, spot].astype(jnp.bfloat16))
                blocks[block] = over_feat(operands[-1], block)
    for block in reversed(blocks[1:]):
        rebuilt = rebuilt + block.astype(jnp.float32)
    turned_features = turned(source, 1)[0]
    turned_tokens = [
        turned(after(tokens[rel], turned_features).reshape(1, tok, cols), 1) for rel in order
    ]
    recon_error = rebuilt - after(targets, turned_features, *turned_tokens).astype(jnp.float32)
    scaled = (loss_scale / tok * recon_error).astype(jnp.bfloat16)

    blocks = all_over_feat(scaled)
    stages = [[0]]
    for level in range(bit_count - 1, 0, -1):
        known = [rel for stage in stages for rel in stage]
        stages.append([rel ^ 2**level for rel in known])
    spans = [[s] for s in range(min(2, feat_count))]
    spans += [list(range(2, feat_count))] if feat_count > 2 else []
    groups_of = {(0, k): [None] * len(spans) for k in range(layers)}
    early, last = [], len(spans) - 1
    for place, group in enumerate(spans):
        stacked = jnp.stack([blocks[s] for s in group], 0)
        groups_of[0, 0][place] = stacked
        for k in range(1, layers):
            groups_of[0, k][place] = from_layer(stacked, k, sub_count)
        known = [0]
        for level in range(bit_count - 1, 0, -1):
            for rel in known:
                other = rel ^ 2**level
                for k in range(layers):
                    if k == 0 or place < last:
                        part = over_members(groups_of[rel, k][place], level)
                    else:
                        part = from_layer(groups_of[other, 0][place], k, sub_count)
                    groups_of.setdefault((other, k), [None] * len(spans))[place] = part
            known += [rel ^ 2**level for rel in known]
        if place == last - 1:
            early = [part for parts in groups_of.values() for part in parts if part is not None]
            early.pop()

    feature_grad, dec_grad, squares = None, None, {}
    for number, stage in enumerate(stages):
        for k in range(layers):
            for rel in stage:
                parts = groups_of[rel, k]
                if feature_grad is None:
                    parts = [after(parts[0], *early)] + parts[1:]
                else:
                    parts = [after(part, feature_grad) for part in parts]
                if k == 0 and number > 0:
                    feature_grad = after(feature_grad, groups_of[rel, layers - 1][-1])
                elif k > 0 and number + 1 < len(stages):
                    coming = [groups_of[other, k - 1][-1] for other in stages[number + 1]]
                    feature_grad = after(feature_grad, *coming)
                feature_grad, dec_grad, squares[k, rel] = backward_pair(
                    info,
                    rel,
                    k,
                    parts,
                    [over_members(part, 0) for part in parts],
                    turned_features,
                    dec_held,
                    feature_grad,
                    dec_grad,
                )
    scale = (tok / loss_scale) ** 2 / (layers * tok * depth)
    enc_grad, bias_grad, mean_square = encoder_grad(
        info,
        order,
        turned_tokens,
        features,
        feature_grad,
        [squares[key] for key in sorted(squares)],
        scale,
    )
    return (recon_error, mean_square[0, 0], enc_grad, bias_grad[0], dec_grad)


def solution(mesh):
    placed = (
        P("feat", "layer"),
        P("feat", "layer"),
        P(None, ("layer", "feat")),
        P(("layer", "feat")),
        P(None, ("layer", "feat"), None),
    )
    return jax.shard_map(
        on_device,
        mesh=mesh,
        in_specs=placed,
        out_specs=(
            P("feat", "layer"),
            P(),
            P(None, ("layer", "feat")),
            P(("layer", "feat")),
            P(None, ("layer", "feat"), None),
        ),
        check_vma=False,
    )
```

```python
import jax
import jax.numpy as jnp
from jax import lax
from jax.experimental import pallas as pl
from jax.experimental.pallas import tpu as pltpu
from jax.sharding import PartitionSpec as P

loss_scale = 64.0
tile = 256
in_vmem = pl.BlockSpec(memory_space=pltpu.VMEM)
in_smem = pl.BlockSpec(memory_space=pltpu.SMEM)
in_hbm = pl.BlockSpec(memory_space=pltpu.HBM)


def over_feat(value, mask):
    pairs = [(source, source ^ mask) for source in range(lax.axis_size("feat"))]
    return lax.ppermute(value, "feat", pairs)


def over_members(value, bit_level):
    mask = 2**bit_level
    pairs = [(source, source ^ mask) for source in range(lax.axis_size("layer"))]
    return lax.ppermute(value, "layer", pairs)


def to_layer(value, offset, sub_count, real):
    count = lax.axis_size("layer")
    pairs = [(p, (p + offset * sub_count) % count) for p in range(count)]
    moved = lax.ppermute(value, "layer", pairs)
    return jnp.where(real[offset], moved, jnp.zeros_like(moved))


def from_layer(value, offset, sub_count):
    count = lax.axis_size("layer")
    pairs = [(p, (p - offset * sub_count) % count) for p in range(count)]
    return lax.ppermute(value, "layer", pairs)


def after(value, *others):
    return lax.optimization_barrier((value, *others))[0]


def all_over_feat(value):
    count = lax.axis_size("feat")
    blocks = [value] + [None] * (count - 1)
    mask = count // 2
    while mask > 0:
        for s in range(0, count, 2 * mask):
            blocks[s ^ mask] = over_feat(blocks[s], mask)
        mask //= 2
    return blocks


def params(flops, bytes_accessed, scratch_mib):
    return dict(
        compiler_params=pltpu.CompilerParams(vmem_limit_bytes=scratch_mib * 1024 * 1024),
        cost_estimate=pl.CostEstimate(
            flops=flops, bytes_accessed=bytes_accessed, transcendentals=0
        ),
    )


def dot(left, right, contract):
    return lax.dot_general(
        left, right, ((contract[:1], contract[1:]), ((), ())), preferred_element_type=jnp.float32
    )


def span(index, size):
    return pl.ds(pl.multiple_of(index * size, size), size)


def fetch(*arrays):
    parts = [(number, start) for number, array in enumerate(arrays) for start in range(4)]

    def kernel(*refs):
        copies = []
        for place, (number, start) in enumerate(parts):
            source, target = refs[number], refs[len(arrays) + number]
            size = source.shape[-2] // 4
            here = (slice(None),) * (len(source.shape) - 2) + (pl.ds(start * size, size),)
            copies.append(
                pltpu.make_async_copy(source.at[here], target.at[here], refs[-1].at[place])
            )
        for copy in copies:
            copy.start()
        for copy in copies:
            copy.wait()

    total = sum(2 * array.size for array in arrays)
    return pl.pallas_call(
        kernel,
        in_specs=[in_hbm] * len(arrays),
        out_specs=[in_vmem] * len(arrays),
        out_shape=[jax.ShapeDtypeStruct(array.shape, array.dtype) for array in arrays],
        scratch_shapes=[pltpu.SemaphoreType.DMA((len(parts),))],
        name="fetch",
        **params(0, total, 14),
    )(*arrays)


def encode(info, rels, pieces, weights, partial, bias):
    feat_count, rows, cols = pieces[0].shape
    tok = feat_count * rows
    width = weights.shape[1]
    extra = [value for value in (partial, bias) if value is not None]

    def kernel(info_ref, *refs):
        piece_refs, weight_ref = refs[: len(pieces)], refs[len(pieces)]
        extra_refs, out_ref = refs[len(pieces) + 1 : -1], refs[-1]
        left = jnp.concatenate([ref[...].reshape(tok, cols) for ref in piece_refs], 1)
        for start in range(0, width, tile):
            here = slice(start, start + tile)
            right = jnp.concatenate(
                [weight_ref[span(info_ref[0] ^ rel, cols), here] for rel in rels], 0
            )
            total = dot(left, right, (1, 0))
            if partial is not None:
                total += extra_refs[0][:, here]
            if bias is None:
                out_ref[:, here] = total
            else:
                pre_act = total + extra_refs[-1][:, here]
                out_ref[0, :, here] = jnp.maximum(pre_act, 0.0).astype(jnp.bfloat16)
                out_ref[1, :, here] = jnp.where(pre_act > 0.0, 1.0, 0.0).astype(jnp.bfloat16)

    if bias is None:
        out_shape = jax.ShapeDtypeStruct((tok, width), jnp.float32)
    else:
        out_shape = jax.ShapeDtypeStruct((2, tok, width), jnp.bfloat16)
    return pl.pallas_call(
        kernel,
        in_specs=[in_smem] + [in_vmem] * (len(pieces) + 1 + len(extra)),
        out_specs=in_vmem,
        out_shape=out_shape,
        name="encode",
        **params(
            2 * len(pieces) * tok * cols * width, 2 * len(pieces) * cols * (tok + width), 4
        ),
    )(info, *pieces, weights, *extra)


def decode(info, features, weights, offset, groups, rows, cols):
    _, tok, width = features.shape
    count = weights.shape[2] // cols // 2

    def kernel(info_ref, feat_ref, weight_ref, *out_refs):
        left = feat_ref[0]
        even = info_ref[0] % 2 == 0
        for pair in range(count):
            piece = pair ^ (info_ref[0] // 2)
            for start in range(0, cols, tile):
                low, high = (
                    dot(left, weight_ref[offset, :, base + start : base + start + tile], (1, 0)).astype(
                        jnp.bfloat16
                    )
                    for base in (2 * pair * cols, (2 * pair + 1) * cols)
                )
                sides = (jnp.where(even, high, low), jnp.where(even, low, high))
                for side, product in enumerate(sides):
                    for number, group in enumerate(groups):
                        for place, block in enumerate(group):
                            out_refs[side * len(groups) + number][
                                piece, place, :, start : start + tile
                            ] = product[block * rows : (block + 1) * rows]
    out_shape = [
        jax.ShapeDtypeStruct((count, len(group), rows, cols), jnp.bfloat16) for group in groups
    ] * 2
    result = pl.pallas_call(
        kernel,
        in_specs=[in_smem, in_vmem, in_vmem],
        out_specs=[in_vmem] * len(out_shape),
        out_shape=out_shape,
        name="decode",
        **params(4 * count * tok * cols * width, 4 * count * cols * width, 4),
    )(info, features, weights)
    return result[: len(groups)], result[len(groups) :]


def turned(value, count):
    _, tok, width = value.shape

    def kernel(in_ref, out_ref):
        for piece in range(count):
            for start in range(0, width, tile):
                out_ref[piece, start : start + tile, :] = in_ref[
                    piece, :, start : start + tile
                ].T

    return pl.pallas_call(
        kernel,
        in_specs=[in_vmem],
        out_specs=in_vmem,
        out_shape=jax.ShapeDtypeStruct((count, width, tok), value.dtype),
        name="turned",
        **params(0, 4 * count * tok * width, 4),
    )(value)


def tree_sum(values):
    while len(values) > 1:
        values = [values[i] + values[i + 1] for i in range(0, len(values), 2)]
    return values[0]


def backward_pair(info, rel, offset, own, other, turned_features, dec_weight, feature_grad, dec_grad):
    layers, width, depth = dec_weight.shape
    tok = turned_features.shape[1]
    cols = own[0].shape[2]
    first = feature_grad is None
    extra = [] if first else [feature_grad, dec_grad]
    inputs = [*own, *other]

    def kernel(info_ref, *refs):
        grad_refs = refs[: len(inputs)]
        feat_ref, weight_ref = refs[len(inputs) : len(inputs) + 2]
        out_ref, dec_ref, square_ref, held, sems = refs[-5:]
        columns = span((info_ref[0] ^ rel) // 2, 2 * cols)
        starts = range(0, width, tile)
        copies = [
            pltpu.make_async_copy(
                held.at[slice(start, start + tile)],
                dec_ref.at[offset, slice(start, start + tile), columns],
                sems.at[place],
            )
            for place, start in enumerate(starts)
        ]
        sides, sums = [], []
        for side in (grad_refs[: len(own)], grad_refs[len(own) :]):
            blocks = [ref[i] for ref in side for i in range(ref.shape[0])]
            totals = []
            for block in blocks:
                total = jnp.zeros((8, 128), jnp.float32)
                for row in range(0, block.shape[0], 8):
                    for col in range(0, cols, 128):
                        part = block[row : row + 8, col : col + 128].astype(jnp.float32)
                        total += part * part
                totals.append(total)
            sums.append(tree_sum(totals))
            sides.append(jnp.concatenate(blocks, 0))
        square_ref[...] = tree_sum(sums)

        def products():
            second = info_ref[0] % 2 > 0
            grad = jnp.concatenate(
                [jnp.where(second, sides[1], sides[0]), jnp.where(second, sides[0], sides[1])], 1
            )
            for copy, start in zip(copies, starts):
                here = slice(start, start + tile)
                held[here] = dot(feat_ref[here], grad, (1, 0)).astype(jnp.bfloat16)
                copy.start()
            for start in starts:
                here = slice(start, start + tile)
                product = dot(grad, weight_ref[offset, here, columns], (1, 1))
                if not first:
                    product += refs[len(inputs) + 2][:, here]
                out_ref[:, here] = product

        def nothing():
            held[...] = jnp.zeros_like(held)
            for copy in copies:
                copy.start()
            out_ref[...] = refs[len(inputs) + 2][...]

        if offset == 0:
            products()
        else:
            pl.when(info_ref[1] >= offset)(products)
            pl.when(info_ref[1] < offset)(nothing)
        for copy in copies:
            copy.wait()

    return pl.pallas_call(
        kernel,
        in_specs=[in_smem]
        + [in_vmem] * (len(inputs) + 2)
        + ([] if first else [in_vmem, in_hbm]),
        out_specs=[in_vmem, in_hbm, in_vmem],
        out_shape=[
            jax.ShapeDtypeStruct((tok, width), jnp.float32),
            jax.ShapeDtypeStruct((layers, width, depth), jnp.bfloat16),
            jax.ShapeDtypeStruct((8, 128), jnp.float32),
        ],
        scratch_shapes=[
            pltpu.VMEM((width, 2 * cols), jnp.bfloat16),
            pltpu.SemaphoreType.DMA((width // tile,)),
        ],
        input_output_aliases={} if first else {len(inputs) + 3: 0, len(inputs) + 4: 1},
        name="backward_pair",
        **params(tok * cols, tok * cols, 8),
    )(info, *inputs, turned_features, dec_weight, *extra)


def encoder_grad(info, rels, turned_tokens, features, feature_grad, squares, scale):
    count, cols, tok = turned_tokens[0].shape
    width = features.shape[2]
    pieces = len(turned_tokens) * count

    def kernel(info_ref, *refs):
        token_refs = refs[: len(turned_tokens)]
        mask_ref, grad_ref = refs[len(turned_tokens) : len(turned_tokens) + 2]
        square_refs = refs[len(turned_tokens) + 2 : -6]
        enc_ref, bias_ref, mean_ref, preact, held, sems = refs[-6:]
        mean_ref[...] = scale * jnp.sum(
            tree_sum([ref[...] for ref in square_refs]), (0, 1), keepdims=True
        )
        for start in range(0, width, tile):
            here = slice(start, start + tile)
            kept = jnp.where(mask_ref[1, :, here] > 0.0, grad_ref[:, here], 0.0).astype(jnp.bfloat16)
            preact[:, here] = kept
            bias_ref[:, here] = jnp.sum(kept.astype(jnp.float32), 0, keepdims=True)
        copies = []
        for piece in range(pieces):
            held[piece] = dot(
                token_refs[piece // count][piece % count], preact[...], (1, 0)
            ).astype(jnp.bfloat16)
            copy = pltpu.make_async_copy(
                held.at[piece], enc_ref.at[span(info_ref[0] ^ rels[piece], cols)], sems.at[piece]
            )
            copy.start()
            copies.append(copy)
        for copy in copies:
            copy.wait()

    return pl.pallas_call(
        kernel,
        in_specs=[in_smem] + [in_vmem] * (len(turned_tokens) + 2 + len(squares)),
        out_specs=[in_hbm, in_vmem, in_vmem],
        out_shape=[
            jax.ShapeDtypeStruct((pieces * cols, width), jnp.bfloat16),
            jax.ShapeDtypeStruct((1, width), jnp.float32),
            jax.ShapeDtypeStruct((1, 1), jnp.float32),
        ],
        scratch_shapes=[
            pltpu.VMEM((tok, width), jnp.bfloat16),
            pltpu.VMEM((pieces, cols, width), jnp.bfloat16),
            pltpu.SemaphoreType.DMA((pieces,)),
        ],
        name="encoder_grad",
        **params(
            2 * pieces * tok * cols * width, 2 * pieces * cols * (tok + width) + 6 * tok * width, 10
        ),
    )(info, *turned_tokens, features, feature_grad, *squares)


def add_pair(left, right):
    return (left.astype(jnp.float32) + right.astype(jnp.float32)).astype(jnp.bfloat16)


def on_device(tokens_in, targets, enc_weight, enc_bias, dec_weight):
    layers, width, depth = dec_weight.shape
    feat_count = lax.axis_size("feat")
    sub_count = lax.axis_size("layer") // layers
    position = lax.axis_index("layer")
    layer = position // sub_count
    rows, cols = tokens_in.shape
    tok = feat_count * rows
    bit_count = sub_count.bit_length() - 1
    groups = [list(range(feat_count // 2))]
    groups += [[s] for s in range(feat_count // 2, feat_count)]

    info = jnp.stack([position % sub_count, layers - 1 - layer]).astype(jnp.int32)
    real = [layer >= k for k in range(layers)]
    tokens_in, info, *real = lax.optimization_barrier((tokens_in, info, *real))

    enc_weight = pltpu.with_memory_space_constraint(enc_weight, pltpu.HBM)
    dec_weight = pltpu.with_memory_space_constraint(dec_weight, pltpu.HBM)

    held = {0: all_over_feat(tokens_in)}
    for bit_level in range(bit_count - 1, 0, -1):
        for rel in list(held):
            held[rel ^ 2**bit_level] = [None] * feat_count
    for s in range(feat_count):
        known = [0]
        for bit_level in range(bit_count - 1, 0, -1):
            for rel in known:
                held[rel ^ 2**bit_level][s] = over_members(held[rel][s], bit_level)
            known += [rel ^ 2**bit_level for rel in known]
    order = [rel for pair in sorted(held) for rel in (pair, pair ^ 1)]
    (enc_held,) = fetch(after(enc_weight, held[0][1]))
    early = [held[rel][s] for rel in order[2::2] for s in range(feat_count - 1)]
    tokens = {0: after(jnp.stack(held[0], 0), enc_held, *early)}
    tokens[1] = over_members(tokens[0], 0)
    partial = encode(info, [0, 1], [tokens[0], tokens[1]], enc_held, None, None)
    (dec_held,) = fetch(after(dec_weight, partial))
    for rel in order[2::2]:
        tokens[rel] = jnp.stack([after(block, dec_held) for block in held[rel]], 0)
        tokens[rel ^ 1] = over_members(tokens[rel], 0)
    for rel in order[2:-1]:
        partial = encode(info, [rel], [tokens[rel]], enc_held, partial, None)
    features = encode(info, order[-1:], [tokens[order[-1]]], enc_held, partial, enc_bias[None])

    current, source = {}, features
    for k in reversed(range(layers)):
        sent, kept = decode(info, source, dec_held, k, groups, rows, cols)
        for place in reversed(range(len(groups))):
            current[place, k] = add_pair(kept[place], over_members(sent[place], 0))
        source = after(features, kept[-1])
    turns = sorted(current, reverse=True)
    joined = {}
    for bit_level in range(1, bit_count):
        halves = {}
        for turn, value in current.items():
            split = value.reshape((value.shape[0] // 2, 2) + value.shape[1:])
            halves[turn] = (split[:, 0], split[:, 1])
        if bit_level == bit_count - 1:
            for k in range(1, layers):
                joined[k], sent = halves.pop((0, k))
                sent = to_layer(after(sent, halves[len(groups) - 1, 0][1]), k, sub_count, real)
                halves[0, 0] = (halves[0, 0][0], add_pair(halves[0, 0][1], sent))
        turns = [turn for turn in turns if turn in halves]
        received, operands = [], []
        for turn in turns:
            operand = halves[turn][1]
            if len(received) > 1:
                operand = after(operand, received[-2], operands[-1])
            operands.append(operand)
            received.append(over_members(operand, bit_level))
        for place, turn in enumerate(turns):
            arrived = after(received[place], *operands[place + 1 :][:1])
            if bit_level < bit_count - 1:
                current[turn] = add_pair(halves[turn][0], arrived)
            else:
                current[turn] = (halves[turn][0], arrived)
    blocks, operands = [None] * feat_count, []
    for place in reversed(range(len(groups))):
        total = sum(part.astype(jnp.float32) for part in current[place, 0])
        for k in range(1, layers):
            if place > 0:
                moved = to_layer(add_pair(*current[place, k]), k, sub_count, real)
            else:
                moved = to_layer(after(joined[k], *operands), k, sub_count, real)
            total = total + moved.astype(jnp.float32)
        for spot, block in enumerate(groups[place]):
            blocks[block] = total[0, spot]
            if place > 0:
                operands.append(blocks[block].astype(jnp.bfloat16))
    mask = 1
    while mask < feat_count:
        for s in range(0, feat_count, 2 * mask):
            sent = blocks[s ^ mask].astype(jnp.bfloat16)
            blocks[s] = blocks[s] + over_feat(sent, mask).astype(jnp.float32)
        mask *= 2
    rebuilt = blocks[0]
    turned_features = turned(source, 1)[0]
    turned_tokens = [
        turned(after(tokens[rel], turned_features).reshape(1, tok, cols), 1) for rel in order
    ]
    recon_error = rebuilt - after(targets, turned_features, *turned_tokens).astype(jnp.float32)
    scaled = (loss_scale / tok * recon_error).astype(jnp.bfloat16)

    blocks = all_over_feat(scaled)
    stages = [[0]]
    for level in range(bit_count - 1, 0, -1):
        known = [rel for stage in stages for rel in stage]
        stages.append([rel ^ 2**level for rel in known])
    spans = [list(range(feat_count // 2)), list(range(feat_count // 2, feat_count))]
    groups_of = {(0, k): [None] * len(spans) for k in range(layers)}
    early, last = [], len(spans) - 1
    for place, group in enumerate(spans):
        stacked = jnp.stack([blocks[s] for s in group], 0)
        groups_of[0, 0][place] = stacked
        for k in range(1, layers):
            groups_of[0, k][place] = from_layer(stacked, k, sub_count)
        known = [0]
        for level in range(bit_count - 1, 0, -1):
            for rel in known:
                other = rel ^ 2**level
                for k in range(layers):
                    if k == 0 or place < last:
                        part = over_members(groups_of[rel, k][place], level)
                    else:
                        part = from_layer(groups_of[other, 0][place], k, sub_count)
                    groups_of.setdefault((other, k), [None] * len(spans))[place] = part
            known += [rel ^ 2**level for rel in known]
        if place == last - 1:
            early = [part for parts in groups_of.values() for part in parts if part is not None]
            early.pop()

    feature_grad, dec_grad, squares = None, None, {}
    other_rels = [rel for stage in stages[1:] for rel in stage]
    for k in range(layers):
        for rel in [rel for stage in stages for rel in stage]:
            parts = groups_of[rel, k]
            if feature_grad is None:
                parts = [after(parts[0], *early)] + parts[1:]
            else:
                parts = [after(part, feature_grad) for part in parts]
                if k == 0:
                    coming = [groups_of[0, later][-1] for later in range(1, layers)]
                else:
                    coming = [part for r in other_rels for part in groups_of[r, k]]
                feature_grad = after(feature_grad, *coming)
            feature_grad, dec_grad, squares[k, rel] = backward_pair(
                info,
                rel,
                k,
                parts,
                [over_members(part, 0) for part in parts],
                turned_features,
                dec_held,
                feature_grad,
                dec_grad,
            )
    scale = (tok / loss_scale) ** 2 / (layers * tok * depth)
    enc_grad, bias_grad, mean_square = encoder_grad(
        info,
        order,
        turned_tokens,
        features,
        feature_grad,
        [squares[key] for key in sorted(squares)],
        scale,
    )
    return (recon_error, mean_square[0, 0], enc_grad, bias_grad[0], dec_grad)


def solution(mesh):
    placed = (
        P("feat", "layer"),
        P("feat", "layer"),
        P(None, ("layer", "feat")),
        P(("layer", "feat")),
        P(None, ("layer", "feat"), None),
    )
    return jax.shard_map(
        on_device,
        mesh=mesh,
        in_specs=placed,
        out_specs=(
            P("feat", "layer"),
            P(),
            P(None, ("layer", "feat")),
            P(("layer", "feat")),
            P(None, ("layer", "feat"), None),
        ),
        check_vma=False,
    )
```

```python
import jax
import jax.numpy as jnp
from jax import lax
from jax.experimental import pallas as pl
from jax.experimental.pallas import tpu as pltpu
from jax.sharding import PartitionSpec as P

loss_scale = 64.0
tile = 256
in_vmem = pl.BlockSpec(memory_space=pltpu.VMEM)
in_smem = pl.BlockSpec(memory_space=pltpu.SMEM)
in_hbm = pl.BlockSpec(memory_space=pltpu.HBM)


def over_feat(value, mask):
    pairs = [(source, source ^ mask) for source in range(lax.axis_size("feat"))]
    return lax.ppermute(value, "feat", pairs)


def over_members(value, bit_level):
    mask = 2**bit_level
    pairs = [(source, source ^ mask) for source in range(lax.axis_size("layer"))]
    return lax.ppermute(value, "layer", pairs)


def over_layers(value, offset, sub_count, flip=0):
    count = lax.axis_size("layer")
    pairs = [(p, ((p + offset * sub_count) % count) ^ flip) for p in range(count)]
    return lax.ppermute(value, "layer", pairs)


def after(value, *others):
    return lax.optimization_barrier((value, *others))[0]


def all_over_feat(value):
    blocks = [value, over_feat(value, 1)]
    for s in range(2, lax.axis_size("feat")):
        blocks.append(over_feat(value, s))
    return blocks


def params(flops, bytes_accessed, scratch_mib):
    return dict(
        compiler_params=pltpu.CompilerParams(vmem_limit_bytes=scratch_mib * 1024 * 1024),
        cost_estimate=pl.CostEstimate(
            flops=flops, bytes_accessed=bytes_accessed, transcendentals=0
        ),
    )


def dot(left, right, contract):
    return lax.dot_general(
        left, right, ((contract[:1], contract[1:]), ((), ())), preferred_element_type=jnp.float32
    )


def span(index, size):
    return pl.ds(pl.multiple_of(index * size, size), size)


def fetch(*arrays):
    parts = [(number, start) for number, array in enumerate(arrays) for start in range(4)]

    def kernel(*refs):
        copies = []
        for place, (number, start) in enumerate(parts):
            source, target = refs[number], refs[len(arrays) + number]
            size = source.shape[-2] // 4
            here = (slice(None),) * (len(source.shape) - 2) + (pl.ds(start * size, size),)
            copies.append(
                pltpu.make_async_copy(source.at[here], target.at[here], refs[-1].at[place])
            )
        for copy in copies:
            copy.start()
        for copy in copies:
            copy.wait()

    total = sum(2 * array.size for array in arrays)
    return pl.pallas_call(
        kernel,
        in_specs=[in_hbm] * len(arrays),
        out_specs=[in_vmem] * len(arrays),
        out_shape=[jax.ShapeDtypeStruct(array.shape, array.dtype) for array in arrays],
        scratch_shapes=[pltpu.SemaphoreType.DMA((len(parts),))],
        name="fetch",
        **params(0, total, 14),
    )(*arrays)


def encode(info, rels, pieces, weights, partial, bias):
    feat_count, rows, cols = pieces[0].shape
    tok = feat_count * rows
    width = weights.shape[1]
    extra = [value for value in (partial, bias) if value is not None]

    def kernel(info_ref, *refs):
        piece_refs, weight_ref = refs[: len(pieces)], refs[len(pieces)]
        extra_refs, out_ref = refs[len(pieces) + 1 : -1], refs[-1]
        left = jnp.concatenate([ref[...].reshape(tok, cols) for ref in piece_refs], 1)
        for start in range(0, width, tile):
            here = slice(start, start + tile)
            right = jnp.concatenate(
                [weight_ref[span(info_ref[0] ^ rel, cols), here] for rel in rels], 0
            )
            total = dot(left, right, (1, 0))
            if partial is not None:
                total += extra_refs[0][:, here]
            if bias is None:
                out_ref[:, here] = total
            else:
                pre_act = total + extra_refs[-1][:, here]
                out_ref[0, :, here] = jnp.maximum(pre_act, 0.0).astype(jnp.bfloat16)
                out_ref[1, :, here] = jnp.where(pre_act > 0.0, 1.0, 0.0).astype(jnp.bfloat16)

    if bias is None:
        out_shape = jax.ShapeDtypeStruct((tok, width), jnp.float32)
    else:
        out_shape = jax.ShapeDtypeStruct((2, tok, width), jnp.bfloat16)
    return pl.pallas_call(
        kernel,
        in_specs=[in_smem] + [in_vmem] * (len(pieces) + 1 + len(extra)),
        out_specs=in_vmem,
        out_shape=out_shape,
        name="encode",
        **params(
            2 * len(pieces) * tok * cols * width, 2 * len(pieces) * cols * (tok + width), 4
        ),
    )(info, *pieces, weights, *extra)


def decode(info, features, weights, offset, groups, rows, cols):
    _, tok, width = features.shape
    count = weights.shape[2] // cols // 2

    def kernel(info_ref, feat_ref, weight_ref, *out_refs):
        left = feat_ref[0]
        even = info_ref[0] % 2 == 0
        for pair in range(count):
            piece = pair ^ (info_ref[0] // 2)
            for start in range(0, cols, tile):
                low, high = (
                    dot(left, weight_ref[offset, :, base + start : base + start + tile], (1, 0)).astype(
                        jnp.bfloat16
                    )
                    for base in (2 * pair * cols, (2 * pair + 1) * cols)
                )
                sides = (jnp.where(even, high, low), jnp.where(even, low, high))
                for side, product in enumerate(sides):
                    for number, group in enumerate(groups):
                        for place, block in enumerate(group):
                            out_refs[side * len(groups) + number][
                                piece, place, :, start : start + tile
                            ] = product[block * rows : (block + 1) * rows]
    out_shape = [
        jax.ShapeDtypeStruct((count, len(group), rows, cols), jnp.bfloat16) for group in groups
    ] * 2
    result = pl.pallas_call(
        kernel,
        in_specs=[in_smem, in_vmem, in_vmem],
        out_specs=[in_vmem] * len(out_shape),
        out_shape=out_shape,
        name="decode",
        **params(4 * count * tok * cols * width, 4 * count * cols * width, 4),
    )(info, features, weights)
    return result[: len(groups)], result[len(groups) :]


def turned(value, count):
    _, tok, width = value.shape

    def kernel(in_ref, out_ref):
        for piece in range(count):
            for start in range(0, width, tile):
                out_ref[piece, start : start + tile, :] = in_ref[
                    piece, :, start : start + tile
                ].T

    return pl.pallas_call(
        kernel,
        in_specs=[in_vmem],
        out_specs=in_vmem,
        out_shape=jax.ShapeDtypeStruct((count, width, tok), value.dtype),
        name="turned",
        **params(0, 4 * count * tok * width, 4),
    )(value)


def tree_sum(values):
    while len(values) > 1:
        values = [values[i] + values[i + 1] for i in range(0, len(values), 2)]
    return values[0]


def backward_pair(info, rel, offset, own, other, turned_features, dec_weight, feature_grad, dec_grad):
    layers, width, depth = dec_weight.shape
    tok = turned_features.shape[1]
    cols = own[0].shape[2]
    first = feature_grad is None
    extra = [] if first else [feature_grad, dec_grad]
    inputs = [*own, *other]

    def kernel(info_ref, *refs):
        grad_refs = refs[: len(inputs)]
        feat_ref, weight_ref = refs[len(inputs) : len(inputs) + 2]
        out_ref, dec_ref, square_ref, held, sems = refs[-5:]
        columns = span((info_ref[0] ^ rel) // 2, 2 * cols)
        starts = range(0, width, tile)
        copies = [
            pltpu.make_async_copy(
                held.at[slice(start, start + tile)],
                dec_ref.at[offset, slice(start, start + tile), columns],
                sems.at[place],
            )
            for place, start in enumerate(starts)
        ]
        sides, sums = [], []
        for side in (grad_refs[: len(own)], grad_refs[len(own) :]):
            blocks = [ref[i] for ref in side for i in range(ref.shape[0])]
            totals = []
            for block in blocks:
                total = jnp.zeros((8, 128), jnp.float32)
                for row in range(0, block.shape[0], 8):
                    for col in range(0, cols, 128):
                        part = block[row : row + 8, col : col + 128].astype(jnp.float32)
                        total += part * part
                totals.append(total)
            sums.append(tree_sum(totals))
            sides.append(jnp.concatenate(blocks, 0))
        square_ref[...] = tree_sum(sums)

        def products():
            second = info_ref[0] % 2 > 0
            grad = jnp.concatenate(
                [jnp.where(second, sides[1], sides[0]), jnp.where(second, sides[0], sides[1])], 1
            )
            for copy, start in zip(copies, starts):
                here = slice(start, start + tile)
                held[here] = dot(feat_ref[here], grad, (1, 0)).astype(jnp.bfloat16)
                copy.start()
            for start in starts:
                here = slice(start, start + tile)
                product = dot(grad, weight_ref[offset, here, columns], (1, 1))
                if not first:
                    product += refs[len(inputs) + 2][:, here]
                out_ref[:, here] = product

        def nothing():
            held[...] = jnp.zeros_like(held)
            for copy in copies:
                copy.start()
            out_ref[...] = refs[len(inputs) + 2][...]

        if offset == 0:
            products()
        else:
            pl.when(info_ref[1] >= offset)(products)
            pl.when(info_ref[1] < offset)(nothing)
        for copy in copies:
            copy.wait()

    return pl.pallas_call(
        kernel,
        in_specs=[in_smem]
        + [in_vmem] * (len(inputs) + 2)
        + ([] if first else [in_vmem, in_hbm]),
        out_specs=[in_vmem, in_hbm, in_vmem],
        out_shape=[
            jax.ShapeDtypeStruct((tok, width), jnp.float32),
            jax.ShapeDtypeStruct((layers, width, depth), jnp.bfloat16),
            jax.ShapeDtypeStruct((8, 128), jnp.float32),
        ],
        scratch_shapes=[
            pltpu.VMEM((width, 2 * cols), jnp.bfloat16),
            pltpu.SemaphoreType.DMA((width // tile,)),
        ],
        input_output_aliases={} if first else {len(inputs) + 3: 0, len(inputs) + 4: 1},
        name="backward_pair",
        **params(tok * cols, tok * cols, 8),
    )(info, *inputs, turned_features, dec_weight, *extra)


def encoder_grad(info, rels, turned_tokens, features, feature_grad, squares, scale):
    count, cols, tok = turned_tokens[0].shape
    width = features.shape[2]
    pieces = len(turned_tokens) * count

    def kernel(info_ref, *refs):
        token_refs = refs[: len(turned_tokens)]
        mask_ref, grad_ref = refs[len(turned_tokens) : len(turned_tokens) + 2]
        square_refs = refs[len(turned_tokens) + 2 : -6]
        enc_ref, bias_ref, mean_ref, preact, held, sems = refs[-6:]
        mean_ref[...] = scale * jnp.sum(
            tree_sum([ref[...] for ref in square_refs]), (0, 1), keepdims=True
        )
        for start in range(0, width, tile):
            here = slice(start, start + tile)
            kept = jnp.where(mask_ref[1, :, here] > 0.0, grad_ref[:, here], 0.0).astype(jnp.bfloat16)
            preact[:, here] = kept
            bias_ref[:, here] = jnp.sum(kept.astype(jnp.float32), 0, keepdims=True)
        copies = []
        for piece in range(pieces):
            held[piece] = dot(
                token_refs[piece // count][piece % count], preact[...], (1, 0)
            ).astype(jnp.bfloat16)
            copy = pltpu.make_async_copy(
                held.at[piece], enc_ref.at[span(info_ref[0] ^ rels[piece], cols)], sems.at[piece]
            )
            copy.start()
            copies.append(copy)
        for copy in copies:
            copy.wait()

    return pl.pallas_call(
        kernel,
        in_specs=[in_smem] + [in_vmem] * (len(turned_tokens) + 2 + len(squares)),
        out_specs=[in_hbm, in_vmem, in_vmem],
        out_shape=[
            jax.ShapeDtypeStruct((pieces * cols, width), jnp.bfloat16),
            jax.ShapeDtypeStruct((1, width), jnp.float32),
            jax.ShapeDtypeStruct((1, 1), jnp.float32),
        ],
        scratch_shapes=[
            pltpu.VMEM((tok, width), jnp.bfloat16),
            pltpu.VMEM((pieces, cols, width), jnp.bfloat16),
            pltpu.SemaphoreType.DMA((pieces,)),
        ],
        name="encoder_grad",
        **params(
            2 * pieces * tok * cols * width, 2 * pieces * cols * (tok + width) + 6 * tok * width, 10
        ),
    )(info, *turned_tokens, features, feature_grad, *squares)


def add_pair(left, right):
    return (left.astype(jnp.float32) + right.astype(jnp.float32)).astype(jnp.bfloat16)


def on_device(tokens_in, targets, enc_weight, enc_bias, dec_weight):
    layers, width, depth = dec_weight.shape
    feat_count = lax.axis_size("feat")
    sub_count = lax.axis_size("layer") // layers
    position = lax.axis_index("layer")
    layer = position // sub_count
    rows, cols = tokens_in.shape
    tok = feat_count * rows
    bit_count = sub_count.bit_length() - 1
    groups = [list(range(feat_count // 2)), list(range(feat_count // 2, feat_count))]

    info = jnp.stack([position % sub_count, layers - 1 - layer]).astype(jnp.int32)
    real = [layer >= k for k in range(layers)]
    tokens_in, info, *real = lax.optimization_barrier((tokens_in, info, *real))
    enc_weight = pltpu.with_memory_space_constraint(enc_weight, pltpu.HBM)
    dec_weight = pltpu.with_memory_space_constraint(dec_weight, pltpu.HBM)

    order = list(range(0, sub_count, 2)) + list(range(1, sub_count, 2))
    held = {rel: [None] * feat_count for rel in order[: sub_count // 2]}

    def take(s, *others):
        known = [0]
        for bit_level in range(bit_count - 1, 0, -1):
            for rel in known:
                value = after(held[rel][s], *others) if others else held[rel][s]
                held[rel ^ 2**bit_level][s] = over_members(value, bit_level)
            known += [rel ^ 2**bit_level for rel in known]
        return [held[rel][s] for rel in known[1:]]

    held[0][0] = tokens_in
    taken = take(0)
    mask = feat_count // 2
    while mask > 0:
        for s in range(0, feat_count, 2 * mask):
            value = held[0][s]
            held[0][s ^ mask] = over_feat(after(value, taken[0]) if s > 0 else value, mask)
        mask //= 2
    (enc_held,) = fetch(enc_weight)
    for s in range(1, feat_count - 1):
        taken += take(s, *([enc_held] if s == 1 else []))
    take(feat_count - 1, *taken)
    (dec_held,) = fetch(after(dec_weight, held[0][feat_count - 1], enc_held))
    tokens = {}
    for rel in order[: sub_count // 2]:
        tokens[rel] = after(jnp.stack(held[rel], 0), dec_held)
        tokens[rel ^ 1] = over_members(tokens[rel], 0)
    near, far = order[: sub_count // 2], order[sub_count // 2 :]
    partial = encode(info, near, [tokens[rel] for rel in near], enc_held, None, None)
    features = encode(
        info, far, [tokens[rel] for rel in far], enc_held, partial, enc_bias[None]
    )

    current, source = {}, features
    for k in reversed(range(layers)):
        sent, kept = decode(info, source, dec_held, k, groups, rows, cols)
        for place in reversed(range(len(groups))):
            current[place, k] = add_pair(kept[place], over_members(sent[place], 0))
        source = after(features, current[len(groups) - 1, k])
    def split_pairs(value):
        return value.reshape((value.shape[0] // 2, 2) + value.shape[1:])

    for bit_level in range(1, bit_count - 1):
        for turn, value in current.items():
            split = split_pairs(value)
            current[turn] = add_pair(split[:, 0], over_members(split[:, 1], bit_level))
    top = 2 ** (bit_count - 1)
    blocks, arrived = [None] * feat_count, []
    for place in reversed(range(len(groups))):
        split = split_pairs(current[place, 0])
        moved = over_members(after(split[:, 1], *arrived), bit_count - 1)
        total = split[:, 0].astype(jnp.float32) + moved.astype(jnp.float32)
        last = arrived
        arrived = [moved]
        for k in range(1, layers):
            split = split_pairs(current[place, k])
            for half, flip in ((0, 0), (1, top)):
                moved = over_layers(after(split[:, half], *last), k, sub_count, flip)
                moved = jnp.where(real[k], moved, jnp.zeros_like(moved))
                total = total + moved.astype(jnp.float32)
        for spot, block in enumerate(groups[place]):
            blocks[block] = total[0, spot]
    rebuilt = blocks[0]
    for s in reversed(range(1, feat_count)):
        rebuilt = rebuilt + over_feat(blocks[s].astype(jnp.bfloat16), s).astype(jnp.float32)
    turned_features = turned(source, 1)[0]
    turned_tokens = [
        turned(after(tokens[rel], turned_features).reshape(1, tok, cols), 1) for rel in order
    ]
    recon_error = rebuilt - after(targets, turned_features, *turned_tokens).astype(jnp.float32)
    scaled = (loss_scale / tok * recon_error).astype(jnp.bfloat16)

    blocks = all_over_feat(scaled)
    spans = [[s] for s in range(min(2, feat_count))]
    spans += [list(range(2, feat_count))] if feat_count > 2 else []
    groups_of = {(rel, k): [] for rel in range(0, sub_count, 2) for k in range(layers)}
    early = []
    for place, group in enumerate(spans):
        stacked = jnp.stack([blocks[s] for s in group], 0)
        for k in range(layers):
            for rel in range(0, sub_count, 2):
                low = rel & -rel
                if k == 0 and rel == 0:
                    part = stacked
                elif rel == 0 or (k > 0 and place == len(spans) - 1):
                    part = over_layers(stacked, -k, sub_count, rel)
                else:
                    part = over_members(groups_of[rel ^ low, k][place], low.bit_length() - 1)
                groups_of[rel, k].append(part)
                if place < len(spans) - 1:
                    early.append(part)
    later = early[-1:] + [groups_of[0, k][-1] for k in range(1, layers)]
    early = early[:-1]

    feature_grad, dec_grad, squares = None, None, {}
    for k in range(layers):
        for rel in range(0, sub_count, 2):
            parts = groups_of[rel, k]
            if feature_grad is None:
                parts = [after(parts[0], *early)] + parts[1:]
            else:
                parts = [after(part, feature_grad) for part in parts]
                feature_grad = after(feature_grad, *(later if k == 0 else groups_of[2, k]))
            feature_grad, dec_grad, squares[k, rel] = backward_pair(
                info,
                rel,
                k,
                parts,
                [over_members(part, 0) for part in parts],
                turned_features,
                dec_held,
                feature_grad,
                dec_grad,
            )
    scale = (tok / loss_scale) ** 2 / (layers * tok * depth)
    enc_grad, bias_grad, mean_square = encoder_grad(
        info,
        order,
        turned_tokens,
        features,
        feature_grad,
        [squares[key] for key in sorted(squares)],
        scale,
    )
    return (recon_error, mean_square[0, 0], enc_grad, bias_grad[0], dec_grad)


def solution(mesh):
    placed = (
        P("feat", "layer"),
        P("feat", "layer"),
        P(None, ("layer", "feat")),
        P(("layer", "feat")),
        P(None, ("layer", "feat"), None),
    )
    return jax.shard_map(
        on_device,
        mesh=mesh,
        in_specs=placed,
        out_specs=(
            P("feat", "layer"),
            P(),
            P(None, ("layer", "feat")),
            P(("layer", "feat")),
            P(None, ("layer", "feat"), None),
        ),
        check_vma=False,
    )
```

```python
import jax
import jax.numpy as jnp
from jax import lax
from jax.experimental import pallas as pl
from jax.experimental.pallas import tpu as pltpu
from jax.sharding import PartitionSpec as P

loss_scale = 64.0
tile = 256
in_vmem = pl.BlockSpec(memory_space=pltpu.VMEM)
in_smem = pl.BlockSpec(memory_space=pltpu.SMEM)
in_hbm = pl.BlockSpec(memory_space=pltpu.HBM)


def over_feat(value, mask):
    pairs = [(source, source ^ mask) for source in range(lax.axis_size("feat"))]
    return lax.ppermute(value, "feat", pairs)


def over_members(value, bit_level):
    mask = 2**bit_level
    pairs = [(source, source ^ mask) for source in range(lax.axis_size("layer"))]
    return lax.ppermute(value, "layer", pairs)


def to_layer(value, offset, sub_count, real):
    count = lax.axis_size("layer")
    pairs = [(p, (p + offset * sub_count) % count) for p in range(count)]
    moved = lax.ppermute(value, "layer", pairs)
    return jnp.where(real[offset], moved, jnp.zeros_like(moved))


def from_layer(value, offset, sub_count):
    count = lax.axis_size("layer")
    pairs = [(p, (p - offset * sub_count) % count) for p in range(count)]
    return lax.ppermute(value, "layer", pairs)


def after(value, *others):
    return lax.optimization_barrier((value, *others))[0]


def all_over_feat(value):
    blocks = [value, over_feat(value, 1)]
    for s in range(2, lax.axis_size("feat")):
        blocks.append(over_feat(value, s))
    return blocks


def params(flops, bytes_accessed, scratch_mib):
    return dict(
        compiler_params=pltpu.CompilerParams(vmem_limit_bytes=scratch_mib * 1024 * 1024),
        cost_estimate=pl.CostEstimate(
            flops=flops, bytes_accessed=bytes_accessed, transcendentals=0
        ),
    )


def dot(left, right, contract):
    return lax.dot_general(
        left, right, ((contract[:1], contract[1:]), ((), ())), preferred_element_type=jnp.float32
    )


def span(index, size):
    return pl.ds(pl.multiple_of(index * size, size), size)


def fetch(*arrays):
    parts = [(number, start) for number, array in enumerate(arrays) for start in range(4)]

    def kernel(*refs):
        copies = []
        for place, (number, start) in enumerate(parts):
            source, target = refs[number], refs[len(arrays) + number]
            size = source.shape[-2] // 4
            here = (slice(None),) * (len(source.shape) - 2) + (pl.ds(start * size, size),)
            copies.append(
                pltpu.make_async_copy(source.at[here], target.at[here], refs[-1].at[place])
            )
        for copy in copies:
            copy.start()
        for copy in copies:
            copy.wait()

    total = sum(2 * array.size for array in arrays)
    return pl.pallas_call(
        kernel,
        in_specs=[in_hbm] * len(arrays),
        out_specs=[in_vmem] * len(arrays),
        out_shape=[jax.ShapeDtypeStruct(array.shape, array.dtype) for array in arrays],
        scratch_shapes=[pltpu.SemaphoreType.DMA((len(parts),))],
        name="fetch",
        **params(0, total, 14),
    )(*arrays)


def encode(info, rels, pieces, weights, partial, bias):
    feat_count, rows, cols = pieces[0].shape
    tok = feat_count * rows
    width = weights.shape[1]
    extra = [value for value in (partial, bias) if value is not None]

    def kernel(info_ref, *refs):
        piece_refs, weight_ref = refs[: len(pieces)], refs[len(pieces)]
        extra_refs, out_ref = refs[len(pieces) + 1 : -1], refs[-1]
        left = jnp.concatenate([ref[...].reshape(tok, cols) for ref in piece_refs], 1)
        for start in range(0, width, tile):
            here = slice(start, start + tile)
            right = jnp.concatenate(
                [weight_ref[span(info_ref[0] ^ rel, cols), here] for rel in rels], 0
            )
            total = dot(left, right, (1, 0))
            if partial is not None:
                total += extra_refs[0][:, here]
            if bias is None:
                out_ref[:, here] = total
            else:
                pre_act = total + extra_refs[-1][:, here]
                out_ref[0, :, here] = jnp.maximum(pre_act, 0.0).astype(jnp.bfloat16)
                out_ref[1, :, here] = jnp.where(pre_act > 0.0, 1.0, 0.0).astype(jnp.bfloat16)

    if bias is None:
        out_shape = jax.ShapeDtypeStruct((tok, width), jnp.float32)
    else:
        out_shape = jax.ShapeDtypeStruct((2, tok, width), jnp.bfloat16)
    return pl.pallas_call(
        kernel,
        in_specs=[in_smem] + [in_vmem] * (len(pieces) + 1 + len(extra)),
        out_specs=in_vmem,
        out_shape=out_shape,
        name="encode",
        **params(
            2 * len(pieces) * tok * cols * width, 2 * len(pieces) * cols * (tok + width), 4
        ),
    )(info, *pieces, weights, *extra)


def decode(info, features, weights, offset, groups, rows, cols):
    _, tok, width = features.shape
    count = weights.shape[2] // cols // 2

    def kernel(info_ref, feat_ref, weight_ref, *out_refs):
        left = feat_ref[0]
        even = info_ref[0] % 2 == 0
        for pair in range(count):
            piece = pair ^ (info_ref[0] // 2)
            for start in range(0, cols, tile):
                low, high = (
                    dot(left, weight_ref[offset, :, base + start : base + start + tile], (1, 0)).astype(
                        jnp.bfloat16
                    )
                    for base in (2 * pair * cols, (2 * pair + 1) * cols)
                )
                sides = (jnp.where(even, high, low), jnp.where(even, low, high))
                for side, product in enumerate(sides):
                    for number, group in enumerate(groups):
                        for place, block in enumerate(group):
                            out_refs[side * len(groups) + number][
                                piece, place, :, start : start + tile
                            ] = product[block * rows : (block + 1) * rows]
    out_shape = [
        jax.ShapeDtypeStruct((count, len(group), rows, cols), jnp.bfloat16) for group in groups
    ] * 2
    result = pl.pallas_call(
        kernel,
        in_specs=[in_smem, in_vmem, in_vmem],
        out_specs=[in_vmem] * len(out_shape),
        out_shape=out_shape,
        name="decode",
        **params(4 * count * tok * cols * width, 4 * count * cols * width, 4),
    )(info, features, weights)
    return result[: len(groups)], result[len(groups) :]


def turned(value, count):
    _, tok, width = value.shape

    def kernel(in_ref, out_ref):
        for piece in range(count):
            for start in range(0, width, tile):
                out_ref[piece, start : start + tile, :] = in_ref[
                    piece, :, start : start + tile
                ].T

    return pl.pallas_call(
        kernel,
        in_specs=[in_vmem],
        out_specs=in_vmem,
        out_shape=jax.ShapeDtypeStruct((count, width, tok), value.dtype),
        name="turned",
        **params(0, 4 * count * tok * width, 4),
    )(value)


def tree_sum(values):
    while len(values) > 1:
        values = [values[i] + values[i + 1] for i in range(0, len(values), 2)]
    return values[0]


def backward_pair(info, rel, offset, own, other, turned_features, dec_weight, feature_grad, dec_grad):
    layers, width, depth = dec_weight.shape
    tok = turned_features.shape[1]
    cols = own[0].shape[2]
    first = feature_grad is None
    extra = [] if first else [feature_grad, dec_grad]
    inputs = [*own, *other]

    def kernel(info_ref, *refs):
        grad_refs = refs[: len(inputs)]
        feat_ref, weight_ref = refs[len(inputs) : len(inputs) + 2]
        out_ref, dec_ref, square_ref, held, sems = refs[-5:]
        columns = span((info_ref[0] ^ rel) // 2, 2 * cols)
        starts = range(0, width, tile)
        copies = [
            pltpu.make_async_copy(
                held.at[slice(start, start + tile)],
                dec_ref.at[offset, slice(start, start + tile), columns],
                sems.at[place],
            )
            for place, start in enumerate(starts)
        ]
        sides, sums = [], []
        for side in (grad_refs[: len(own)], grad_refs[len(own) :]):
            blocks = [ref[i] for ref in side for i in range(ref.shape[0])]
            totals = []
            for block in blocks:
                total = jnp.zeros((8, 128), jnp.float32)
                for row in range(0, block.shape[0], 8):
                    for col in range(0, cols, 128):
                        part = block[row : row + 8, col : col + 128].astype(jnp.float32)
                        total += part * part
                totals.append(total)
            sums.append(tree_sum(totals))
            sides.append(jnp.concatenate(blocks, 0))
        square_ref[...] = tree_sum(sums)

        def products():
            second = info_ref[0] % 2 > 0
            grad = jnp.concatenate(
                [jnp.where(second, sides[1], sides[0]), jnp.where(second, sides[0], sides[1])], 1
            )
            for copy, start in zip(copies, starts):
                here = slice(start, start + tile)
                held[here] = dot(feat_ref[here], grad, (1, 0)).astype(jnp.bfloat16)
                copy.start()
            for start in starts:
                here = slice(start, start + tile)
                product = dot(grad, weight_ref[offset, here, columns], (1, 1))
                if not first:
                    product += refs[len(inputs) + 2][:, here]
                out_ref[:, here] = product

        def nothing():
            held[...] = jnp.zeros_like(held)
            for copy in copies:
                copy.start()
            out_ref[...] = refs[len(inputs) + 2][...]

        if offset == 0:
            products()
        else:
            pl.when(info_ref[1] >= offset)(products)
            pl.when(info_ref[1] < offset)(nothing)
        for copy in copies:
            copy.wait()

    return pl.pallas_call(
        kernel,
        in_specs=[in_smem]
        + [in_vmem] * (len(inputs) + 2)
        + ([] if first else [in_vmem, in_hbm]),
        out_specs=[in_vmem, in_hbm, in_vmem],
        out_shape=[
            jax.ShapeDtypeStruct((tok, width), jnp.float32),
            jax.ShapeDtypeStruct((layers, width, depth), jnp.bfloat16),
            jax.ShapeDtypeStruct((8, 128), jnp.float32),
        ],
        scratch_shapes=[
            pltpu.VMEM((width, 2 * cols), jnp.bfloat16),
            pltpu.SemaphoreType.DMA((width // tile,)),
        ],
        input_output_aliases={} if first else {len(inputs) + 3: 0, len(inputs) + 4: 1},
        name="backward_pair",
        **params(tok * cols, tok * cols, 8),
    )(info, *inputs, turned_features, dec_weight, *extra)


def encoder_grad(info, rels, turned_tokens, features, feature_grad, squares, scale):
    count, cols, tok = turned_tokens[0].shape
    width = features.shape[2]
    pieces = len(turned_tokens) * count

    def kernel(info_ref, *refs):
        token_refs = refs[: len(turned_tokens)]
        mask_ref, grad_ref = refs[len(turned_tokens) : len(turned_tokens) + 2]
        square_refs = refs[len(turned_tokens) + 2 : -6]
        enc_ref, bias_ref, mean_ref, preact, held, sems = refs[-6:]
        mean_ref[...] = scale * jnp.sum(
            tree_sum([ref[...] for ref in square_refs]), (0, 1), keepdims=True
        )
        for start in range(0, width, tile):
            here = slice(start, start + tile)
            kept = jnp.where(mask_ref[1, :, here] > 0.0, grad_ref[:, here], 0.0).astype(jnp.bfloat16)
            preact[:, here] = kept
            bias_ref[:, here] = jnp.sum(kept.astype(jnp.float32), 0, keepdims=True)
        copies = []
        for piece in range(pieces):
            held[piece] = dot(
                token_refs[piece // count][piece % count], preact[...], (1, 0)
            ).astype(jnp.bfloat16)
            copy = pltpu.make_async_copy(
                held.at[piece], enc_ref.at[span(info_ref[0] ^ rels[piece], cols)], sems.at[piece]
            )
            copy.start()
            copies.append(copy)
        for copy in copies:
            copy.wait()

    return pl.pallas_call(
        kernel,
        in_specs=[in_smem] + [in_vmem] * (len(turned_tokens) + 2 + len(squares)),
        out_specs=[in_hbm, in_vmem, in_vmem],
        out_shape=[
            jax.ShapeDtypeStruct((pieces * cols, width), jnp.bfloat16),
            jax.ShapeDtypeStruct((1, width), jnp.float32),
            jax.ShapeDtypeStruct((1, 1), jnp.float32),
        ],
        scratch_shapes=[
            pltpu.VMEM((tok, width), jnp.bfloat16),
            pltpu.VMEM((pieces, cols, width), jnp.bfloat16),
            pltpu.SemaphoreType.DMA((pieces,)),
        ],
        name="encoder_grad",
        **params(
            2 * pieces * tok * cols * width, 2 * pieces * cols * (tok + width) + 6 * tok * width, 10
        ),
    )(info, *turned_tokens, features, feature_grad, *squares)


def add_pair(left, right):
    return (left.astype(jnp.float32) + right.astype(jnp.float32)).astype(jnp.bfloat16)


def on_device(tokens_in, targets, enc_weight, enc_bias, dec_weight):
    layers, width, depth = dec_weight.shape
    feat_count = lax.axis_size("feat")
    sub_count = lax.axis_size("layer") // layers
    position = lax.axis_index("layer")
    layer = position // sub_count
    rows, cols = tokens_in.shape
    tok = feat_count * rows
    bit_count = sub_count.bit_length() - 1
    groups = [list(range(feat_count // 2))]
    groups += [[s] for s in range(feat_count // 2, feat_count)]

    info = jnp.stack([position % sub_count, layers - 1 - layer]).astype(jnp.int32)
    real = [layer >= k for k in range(layers)]
    tokens_in, info, *real = lax.optimization_barrier((tokens_in, info, *real))
    enc_weight = pltpu.with_memory_space_constraint(enc_weight, pltpu.HBM)
    dec_weight = pltpu.with_memory_space_constraint(dec_weight, pltpu.HBM)

    order = [rel for pair in range(0, sub_count, 2) for rel in (pair, pair ^ 1)]
    held = {rel: [None] * feat_count for rel in order[::2]}
    held[0] = all_over_feat(tokens_in)
    enc_held, dec_held = fetch(enc_weight, after(dec_weight, held[0][1]))
    for s in range(feat_count):
        known = [0]
        for bit_level in range(bit_count - 1, 0, -1):
            for rel in known:
                value = after(held[rel][s], dec_held) if s > 1 else held[rel][s]
                held[rel ^ 2**bit_level][s] = over_members(value, bit_level)
            known += [rel ^ 2**bit_level for rel in known]
    early = [
        held[rel][s] for rel in order[2::2] for s in range(feat_count) if 2 * s != feat_count
    ]
    tokens = {0: after(jnp.stack(held[0], 0), enc_held, *early)}
    tokens[1] = over_members(tokens[0], 0)
    partial = encode(info, [0, 1], [tokens[0], tokens[1]], enc_held, None, None)
    for rel in order[2::2]:
        tokens[rel] = jnp.stack([after(block, partial) for block in held[rel]], 0)
        tokens[rel ^ 1] = over_members(tokens[rel], 0)
    for rel in order[2:-1]:
        partial = encode(info, [rel], [tokens[rel]], enc_held, partial, None)
    features = encode(info, order[-1:], [tokens[order[-1]]], enc_held, partial, enc_bias[None])

    current, source = {}, features
    for k in reversed(range(layers)):
        sent, kept = decode(info, source, dec_held, k, groups, rows, cols)
        for place in reversed(range(len(groups))):
            current[place, k] = add_pair(kept[place], over_members(sent[place], 0))
        source = after(features, current[len(groups) - 1, k])
    turns = sorted(current, reverse=True)
    joined = {}
    for bit_level in range(1, bit_count):
        halves = {}
        for turn, value in current.items():
            split = value.reshape((value.shape[0] // 2, 2) + value.shape[1:])
            halves[turn] = (split[:, 0], split[:, 1])
        if bit_level == bit_count - 1:
            for k in range(1, layers):
                joined[k], sent = halves.pop((0, k))
                sent = to_layer(after(sent, halves[len(groups) - 1, 0][1]), k, sub_count, real)
                halves[0, 0] = (halves[0, 0][0], add_pair(halves[0, 0][1], sent))
        turns = [turn for turn in turns if turn in halves]
        received, operands = [], []
        for turn in turns:
            operand = halves[turn][1]
            if len(received) > 1:
                operand = after(operand, received[-2], operands[-1])
            operands.append(operand)
            received.append(over_members(operand, bit_level))
        for place, turn in enumerate(turns):
            arrived = after(received[place], *operands[place + 1 :][:1])
            if bit_level < bit_count - 1:
                current[turn] = add_pair(halves[turn][0], arrived)
            else:
                current[turn] = (halves[turn][0], arrived)
    blocks, operands = [None] * feat_count, []
    for place in reversed(range(len(groups))):
        total = sum(part.astype(jnp.float32) for part in current[place, 0])
        for k in range(1, layers):
            if place > 0:
                moved = to_layer(add_pair(*current[place, k]), k, sub_count, real)
            else:
                moved = to_layer(after(joined[k], *operands), k, sub_count, real)
            total = total + moved.astype(jnp.float32)
        for spot, block in enumerate(groups[place]):
            if block == 0:
                rebuilt = total[0, spot]
            else:
                operands.append(total[0, spot].astype(jnp.bfloat16))
                blocks[block] = over_feat(operands[-1], block)
    for block in reversed(blocks[1:]):
        rebuilt = rebuilt + block.astype(jnp.float32)
    turned_features = turned(source, 1)[0]
    turned_tokens = [
        turned(after(tokens[rel], turned_features).reshape(1, tok, cols), 1) for rel in order
    ]
    recon_error = rebuilt - after(targets, turned_features, *turned_tokens).astype(jnp.float32)
    scaled = (loss_scale / tok * recon_error).astype(jnp.bfloat16)

    blocks = all_over_feat(scaled)
    stages = [[0]]
    for level in range(bit_count - 1, 0, -1):
        known = [rel for stage in stages for rel in stage]
        stages.append([rel ^ 2**level for rel in known])
    spans = [[s] for s in range(min(2, feat_count))]
    spans += [list(range(2, feat_count))] if feat_count > 2 else []
    groups_of = {(0, k): [None] * len(spans) for k in range(layers)}
    early, last = [], len(spans) - 1
    for place, group in enumerate(spans):
        stacked = jnp.stack([blocks[s] for s in group], 0)
        groups_of[0, 0][place] = stacked
        for k in range(1, layers):
            groups_of[0, k][place] = from_layer(stacked, k, sub_count)
        known = [0]
        for level in range(bit_count - 1, 0, -1):
            for rel in known:
                other = rel ^ 2**level
                for k in range(layers):
                    if k == 0 or place < last:
                        part = over_members(groups_of[rel, k][place], level)
                    else:
                        part = from_layer(groups_of[other, 0][place], k, sub_count)
                    groups_of.setdefault((other, k), [None] * len(spans))[place] = part
            known += [rel ^ 2**level for rel in known]
        if place == last - 1:
            early = [part for parts in groups_of.values() for part in parts if part is not None]
            early.pop()

    feature_grad, dec_grad, squares = None, None, {}
    for k in range(layers):
        for rel in [rel for stage in stages for rel in stage]:
            parts = groups_of[rel, k]
            if feature_grad is None:
                parts = [after(parts[0], *early)] + parts[1:]
            elif rel > 0:
                parts = [after(part, feature_grad) for part in parts]
            feature_grad, dec_grad, squares[k, rel] = backward_pair(
                info,
                rel,
                k,
                parts,
                [over_members(part, 0) for part in parts],
                turned_features,
                dec_held,
                feature_grad,
                dec_grad,
            )
    scale = (tok / loss_scale) ** 2 / (layers * tok * depth)
    enc_grad, bias_grad, mean_square = encoder_grad(
        info,
        order,
        turned_tokens,
        features,
        feature_grad,
        [squares[key] for key in sorted(squares)],
        scale,
    )
    return (recon_error, mean_square[0, 0], enc_grad, bias_grad[0], dec_grad)


def solution(mesh):
    placed = (
        P("feat", "layer"),
        P("feat", "layer"),
        P(None, ("layer", "feat")),
        P(("layer", "feat")),
        P(None, ("layer", "feat"), None),
    )
    return jax.shard_map(
        on_device,
        mesh=mesh,
        in_specs=placed,
        out_specs=(
            P("feat", "layer"),
            P(),
            P(None, ("layer", "feat")),
            P(("layer", "feat")),
            P(None, ("layer", "feat"), None),
        ),
        check_vma=False,
    )
```

```python
import jax
import jax.numpy as jnp
from jax import lax
from jax.experimental import pallas as pl
from jax.experimental.pallas import tpu as pltpu
from jax.sharding import PartitionSpec as P

loss_scale = 64.0
tile = 256
in_vmem = pl.BlockSpec(memory_space=pltpu.VMEM)
in_smem = pl.BlockSpec(memory_space=pltpu.SMEM)
in_hbm = pl.BlockSpec(memory_space=pltpu.HBM)


def over_feat(value, mask):
    pairs = [(source, source ^ mask) for source in range(lax.axis_size("feat"))]
    return lax.ppermute(value, "feat", pairs)


def over_members(value, bit_level):
    mask = 2**bit_level
    pairs = [(source, source ^ mask) for source in range(lax.axis_size("layer"))]
    return lax.ppermute(value, "layer", pairs)


def to_layer(value, offset, sub_count, real):
    count = lax.axis_size("layer")
    pairs = [(p, (p + offset * sub_count) % count) for p in range(count)]
    moved = lax.ppermute(value, "layer", pairs)
    return jnp.where(real[offset], moved, jnp.zeros_like(moved))


def from_layer(value, offset, sub_count):
    count = lax.axis_size("layer")
    pairs = [(p, (p - offset * sub_count) % count) for p in range(count)]
    return lax.ppermute(value, "layer", pairs)


def after(value, *others):
    return lax.optimization_barrier((value, *others))[0]


def all_over_feat(value):
    blocks = [value, over_feat(value, 1)]
    for s in range(2, lax.axis_size("feat")):
        blocks.append(over_feat(value, s))
    return blocks


def params(flops, bytes_accessed, scratch_mib):
    return dict(
        compiler_params=pltpu.CompilerParams(vmem_limit_bytes=scratch_mib * 1024 * 1024),
        cost_estimate=pl.CostEstimate(
            flops=flops, bytes_accessed=bytes_accessed, transcendentals=0
        ),
    )


def dot(left, right, contract):
    return lax.dot_general(
        left, right, ((contract[:1], contract[1:]), ((), ())), preferred_element_type=jnp.float32
    )


def span(index, size):
    return pl.ds(pl.multiple_of(index * size, size), size)


def fetch(*arrays):
    parts = [(number, start) for number, array in enumerate(arrays) for start in range(4)]

    def kernel(*refs):
        copies = []
        for place, (number, start) in enumerate(parts):
            source, target = refs[number], refs[len(arrays) + number]
            size = source.shape[-2] // 4
            here = (slice(None),) * (len(source.shape) - 2) + (pl.ds(start * size, size),)
            copies.append(
                pltpu.make_async_copy(source.at[here], target.at[here], refs[-1].at[place])
            )
        for copy in copies:
            copy.start()
        for copy in copies:
            copy.wait()

    total = sum(2 * array.size for array in arrays)
    return pl.pallas_call(
        kernel,
        in_specs=[in_hbm] * len(arrays),
        out_specs=[in_vmem] * len(arrays),
        out_shape=[jax.ShapeDtypeStruct(array.shape, array.dtype) for array in arrays],
        scratch_shapes=[pltpu.SemaphoreType.DMA((len(parts),))],
        name="fetch",
        **params(0, total, 14),
    )(*arrays)


def encode(info, rels, pieces, weights, partial, bias):
    feat_count, rows, cols = pieces[0].shape
    tok = feat_count * rows
    width = weights.shape[1]
    extra = [value for value in (partial, bias) if value is not None]

    def kernel(info_ref, *refs):
        piece_refs, weight_ref = refs[: len(pieces)], refs[len(pieces)]
        extra_refs, out_ref = refs[len(pieces) + 1 : -1], refs[-1]
        left = jnp.concatenate([ref[...].reshape(tok, cols) for ref in piece_refs], 1)
        for start in range(0, width, tile):
            here = slice(start, start + tile)
            right = jnp.concatenate(
                [weight_ref[span(info_ref[0] ^ rel, cols), here] for rel in rels], 0
            )
            total = dot(left, right, (1, 0))
            if partial is not None:
                total += extra_refs[0][:, here]
            if bias is None:
                out_ref[:, here] = total
            else:
                pre_act = total + extra_refs[-1][:, here]
                out_ref[0, :, here] = jnp.maximum(pre_act, 0.0).astype(jnp.bfloat16)
                out_ref[1, :, here] = jnp.where(pre_act > 0.0, 1.0, 0.0).astype(jnp.bfloat16)

    if bias is None:
        out_shape = jax.ShapeDtypeStruct((tok, width), jnp.float32)
    else:
        out_shape = jax.ShapeDtypeStruct((2, tok, width), jnp.bfloat16)
    return pl.pallas_call(
        kernel,
        in_specs=[in_smem] + [in_vmem] * (len(pieces) + 1 + len(extra)),
        out_specs=in_vmem,
        out_shape=out_shape,
        name="encode",
        **params(
            2 * len(pieces) * tok * cols * width, 2 * len(pieces) * cols * (tok + width), 4
        ),
    )(info, *pieces, weights, *extra)


def decode(info, features, weights, offset, groups, rows, cols):
    _, tok, width = features.shape
    count = weights.shape[2] // cols // 2

    def kernel(info_ref, feat_ref, weight_ref, *out_refs):
        left = feat_ref[0]
        even = info_ref[0] % 2 == 0
        for pair in range(count):
            piece = pair ^ (info_ref[0] // 2)
            for start in range(0, cols, tile):
                low, high = (
                    dot(left, weight_ref[offset, :, base + start : base + start + tile], (1, 0)).astype(
                        jnp.bfloat16
                    )
                    for base in (2 * pair * cols, (2 * pair + 1) * cols)
                )
                sides = (jnp.where(even, high, low), jnp.where(even, low, high))
                for side, product in enumerate(sides):
                    for number, group in enumerate(groups):
                        for place, block in enumerate(group):
                            out_refs[side * len(groups) + number][
                                piece, place, :, start : start + tile
                            ] = product[block * rows : (block + 1) * rows]
    out_shape = [
        jax.ShapeDtypeStruct((count, len(group), rows, cols), jnp.bfloat16) for group in groups
    ] * 2
    result = pl.pallas_call(
        kernel,
        in_specs=[in_smem, in_vmem, in_vmem],
        out_specs=[in_vmem] * len(out_shape),
        out_shape=out_shape,
        name="decode",
        **params(4 * count * tok * cols * width, 4 * count * cols * width, 4),
    )(info, features, weights)
    return result[: len(groups)], result[len(groups) :]


def turned(value, count):
    _, tok, width = value.shape

    def kernel(in_ref, out_ref):
        for piece in range(count):
            for start in range(0, width, tile):
                out_ref[piece, start : start + tile, :] = in_ref[
                    piece, :, start : start + tile
                ].T

    return pl.pallas_call(
        kernel,
        in_specs=[in_vmem],
        out_specs=in_vmem,
        out_shape=jax.ShapeDtypeStruct((count, width, tok), value.dtype),
        name="turned",
        **params(0, 4 * count * tok * width, 4),
    )(value)


def tree_sum(values):
    while len(values) > 1:
        values = [values[i] + values[i + 1] for i in range(0, len(values), 2)]
    return values[0]


def backward_pair(
    info, rel, offset, own, other, turned_features, dec_weight, feature_grad, dec_grad, features
):
    layers, width, depth = dec_weight.shape
    tok = turned_features.shape[1]
    cols = own[0].shape[2]
    first = feature_grad is None
    extra = [] if first else [feature_grad, dec_grad]
    final = features is not None
    if final:
        extra.append(features)
    inputs = [*own, *other]

    def kernel(info_ref, *refs):
        grad_refs = refs[: len(inputs)]
        feat_ref, weight_ref = refs[len(inputs) : len(inputs) + 2]
        held, sems = refs[-2:]
        out_ref, dec_ref, square_ref = refs[len(inputs) + 2 + len(extra) :][:3]
        columns = span((info_ref[0] ^ rel) // 2, 2 * cols)
        starts = range(0, width, tile)
        copies = [
            pltpu.make_async_copy(
                held.at[slice(start, start + tile)],
                dec_ref.at[offset, slice(start, start + tile), columns],
                sems.at[place],
            )
            for place, start in enumerate(starts)
        ]
        sides, sums = [], []
        for side in (grad_refs[: len(own)], grad_refs[len(own) :]):
            blocks = [ref[i] for ref in side for i in range(ref.shape[0])]
            totals = []
            for block in blocks:
                total = jnp.zeros((8, 128), jnp.float32)
                for row in range(0, block.shape[0], 8):
                    for col in range(0, cols, 128):
                        part = block[row : row + 8, col : col + 128].astype(jnp.float32)
                        total += part * part
                totals.append(total)
            sums.append(tree_sum(totals))
            sides.append(jnp.concatenate(blocks, 0))
        square_ref[...] = tree_sum(sums)

        def products():
            second = info_ref[0] % 2 > 0
            grad = jnp.concatenate(
                [jnp.where(second, sides[1], sides[0]), jnp.where(second, sides[0], sides[1])], 1
            )
            for copy, start in zip(copies, starts):
                here = slice(start, start + tile)
                held[here] = dot(feat_ref[here], grad, (1, 0)).astype(jnp.bfloat16)
                copy.start()
            for start in starts:
                here = slice(start, start + tile)
                product = dot(grad, weight_ref[offset, here, columns], (1, 1))
                if not first:
                    product += refs[len(inputs) + 2][:, here]
                store(here, product)

        def store(here, total):
            if not final:
                out_ref[:, here] = total
                return
            mask_ref, bias_ref = refs[len(inputs) + 4], refs[-3]
            kept = jnp.where(mask_ref[1, :, here] > 0.0, total, 0.0).astype(jnp.bfloat16)
            out_ref[:, here] = kept
            bias_ref[:, here] = jnp.sum(kept.astype(jnp.float32), 0, keepdims=True)

        def nothing():
            held[...] = jnp.zeros_like(held)
            for copy in copies:
                copy.start()
            for start in starts:
                here = slice(start, start + tile)
                store(here, refs[len(inputs) + 2][:, here])

        if offset == 0:
            products()
        else:
            pl.when(info_ref[1] >= offset)(products)
            pl.when(info_ref[1] < offset)(nothing)
        for copy in copies:
            copy.wait()

    out_shape = [
        jax.ShapeDtypeStruct((tok, width), jnp.bfloat16 if final else jnp.float32),
        jax.ShapeDtypeStruct((layers, width, depth), jnp.bfloat16),
        jax.ShapeDtypeStruct((8, 128), jnp.float32),
    ]
    aliases = {} if first else {len(inputs) + 4: 1}
    if not first and not final:
        aliases[len(inputs) + 3] = 0
    if final:
        out_shape.append(jax.ShapeDtypeStruct((1, width), jnp.float32))
    return pl.pallas_call(
        kernel,
        in_specs=[in_smem]
        + [in_vmem] * (len(inputs) + 2)
        + ([] if first else [in_vmem, in_hbm])
        + ([in_vmem] if final else []),
        out_specs=[in_vmem, in_hbm, in_vmem] + ([in_vmem] if final else []),
        out_shape=out_shape,
        scratch_shapes=[
            pltpu.VMEM((width, 2 * cols), jnp.bfloat16),
            pltpu.SemaphoreType.DMA((width // tile,)),
        ],
        input_output_aliases=aliases,
        name="backward_pair",
        **params(tok * cols, tok * cols, 8),
    )(info, *inputs, turned_features, dec_weight, *extra)


def encoder_grad(info, rels, turned_tokens, preact_grad, squares, scale):
    _, cols, tok = turned_tokens[0].shape
    width = preact_grad.shape[1]
    pieces = len(turned_tokens)
    step = min(tile, cols)
    parts = [(piece, start) for piece in range(pieces) for start in range(0, cols, step)]

    def kernel(info_ref, *refs):
        token_refs, grad_ref = refs[:pieces], refs[pieces]
        square_refs = refs[pieces + 1 : -4]
        enc_ref, mean_ref, held, sems = refs[-4:]
        copies = []
        for place, (piece, start) in enumerate(parts):
            held[piece, start : start + step] = dot(
                token_refs[piece][0, start : start + step], grad_ref[...], (1, 0)
            ).astype(jnp.bfloat16)
            row = pl.multiple_of((info_ref[0] ^ rels[piece]) * cols + start, step)
            copy = pltpu.make_async_copy(
                held.at[piece, pl.ds(start, step)], enc_ref.at[pl.ds(row, step)], sems.at[place]
            )
            copy.start()
            copies.append(copy)
        mean_ref[...] = scale * jnp.sum(
            tree_sum([ref[...] for ref in square_refs]), (0, 1), keepdims=True
        )
        for copy in copies:
            copy.wait()

    return pl.pallas_call(
        kernel,
        in_specs=[in_smem] + [in_vmem] * (pieces + 1 + len(squares)),
        out_specs=[in_hbm, in_vmem],
        out_shape=[
            jax.ShapeDtypeStruct((pieces * cols, width), jnp.bfloat16),
            jax.ShapeDtypeStruct((1, 1), jnp.float32),
        ],
        scratch_shapes=[
            pltpu.VMEM((pieces, cols, width), jnp.bfloat16),
            pltpu.SemaphoreType.DMA((len(parts),)),
        ],
        name="encoder_grad",
        **params(2 * pieces * tok * cols * width, 2 * pieces * cols * (tok + width), 8),
    )(info, *turned_tokens, preact_grad, *squares)


def add_pair(left, right):
    return (left.astype(jnp.float32) + right.astype(jnp.float32)).astype(jnp.bfloat16)


def on_device(tokens_in, targets, enc_weight, enc_bias, dec_weight):
    layers, width, depth = dec_weight.shape
    feat_count = lax.axis_size("feat")
    sub_count = lax.axis_size("layer") // layers
    position = lax.axis_index("layer")
    layer = position // sub_count
    rows, cols = tokens_in.shape
    tok = feat_count * rows
    bit_count = sub_count.bit_length() - 1
    groups = [list(range(feat_count // 2))]
    groups += [[s] for s in range(feat_count // 2, feat_count)]

    info = jnp.stack([position % sub_count, layers - 1 - layer]).astype(jnp.int32)
    real = [layer >= k for k in range(layers)]
    tokens_in, info, *real = lax.optimization_barrier((tokens_in, info, *real))
    enc_weight = pltpu.with_memory_space_constraint(enc_weight, pltpu.HBM)
    dec_weight = pltpu.with_memory_space_constraint(dec_weight, pltpu.HBM)

    order = [rel for pair in range(0, sub_count, 2) for rel in (pair, pair ^ 1)]
    held = {rel: [None] * feat_count for rel in order[::2]}
    first = tokens_in
    if bit_count > 1:
        first = over_members(tokens_in, bit_count - 1)
    held[0] = all_over_feat(tokens_in)
    enc_held, dec_held = fetch(enc_weight, after(dec_weight, held[0][1]))
    for s in range(feat_count):
        known = [0]
        for bit_level in range(bit_count - 1, 0, -1):
            for rel in known:
                value = after(held[rel][s], dec_held) if s > 1 else held[rel][s]
                if s == 0 and bit_level == bit_count - 1:
                    held[rel ^ 2**bit_level][s] = first
                else:
                    held[rel ^ 2**bit_level][s] = over_members(value, bit_level)
            known += [rel ^ 2**bit_level for rel in known]
    early = [
        held[rel][s] for rel in order[2::2] for s in range(feat_count) if 2 * s != feat_count
    ]
    tokens = {0: after(jnp.stack(held[0], 0), enc_held, *early)}
    tokens[1] = over_members(tokens[0], 0)
    partial = encode(info, [0, 1], [tokens[0], tokens[1]], enc_held, None, None)
    for rel in order[2::2]:
        tokens[rel] = jnp.stack([after(block, partial) for block in held[rel]], 0)
        tokens[rel ^ 1] = over_members(tokens[rel], 0)
    for rel in order[2:-1]:
        partial = encode(info, [rel], [tokens[rel]], enc_held, partial, None)
    features = encode(info, order[-1:], [tokens[order[-1]]], enc_held, partial, enc_bias[None])

    current, source = {}, features
    for k in reversed(range(layers)):
        sent, kept = decode(info, source, dec_held, k, groups, rows, cols)
        for place in reversed(range(len(groups))):
            current[place, k] = add_pair(kept[place], over_members(sent[place], 0))
        source = after(features, current[len(groups) - 1, k])
    turns = sorted(current, reverse=True)
    for bit_level in range(1, bit_count):
        kept, received, operands = {}, [], []
        for turn in turns:
            value = current[turn]
            split = value.reshape((value.shape[0] // 2, 2) + value.shape[1:])
            kept[turn], operand = split[:, 0], split[:, 1]
            if len(received) > 1:
                operand = after(operand, received[-2], operands[-1])
            operands.append(operand)
            received.append(over_members(operand, bit_level))
        for place, turn in enumerate(turns):
            arrived = after(received[place], *operands[place + 1 :][:1])
            if bit_level < bit_count - 1:
                current[turn] = add_pair(kept[turn], arrived)
            else:
                current[turn] = (kept[turn], arrived)
    blocks, operands = [None] * feat_count, []
    for place in reversed(range(len(groups))):
        total = sum(part.astype(jnp.float32) for part in current[place, 0])
        for k in range(1, layers):
            value = add_pair(*current[place, k])
            if place == 0:
                value = after(value, *operands)
            total = total + to_layer(value, k, sub_count, real).astype(jnp.float32)
        for spot, block in enumerate(groups[place]):
            if block == 0:
                rebuilt = total[0, spot]
            else:
                operands.append(total[0, spot].astype(jnp.bfloat16))
                blocks[block] = over_feat(operands[-1], block)
    for block in reversed(blocks[1:]):
        rebuilt = rebuilt + block.astype(jnp.float32)
    turned_features = turned(source, 1)[0]
    turned_tokens = [
        turned(after(tokens[rel], turned_features).reshape(1, tok, cols), 1) for rel in order
    ]
    recon_error = rebuilt - after(targets, turned_features, *turned_tokens).astype(jnp.float32)
    scaled = (loss_scale / tok * recon_error).astype(jnp.bfloat16)

    blocks = all_over_feat(scaled)
    stages = [[0]]
    for level in range(bit_count - 1, 0, -1):
        known = [rel for stage in stages for rel in stage]
        stages.append([rel ^ 2**level for rel in known])
    spans = [[s] for s in range(min(2, feat_count))]
    spans += [list(range(2, feat_count))] if feat_count > 2 else []
    groups_of = {(0, k): [None] * len(spans) for k in range(layers)}
    early, last = [], len(spans) - 1
    for place, group in enumerate(spans):
        stacked = jnp.stack([blocks[s] for s in group], 0)
        groups_of[0, 0][place] = stacked
        for k in range(1, layers):
            groups_of[0, k][place] = from_layer(stacked, k, sub_count)
        known = [0]
        for level in range(bit_count - 1, 0, -1):
            for rel in known:
                other = rel ^ 2**level
                for k in range(layers):
                    if k == 0 or place < last:
                        part = over_members(groups_of[rel, k][place], level)
                    else:
                        part = from_layer(groups_of[other, 0][place], k, sub_count)
                    groups_of.setdefault((other, k), [None] * len(spans))[place] = part
            known += [rel ^ 2**level for rel in known]
        if place == last - 1:
            early = [groups_of[rel, k][spot] for rel, k in groups_of for spot in range(place)]
            early += [groups_of[0, k][place] for k in range(1, layers)]

    feature_grad, dec_grad, squares = None, None, {}
    uses = [(rel, k) for k in range(layers) for stage in stages for rel in stage]
    for rel, k in uses:
        parts = groups_of[rel, k]
        if feature_grad is None:
            parts = [after(parts[0], *early)] + parts[1:]
        elif rel > 0:
            parts = [after(part, feature_grad) for part in parts]
        feature_grad, dec_grad, squares[k, rel], *sums = backward_pair(
            info,
            rel,
            k,
            parts,
            [over_members(part, 0) for part in parts],
            turned_features,
            dec_held,
            feature_grad,
            dec_grad,
            features if (rel, k) == uses[-1] else None,
        )
    scale = (tok / loss_scale) ** 2 / (layers * tok * depth)
    enc_grad, mean_square = encoder_grad(
        info,
        order,
        turned_tokens,
        feature_grad,
        [squares[key] for key in sorted(squares)],
        scale,
    )
    return (recon_error, mean_square[0, 0], enc_grad, sums[0][0], dec_grad)


def solution(mesh):
    placed = (
        P("feat", "layer"),
        P("feat", "layer"),
        P(None, ("layer", "feat")),
        P(("layer", "feat")),
        P(None, ("layer", "feat"), None),
    )
    return jax.shard_map(
        on_device,
        mesh=mesh,
        in_specs=placed,
        out_specs=(
            P("feat", "layer"),
            P(),
            P(None, ("layer", "feat")),
            P(("layer", "feat")),
            P(None, ("layer", "feat"), None),
        ),
        check_vma=False,
    )
```

```python
import jax
import jax.numpy as jnp
from jax import lax
from jax.experimental import pallas as pl
from jax.experimental.pallas import tpu as pltpu
from jax.sharding import PartitionSpec as P

loss_scale = 64.0
tile = 256
in_vmem = pl.BlockSpec(memory_space=pltpu.VMEM)
in_smem = pl.BlockSpec(memory_space=pltpu.SMEM)
in_hbm = pl.BlockSpec(memory_space=pltpu.HBM)


def over_feat(value, mask):
    pairs = [(source, source ^ mask) for source in range(lax.axis_size("feat"))]
    return lax.ppermute(value, "feat", pairs)


def over_members(value, bit_level):
    mask = 2**bit_level
    pairs = [(source, source ^ mask) for source in range(lax.axis_size("layer"))]
    return lax.ppermute(value, "layer", pairs)


def to_layer(value, offset, sub_count, real):
    count = lax.axis_size("layer")
    pairs = [(p, (p + offset * sub_count) % count) for p in range(count)]
    moved = lax.ppermute(value, "layer", pairs)
    return jnp.where(real[offset], moved, jnp.zeros_like(moved))


def from_layer(value, offset, sub_count):
    count = lax.axis_size("layer")
    pairs = [(p, (p - offset * sub_count) % count) for p in range(count)]
    return lax.ppermute(value, "layer", pairs)


def after(value, *others):
    return lax.optimization_barrier((value, *others))[0]


def all_over_feat(value, turn=0):
    count = lax.axis_size("feat")
    blocks = [value] + [None] * (count - 1)
    for s in (range(1, count) if turn == 0 else reversed(range(1, count))):
        blocks[s] = over_feat(value, s)
    return blocks


def params(flops, bytes_accessed, scratch_mib):
    return dict(
        compiler_params=pltpu.CompilerParams(vmem_limit_bytes=scratch_mib * 1024 * 1024),
        cost_estimate=pl.CostEstimate(
            flops=flops, bytes_accessed=bytes_accessed, transcendentals=0
        ),
    )


def dot(left, right, contract):
    return lax.dot_general(
        left, right, ((contract[:1], contract[1:]), ((), ())), preferred_element_type=jnp.float32
    )


def span(index, size):
    return pl.ds(pl.multiple_of(index * size, size), size)


def fetch(*arrays):
    parts = [(number, start) for number, array in enumerate(arrays) for start in range(4)]

    def kernel(*refs):
        copies = []
        for place, (number, start) in enumerate(parts):
            source, target = refs[number], refs[len(arrays) + number]
            size = source.shape[-2] // 4
            here = (slice(None),) * (len(source.shape) - 2) + (pl.ds(start * size, size),)
            copies.append(
                pltpu.make_async_copy(source.at[here], target.at[here], refs[-1].at[place])
            )
        for copy in copies:
            copy.start()
        for copy in copies:
            copy.wait()

    total = sum(2 * array.size for array in arrays)
    return pl.pallas_call(
        kernel,
        in_specs=[in_hbm] * len(arrays),
        out_specs=[in_vmem] * len(arrays),
        out_shape=[jax.ShapeDtypeStruct(array.shape, array.dtype) for array in arrays],
        scratch_shapes=[pltpu.SemaphoreType.DMA((len(parts),))],
        name="fetch",
        **params(0, total, 14),
    )(*arrays)


def encode(info, rels, pieces, weights, partial, bias):
    feat_count, rows, cols = pieces[0].shape
    tok = feat_count * rows
    width = weights.shape[1]
    extra = [value for value in (partial, bias) if value is not None]

    def kernel(info_ref, *refs):
        piece_refs, weight_ref = refs[: len(pieces)], refs[len(pieces)]
        extra_refs, out_ref = refs[len(pieces) + 1 : -1], refs[-1]
        left = jnp.concatenate([ref[...].reshape(tok, cols) for ref in piece_refs], 1)
        for start in range(0, width, tile):
            here = slice(start, start + tile)
            right = jnp.concatenate(
                [weight_ref[span(info_ref[0] ^ rel, cols), here] for rel in rels], 0
            )
            total = dot(left, right, (1, 0))
            if partial is not None:
                total += extra_refs[0][:, here]
            if bias is None:
                out_ref[:, here] = total
            else:
                pre_act = total + extra_refs[-1][:, here]
                out_ref[0, :, here] = jnp.maximum(pre_act, 0.0).astype(jnp.bfloat16)
                out_ref[1, :, here] = jnp.where(pre_act > 0.0, 1.0, 0.0).astype(jnp.bfloat16)

    if bias is None:
        out_shape = jax.ShapeDtypeStruct((tok, width), jnp.float32)
    else:
        out_shape = jax.ShapeDtypeStruct((2, tok, width), jnp.bfloat16)
    return pl.pallas_call(
        kernel,
        in_specs=[in_smem] + [in_vmem] * (len(pieces) + 1 + len(extra)),
        out_specs=in_vmem,
        out_shape=out_shape,
        name="encode",
        **params(
            2 * len(pieces) * tok * cols * width, 2 * len(pieces) * cols * (tok + width), 4
        ),
    )(info, *pieces, weights, *extra)


def decode(info, features, weights, offset, groups, rows, cols):
    _, tok, width = features.shape
    count = weights.shape[2] // cols // 2

    def kernel(info_ref, feat_ref, weight_ref, *out_refs):
        left = feat_ref[0]
        even = info_ref[0] % 2 == 0
        for pair in range(count):
            piece = pair ^ (info_ref[0] // 2)
            for start in range(0, cols, tile):
                low, high = (
                    dot(left, weight_ref[offset, :, base + start : base + start + tile], (1, 0)).astype(
                        jnp.bfloat16
                    )
                    for base in (2 * pair * cols, (2 * pair + 1) * cols)
                )
                sides = (jnp.where(even, high, low), jnp.where(even, low, high))
                for side, product in enumerate(sides):
                    for number, group in enumerate(groups):
                        for place, block in enumerate(group):
                            out_refs[side * len(groups) + number][
                                piece, place, :, start : start + tile
                            ] = product[block * rows : (block + 1) * rows]
    out_shape = [
        jax.ShapeDtypeStruct((count, len(group), rows, cols), jnp.bfloat16) for group in groups
    ] * 2
    result = pl.pallas_call(
        kernel,
        in_specs=[in_smem, in_vmem, in_vmem],
        out_specs=[in_vmem] * len(out_shape),
        out_shape=out_shape,
        name="decode",
        **params(4 * count * tok * cols * width, 4 * count * cols * width, 4),
    )(info, features, weights)
    return result[: len(groups)], result[len(groups) :]


def turned(value, count):
    _, tok, width = value.shape

    def kernel(in_ref, out_ref):
        for piece in range(count):
            for start in range(0, width, tile):
                out_ref[piece, start : start + tile, :] = in_ref[
                    piece, :, start : start + tile
                ].T

    return pl.pallas_call(
        kernel,
        in_specs=[in_vmem],
        out_specs=in_vmem,
        out_shape=jax.ShapeDtypeStruct((count, width, tok), value.dtype),
        name="turned",
        **params(0, 4 * count * tok * width, 4),
    )(value)


def tree_sum(values):
    while len(values) > 1:
        values = [values[i] + values[i + 1] for i in range(0, len(values), 2)]
    return values[0]


def backward_pair(info, rel, offset, own, other, turned_features, dec_weight, feature_grad, dec_grad):
    layers, width, depth = dec_weight.shape
    tok = turned_features.shape[1]
    cols = own[0].shape[2]
    first = feature_grad is None
    extra = [] if first else [feature_grad, dec_grad]
    inputs = [*own, *other]

    def kernel(info_ref, *refs):
        grad_refs = refs[: len(inputs)]
        feat_ref, weight_ref = refs[len(inputs) : len(inputs) + 2]
        out_ref, dec_ref, square_ref, held, sems = refs[-5:]
        columns = span((info_ref[0] ^ rel) // 2, 2 * cols)
        starts = range(0, width, tile)
        copies = [
            pltpu.make_async_copy(
                held.at[slice(start, start + tile)],
                dec_ref.at[offset, slice(start, start + tile), columns],
                sems.at[place],
            )
            for place, start in enumerate(starts)
        ]
        sides, sums = [], []
        for side in (grad_refs[: len(own)], grad_refs[len(own) :]):
            blocks = [ref[i] for ref in side for i in range(ref.shape[0])]
            totals = []
            for block in blocks:
                total = jnp.zeros((8, 128), jnp.float32)
                for row in range(0, block.shape[0], 8):
                    for col in range(0, cols, 128):
                        part = block[row : row + 8, col : col + 128].astype(jnp.float32)
                        total += part * part
                totals.append(total)
            sums.append(tree_sum(totals))
            sides.append(jnp.concatenate(blocks, 0))
        square_ref[...] = tree_sum(sums)

        def products():
            second = info_ref[0] % 2 > 0
            grad = jnp.concatenate(
                [jnp.where(second, sides[1], sides[0]), jnp.where(second, sides[0], sides[1])], 1
            )
            for copy, start in zip(copies, starts):
                here = slice(start, start + tile)
                held[here] = dot(feat_ref[here], grad, (1, 0)).astype(jnp.bfloat16)
                copy.start()
            for start in starts:
                here = slice(start, start + tile)
                product = dot(grad, weight_ref[offset, here, columns], (1, 1))
                if not first:
                    product += refs[len(inputs) + 2][:, here]
                out_ref[:, here] = product

        def nothing():
            held[...] = jnp.zeros_like(held)
            for copy in copies:
                copy.start()
            out_ref[...] = refs[len(inputs) + 2][...]

        if offset == 0:
            products()
        else:
            pl.when(info_ref[1] >= offset)(products)
            pl.when(info_ref[1] < offset)(nothing)
        for copy in copies:
            copy.wait()

    return pl.pallas_call(
        kernel,
        in_specs=[in_smem]
        + [in_vmem] * (len(inputs) + 2)
        + ([] if first else [in_vmem, in_hbm]),
        out_specs=[in_vmem, in_hbm, in_vmem],
        out_shape=[
            jax.ShapeDtypeStruct((tok, width), jnp.float32),
            jax.ShapeDtypeStruct((layers, width, depth), jnp.bfloat16),
            jax.ShapeDtypeStruct((8, 128), jnp.float32),
        ],
        scratch_shapes=[
            pltpu.VMEM((width, 2 * cols), jnp.bfloat16),
            pltpu.SemaphoreType.DMA((width // tile,)),
        ],
        input_output_aliases={} if first else {len(inputs) + 3: 0, len(inputs) + 4: 1},
        name="backward_pair",
        **params(tok * cols, tok * cols, 8),
    )(info, *inputs, turned_features, dec_weight, *extra)


def encoder_grad(info, rels, turned_tokens, features, feature_grad, squares, scale):
    count, cols, tok = turned_tokens[0].shape
    width = features.shape[2]
    pieces = len(turned_tokens) * count

    def kernel(info_ref, *refs):
        token_refs = refs[: len(turned_tokens)]
        mask_ref, grad_ref = refs[len(turned_tokens) : len(turned_tokens) + 2]
        square_refs = refs[len(turned_tokens) + 2 : -6]
        enc_ref, bias_ref, mean_ref, preact, held, sems = refs[-6:]
        mean_ref[...] = scale * jnp.sum(
            tree_sum([ref[...] for ref in square_refs]), (0, 1), keepdims=True
        )
        for start in range(0, width, tile):
            here = slice(start, start + tile)
            kept = jnp.where(mask_ref[1, :, here] > 0.0, grad_ref[:, here], 0.0).astype(jnp.bfloat16)
            preact[:, here] = kept
            bias_ref[:, here] = jnp.sum(kept.astype(jnp.float32), 0, keepdims=True)
        copies = []
        for piece in range(pieces):
            held[piece] = dot(
                token_refs[piece // count][piece % count], preact[...], (1, 0)
            ).astype(jnp.bfloat16)
            copy = pltpu.make_async_copy(
                held.at[piece], enc_ref.at[span(info_ref[0] ^ rels[piece], cols)], sems.at[piece]
            )
            copy.start()
            copies.append(copy)
        for copy in copies:
            copy.wait()

    return pl.pallas_call(
        kernel,
        in_specs=[in_smem] + [in_vmem] * (len(turned_tokens) + 2 + len(squares)),
        out_specs=[in_hbm, in_vmem, in_vmem],
        out_shape=[
            jax.ShapeDtypeStruct((pieces * cols, width), jnp.bfloat16),
            jax.ShapeDtypeStruct((1, width), jnp.float32),
            jax.ShapeDtypeStruct((1, 1), jnp.float32),
        ],
        scratch_shapes=[
            pltpu.VMEM((tok, width), jnp.bfloat16),
            pltpu.VMEM((pieces, cols, width), jnp.bfloat16),
            pltpu.SemaphoreType.DMA((pieces,)),
        ],
        name="encoder_grad",
        **params(
            2 * pieces * tok * cols * width, 2 * pieces * cols * (tok + width) + 6 * tok * width, 10
        ),
    )(info, *turned_tokens, features, feature_grad, *squares)


def add_pair(left, right):
    return (left.astype(jnp.float32) + right.astype(jnp.float32)).astype(jnp.bfloat16)


def on_device(tokens_in, targets, enc_weight, enc_bias, dec_weight):
    layers, width, depth = dec_weight.shape
    feat_count = lax.axis_size("feat")
    sub_count = lax.axis_size("layer") // layers
    position = lax.axis_index("layer")
    layer = position // sub_count
    rows, cols = tokens_in.shape
    tok = feat_count * rows
    bit_count = sub_count.bit_length() - 1
    groups = [list(range(feat_count // 2)), list(range(feat_count // 2, feat_count))]

    info = jnp.stack([position % sub_count, layers - 1 - layer]).astype(jnp.int32)
    real = [layer >= k for k in range(layers)]
    tokens_in, info, *real = lax.optimization_barrier((tokens_in, info, *real))
    enc_weight = pltpu.with_memory_space_constraint(enc_weight, pltpu.HBM)
    dec_weight = pltpu.with_memory_space_constraint(dec_weight, pltpu.HBM)

    order = [rel for pair in range(0, sub_count, 2) for rel in (pair, pair ^ 1)]
    held = {rel: [None] * feat_count for rel in order[::2]}
    held[0] = all_over_feat(tokens_in, 0)
    enc_held, dec_held = fetch(enc_weight, after(dec_weight, held[0][1]))
    for s in range(feat_count):
        known = [0]
        for bit_level in range(bit_count - 1, 0, -1):
            for rel in known:
                value = after(held[rel][s], dec_held) if s > 1 else held[rel][s]
                held[rel ^ 2**bit_level][s] = over_members(value, bit_level)
            known += [rel ^ 2**bit_level for rel in known]
    early = [
        held[rel][s] for rel in order[2::2] for s in range(feat_count) if 2 * s != feat_count
    ]
    tokens = {0: after(jnp.stack(held[0], 0), enc_held, *early)}
    tokens[1] = over_members(tokens[0], 0)
    partial = encode(info, [0, 1], [tokens[0], tokens[1]], enc_held, None, None)
    for rel in order[2::2]:
        tokens[rel] = jnp.stack([after(block, partial) for block in held[rel]], 0)
        tokens[rel ^ 1] = over_members(tokens[rel], 0)
    for rel in order[2:-1]:
        partial = encode(info, [rel], [tokens[rel]], enc_held, partial, None)
    features = encode(info, order[-1:], [tokens[order[-1]]], enc_held, partial, enc_bias[None])

    current, source = {}, features
    for k in reversed(range(layers)):
        sent, kept = decode(info, source, dec_held, k, groups, rows, cols)
        for place in reversed(range(len(groups))):
            current[place, k] = add_pair(kept[place], over_members(sent[place], 0))
        source = after(features, kept[-1])
    turns = sorted(current, reverse=True)
    joined = {}
    for bit_level in range(1, bit_count):
        halves = {}
        for turn, value in current.items():
            split = value.reshape((value.shape[0] // 2, 2) + value.shape[1:])
            halves[turn] = (split[:, 0], split[:, 1])
        if bit_level == bit_count - 1:
            for k in range(1, layers):
                joined[k], sent = halves.pop((0, k))
                sent = to_layer(sent, k, sub_count, real)
                ahead = sent
                halves[0, 0] = (halves[0, 0][0], add_pair(halves[0, 0][1], sent))
        turns = [turn for turn in turns if turn in halves]
        received, operands = [], []
        for turn in turns:
            operand = halves[turn][1]
            if len(received) > 1:
                operand = after(operand, received[-2], operands[-1])
            operands.append(operand)
            received.append(over_members(operand, bit_level))
        for place, turn in enumerate(turns):
            arrived = after(received[place], *operands[place + 1 :][:1])
            if bit_level < bit_count - 1:
                current[turn] = add_pair(halves[turn][0], arrived)
            else:
                current[turn] = (halves[turn][0], arrived)
    blocks, operands = [None] * feat_count, []
    for place in reversed(range(len(groups))):
        total = sum(part.astype(jnp.float32) for part in current[place, 0])
        for k in range(1, layers):
            if place > 0:
                value = add_pair(*current[place, k])
                value = after(value, ahead) if place == 1 else value
                moved = to_layer(value, k, sub_count, real)
            else:
                moved = to_layer(after(joined[k], *operands[:1]), k, sub_count, real)
            total = total + moved.astype(jnp.float32)
        for spot, block in enumerate(groups[place]):
            if block == 0:
                rebuilt = total[0, spot]
            else:
                operands.append(total[0, spot].astype(jnp.bfloat16))
                blocks[block] = over_feat(operands[-1], block)
    for block in reversed(blocks[1:]):
        rebuilt = rebuilt + block.astype(jnp.float32)
    turned_features = turned(source, 1)[0]
    turned_tokens = [
        turned(after(tokens[rel], turned_features).reshape(1, tok, cols), 1) for rel in order
    ]
    recon_error = rebuilt - after(targets, turned_features, *turned_tokens).astype(jnp.float32)
    scaled = (loss_scale / tok * recon_error).astype(jnp.bfloat16)

    blocks = all_over_feat(scaled, 0)
    stages = [[0]]
    for level in range(bit_count - 1, 0, -1):
        known = [rel for stage in stages for rel in stage]
        stages.append([rel ^ 2**level for rel in known])
    spans = [[s] for s in range(min(2, feat_count))]
    spans += [list(range(2, feat_count))] if feat_count > 2 else []
    groups_of = {(0, k): [None] * len(spans) for k in range(layers)}
    early, last = [], len(spans) - 1
    for place, group in enumerate(spans):
        stacked = jnp.stack([blocks[s] for s in group], 0)
        if place == last:
            stacked = after(stacked, groups_of[2, 0][1])
        groups_of[0, 0][place] = stacked
        for k in range(1, layers):
            groups_of[0, k][place] = from_layer(stacked, k, sub_count)
        known = [0]
        for level in range(bit_count - 1, 0, -1):
            for rel in known:
                other = rel ^ 2**level
                for k in range(layers):
                    if k == 0 or place < last:
                        part = over_members(groups_of[rel, k][place], level)
                    else:
                        part = from_layer(groups_of[other, 0][place], k, sub_count)
                    groups_of.setdefault((other, k), [None] * len(spans))[place] = part
            known += [rel ^ 2**level for rel in known]
        if place == last - 1:
            early = [part for parts in groups_of.values() for part in parts if part is not None]
            early.pop()

    feature_grad, dec_grad, squares = None, None, {}
    for k in range(layers):
        for rel in [rel for stage in stages for rel in stage]:
            parts = groups_of[rel, k]
            if feature_grad is None:
                parts = [after(parts[0], groups_of[2, 0][0], groups_of[0, 1][0], groups_of[2, 0][1], groups_of[0, 1][1])] + parts[1:]
            elif (rel > 0 and k == 0) or (rel == 0 and k > 0):
                parts = [after(part, feature_grad) for part in parts]
            if feature_grad is not None:
                if rel > 0 and k == 0:
                    feature_grad = after(feature_grad, groups_of[0, layers - 1][-1])
            feature_grad, dec_grad, squares[k, rel] = backward_pair(
                info,
                rel,
                k,
                parts,
                [over_members(part, 0) for part in parts],
                turned_features,
                dec_held,
                feature_grad,
                dec_grad,
            )
    scale = (tok / loss_scale) ** 2 / (layers * tok * depth)
    enc_grad, bias_grad, mean_square = encoder_grad(
        info,
        order,
        turned_tokens,
        features,
        feature_grad,
        [squares[key] for key in sorted(squares)],
        scale,
    )
    return (recon_error, mean_square[0, 0], enc_grad, bias_grad[0], dec_grad)


def solution(mesh):
    placed = (
        P("feat", "layer"),
        P("feat", "layer"),
        P(None, ("layer", "feat")),
        P(("layer", "feat")),
        P(None, ("layer", "feat"), None),
    )
    return jax.shard_map(
        on_device,
        mesh=mesh,
        in_specs=placed,
        out_specs=(
            P("feat", "layer"),
            P(),
            P(None, ("layer", "feat")),
            P(("layer", "feat")),
            P(None, ("layer", "feat"), None),
        ),
        check_vma=False,
    )
```

```python
import jax
import jax.numpy as jnp
from jax import lax
from jax.experimental import pallas as pl
from jax.experimental.pallas import tpu as pltpu
from jax.sharding import PartitionSpec as P

loss_scale = 64.0
tile = 512
in_vmem = pl.BlockSpec(memory_space=pltpu.VMEM)
in_smem = pl.BlockSpec(memory_space=pltpu.SMEM)
in_hbm = pl.BlockSpec(memory_space=pltpu.HBM)


def over_feat(value, mask):
    pairs = [(source, source ^ mask) for source in range(lax.axis_size("feat"))]
    return lax.ppermute(value, "feat", pairs)


def over_members(value, bit_level):
    mask = 2**bit_level
    pairs = [(source, source ^ mask) for source in range(lax.axis_size("layer"))]
    return lax.ppermute(value, "layer", pairs)


def to_layer(value, offset, sub_count, real):
    count = lax.axis_size("layer")
    pairs = [(p, (p + offset * sub_count) % count) for p in range(count)]
    moved = lax.ppermute(value, "layer", pairs)
    return jnp.where(real[offset], moved, jnp.zeros_like(moved))


def from_layer(value, offset, sub_count):
    count = lax.axis_size("layer")
    pairs = [(p, (p - offset * sub_count) % count) for p in range(count)]
    return lax.ppermute(value, "layer", pairs)


def after(value, *others):
    return lax.optimization_barrier((value, *others))[0]


def all_over_feat(value, turn=0):
    count = lax.axis_size("feat")
    blocks = [value] + [None] * (count - 1)
    for s in (range(1, count) if turn == 0 else reversed(range(1, count))):
        blocks[s] = over_feat(value, s)
    return blocks


def params(flops, bytes_accessed, scratch_mib):
    return dict(
        compiler_params=pltpu.CompilerParams(vmem_limit_bytes=scratch_mib * 1024 * 1024),
        cost_estimate=pl.CostEstimate(
            flops=flops, bytes_accessed=bytes_accessed, transcendentals=0
        ),
    )


def dot(left, right, contract):
    return lax.dot_general(
        left, right, ((contract[:1], contract[1:]), ((), ())), preferred_element_type=jnp.float32
    )


def span(index, size):
    return pl.ds(pl.multiple_of(index * size, size), size)


def fetch(*arrays):
    parts = [(number, start) for number, array in enumerate(arrays) for start in range(4)]

    def kernel(*refs):
        copies = []
        for place, (number, start) in enumerate(parts):
            source, target = refs[number], refs[len(arrays) + number]
            size = source.shape[-2] // 4
            here = (slice(None),) * (len(source.shape) - 2) + (pl.ds(start * size, size),)
            copies.append(
                pltpu.make_async_copy(source.at[here], target.at[here], refs[-1].at[place])
            )
        for copy in copies:
            copy.start()
        for copy in copies:
            copy.wait()

    total = sum(2 * array.size for array in arrays)
    return pl.pallas_call(
        kernel,
        in_specs=[in_hbm] * len(arrays),
        out_specs=[in_vmem] * len(arrays),
        out_shape=[jax.ShapeDtypeStruct(array.shape, array.dtype) for array in arrays],
        scratch_shapes=[pltpu.SemaphoreType.DMA((len(parts),))],
        name="fetch",
        **params(0, total, 14),
    )(*arrays)


def encode(info, rels, pieces, weights, partial, bias):
    feat_count, rows, cols = pieces[0].shape
    tok = feat_count * rows
    width = weights.shape[1]
    extra = [value for value in (partial, bias) if value is not None]

    def kernel(info_ref, *refs):
        piece_refs, weight_ref = refs[: len(pieces)], refs[len(pieces)]
        extra_refs, out_ref = refs[len(pieces) + 1 : -1], refs[-1]
        left = jnp.concatenate([ref[...].reshape(tok, cols) for ref in piece_refs], 1)
        for start in range(0, width, tile):
            here = slice(start, start + tile)
            right = jnp.concatenate(
                [weight_ref[span(info_ref[0] ^ rel, cols), here] for rel in rels], 0
            )
            total = dot(left, right, (1, 0))
            if partial is not None:
                total += extra_refs[0][:, here]
            if bias is None:
                out_ref[:, here] = total
            else:
                pre_act = total + extra_refs[-1][:, here]
                out_ref[0, :, here] = jnp.maximum(pre_act, 0.0).astype(jnp.bfloat16)
                out_ref[1, :, here] = jnp.where(pre_act > 0.0, 1.0, 0.0).astype(jnp.bfloat16)

    if bias is None:
        out_shape = jax.ShapeDtypeStruct((tok, width), jnp.float32)
    else:
        out_shape = jax.ShapeDtypeStruct((2, tok, width), jnp.bfloat16)
    return pl.pallas_call(
        kernel,
        in_specs=[in_smem] + [in_vmem] * (len(pieces) + 1 + len(extra)),
        out_specs=in_vmem,
        out_shape=out_shape,
        name="encode",
        **params(
            2 * len(pieces) * tok * cols * width, 2 * len(pieces) * cols * (tok + width), 4
        ),
    )(info, *pieces, weights, *extra)


def decode(info, features, weights, offset, groups, rows, cols):
    _, tok, width = features.shape
    count = weights.shape[2] // cols // 2

    def kernel(info_ref, feat_ref, weight_ref, *out_refs):
        left = feat_ref[0]
        even = info_ref[0] % 2 == 0
        step = min(tile, cols)
        for pair in range(count):
            piece = pair ^ (info_ref[0] // 2)
            for start in range(0, cols, step):
                low, high = (
                    dot(left, weight_ref[offset, :, base + start : base + start + step], (1, 0)).astype(
                        jnp.bfloat16
                    )
                    for base in (2 * pair * cols, (2 * pair + 1) * cols)
                )
                sides = (jnp.where(even, high, low), jnp.where(even, low, high))
                for side, product in enumerate(sides):
                    for number, group in enumerate(groups):
                        for place, block in enumerate(group):
                            out_refs[side * len(groups) + number][
                                piece, place, :, start : start + step
                            ] = product[block * rows : (block + 1) * rows]
    out_shape = [
        jax.ShapeDtypeStruct((count, len(group), rows, cols), jnp.bfloat16) for group in groups
    ] * 2
    result = pl.pallas_call(
        kernel,
        in_specs=[in_smem, in_vmem, in_vmem],
        out_specs=[in_vmem] * len(out_shape),
        out_shape=out_shape,
        name="decode",
        **params(4 * count * tok * cols * width, 4 * count * cols * width, 4),
    )(info, features, weights)
    return result[: len(groups)], result[len(groups) :]


def turned(value, count):
    _, tok, width = value.shape

    step = min(tile, width)

    def kernel(in_ref, out_ref):
        for piece in range(count):
            for start in range(0, width, step):
                out_ref[piece, start : start + step, :] = in_ref[
                    piece, :, start : start + step
                ].T

    return pl.pallas_call(
        kernel,
        in_specs=[in_vmem],
        out_specs=in_vmem,
        out_shape=jax.ShapeDtypeStruct((count, width, tok), value.dtype),
        name="turned",
        **params(0, 4 * count * tok * width, 4),
    )(value)


def tree_sum(values):
    while len(values) > 1:
        values = [values[i] + values[i + 1] for i in range(0, len(values), 2)]
    return values[0]


def backward_pair(info, rel, offset, own, other, turned_features, dec_weight, feature_grad, dec_grad):
    layers, width, depth = dec_weight.shape
    tok = turned_features.shape[1]
    cols = own[0].shape[2]
    first = feature_grad is None
    extra = [] if first else [feature_grad, dec_grad]
    inputs = [*own, *other]

    def kernel(info_ref, *refs):
        grad_refs = refs[: len(inputs)]
        feat_ref, weight_ref = refs[len(inputs) : len(inputs) + 2]
        out_ref, dec_ref, square_ref, held, sems = refs[-5:]
        columns = span((info_ref[0] ^ rel) // 2, 2 * cols)
        starts = range(0, width, tile)
        copies = [
            pltpu.make_async_copy(
                held.at[slice(start, start + tile)],
                dec_ref.at[offset, slice(start, start + tile), columns],
                sems.at[place],
            )
            for place, start in enumerate(starts)
        ]
        sides, sums = [], []
        for side in (grad_refs[: len(own)], grad_refs[len(own) :]):
            blocks = [ref[i] for ref in side for i in range(ref.shape[0])]
            totals = []
            for block in blocks:
                total = jnp.zeros((8, 128), jnp.float32)
                for row in range(0, block.shape[0], 8):
                    for col in range(0, cols, 128):
                        part = block[row : row + 8, col : col + 128].astype(jnp.float32)
                        total += part * part
                totals.append(total)
            sums.append(tree_sum(totals))
            sides.append(jnp.concatenate(blocks, 0))
        square_ref[...] = tree_sum(sums)

        def products():
            second = info_ref[0] % 2 > 0
            grad = jnp.concatenate(
                [jnp.where(second, sides[1], sides[0]), jnp.where(second, sides[0], sides[1])], 1
            )
            for copy, start in zip(copies, starts):
                here = slice(start, start + tile)
                held[here] = dot(feat_ref[here], grad, (1, 0)).astype(jnp.bfloat16)
                copy.start()
            for start in starts:
                here = slice(start, start + tile)
                product = dot(grad, weight_ref[offset, here, columns], (1, 1))
                if not first:
                    product += refs[len(inputs) + 2][:, here]
                out_ref[:, here] = product

        def nothing():
            held[...] = jnp.zeros_like(held)
            for copy in copies:
                copy.start()
            out_ref[...] = refs[len(inputs) + 2][...]

        if offset == 0:
            products()
        else:
            pl.when(info_ref[1] >= offset)(products)
            pl.when(info_ref[1] < offset)(nothing)
        for copy in copies:
            copy.wait()

    return pl.pallas_call(
        kernel,
        in_specs=[in_smem]
        + [in_vmem] * (len(inputs) + 2)
        + ([] if first else [in_vmem, in_hbm]),
        out_specs=[in_vmem, in_hbm, in_vmem],
        out_shape=[
            jax.ShapeDtypeStruct((tok, width), jnp.float32),
            jax.ShapeDtypeStruct((layers, width, depth), jnp.bfloat16),
            jax.ShapeDtypeStruct((8, 128), jnp.float32),
        ],
        scratch_shapes=[
            pltpu.VMEM((width, 2 * cols), jnp.bfloat16),
            pltpu.SemaphoreType.DMA((width // tile,)),
        ],
        input_output_aliases={} if first else {len(inputs) + 3: 0, len(inputs) + 4: 1},
        name="backward_pair",
        **params(tok * cols, tok * cols, 8),
    )(info, *inputs, turned_features, dec_weight, *extra)


def encoder_grad(info, rels, turned_tokens, features, feature_grad, squares, scale):
    count, cols, tok = turned_tokens[0].shape
    width = features.shape[2]
    pieces = len(turned_tokens) * count

    def kernel(info_ref, *refs):
        token_refs = refs[: len(turned_tokens)]
        mask_ref, grad_ref = refs[len(turned_tokens) : len(turned_tokens) + 2]
        square_refs = refs[len(turned_tokens) + 2 : -6]
        enc_ref, bias_ref, mean_ref, preact, held, sems = refs[-6:]
        mean_ref[...] = scale * jnp.sum(
            tree_sum([ref[...] for ref in square_refs]), (0, 1), keepdims=True
        )
        for start in range(0, width, tile):
            here = slice(start, start + tile)
            kept = jnp.where(mask_ref[1, :, here] > 0.0, grad_ref[:, here], 0.0).astype(jnp.bfloat16)
            preact[:, here] = kept
            bias_ref[:, here] = jnp.sum(kept.astype(jnp.float32), 0, keepdims=True)
        copies = []
        for piece in range(pieces):
            held[piece] = dot(
                token_refs[piece // count][piece % count], preact[...], (1, 0)
            ).astype(jnp.bfloat16)
            size = cols // 4
            for part in range(4):
                row = (info_ref[0] ^ rels[piece]) * 4 + part
                copy = pltpu.make_async_copy(
                    held.at[piece, pl.ds(part * size, size)],
                    enc_ref.at[span(row, size)],
                    sems.at[4 * piece + part],
                )
                copy.start()
                copies.append(copy)
        for copy in copies:
            copy.wait()

    return pl.pallas_call(
        kernel,
        in_specs=[in_smem] + [in_vmem] * (len(turned_tokens) + 2 + len(squares)),
        out_specs=[in_hbm, in_vmem, in_vmem],
        out_shape=[
            jax.ShapeDtypeStruct((pieces * cols, width), jnp.bfloat16),
            jax.ShapeDtypeStruct((1, width), jnp.float32),
            jax.ShapeDtypeStruct((1, 1), jnp.float32),
        ],
        scratch_shapes=[
            pltpu.VMEM((tok, width), jnp.bfloat16),
            pltpu.VMEM((pieces, cols, width), jnp.bfloat16),
            pltpu.SemaphoreType.DMA((4 * pieces,)),
        ],
        name="encoder_grad",
        **params(
            2 * pieces * tok * cols * width, 2 * pieces * cols * (tok + width) + 6 * tok * width, 10
        ),
    )(info, *turned_tokens, features, feature_grad, *squares)


def add_pair(left, right):
    return (left.astype(jnp.float32) + right.astype(jnp.float32)).astype(jnp.bfloat16)


def on_device(tokens_in, targets, enc_weight, enc_bias, dec_weight):
    layers, width, depth = dec_weight.shape
    feat_count = lax.axis_size("feat")
    sub_count = lax.axis_size("layer") // layers
    position = lax.axis_index("layer")
    layer = position // sub_count
    rows, cols = tokens_in.shape
    tok = feat_count * rows
    bit_count = sub_count.bit_length() - 1
    groups = [list(range(feat_count // 2)), list(range(feat_count // 2, feat_count))]

    info = jnp.stack([position % sub_count, layers - 1 - layer]).astype(jnp.int32)
    real = [layer >= k for k in range(layers)]
    tokens_in, info, *real = lax.optimization_barrier((tokens_in, info, *real))
    enc_weight = pltpu.with_memory_space_constraint(enc_weight, pltpu.HBM)
    dec_weight = pltpu.with_memory_space_constraint(dec_weight, pltpu.HBM)

    order = [rel for pair in range(0, sub_count, 2) for rel in (pair, pair ^ 1)]
    held = {rel: [None] * feat_count for rel in order[::2]}
    held[0] = all_over_feat(tokens_in, 0)
    enc_held, dec_held = fetch(enc_weight, after(dec_weight, held[0][1]))
    for s in range(feat_count):
        known = [0]
        for bit_level in range(bit_count - 1, 0, -1):
            for rel in known:
                value = after(held[rel][s], dec_held) if s > 1 else held[rel][s]
                held[rel ^ 2**bit_level][s] = over_members(value, bit_level)
            known += [rel ^ 2**bit_level for rel in known]
    early = [
        held[rel][s] for rel in order[2::2] for s in range(feat_count) if 2 * s != feat_count
    ]
    tokens = {0: after(jnp.stack(held[0], 0), enc_held, *early)}
    tokens[1] = over_members(tokens[0], 0)
    partial = encode(info, [0, 1], [tokens[0], tokens[1]], enc_held, None, None)
    for rel in order[2::2]:
        tokens[rel] = jnp.stack([after(block, partial) for block in held[rel]], 0)
        tokens[rel ^ 1] = over_members(tokens[rel], 0)
    for rel in order[2:-1]:
        partial = encode(info, [rel], [tokens[rel]], enc_held, partial, None)
    features = encode(info, order[-1:], [tokens[order[-1]]], enc_held, partial, enc_bias[None])

    current, source = {}, features
    for k in reversed(range(layers)):
        sent, kept = decode(info, source, dec_held, k, groups, rows, cols)
        for place in reversed(range(len(groups))):
            current[place, k] = add_pair(kept[place], over_members(sent[place], 0))
        source = after(features, kept[-1])
    turns = sorted(current, reverse=True)
    joined = {}
    for bit_level in range(1, bit_count):
        halves = {}
        for turn, value in current.items():
            split = value.reshape((value.shape[0] // 2, 2) + value.shape[1:])
            halves[turn] = (split[:, 0], split[:, 1])
        if bit_level == bit_count - 1:
            for k in range(1, layers):
                joined[k], sent = halves.pop((0, k))
                sent = to_layer(sent, k, sub_count, real)
                ahead = sent
                halves[0, 0] = (halves[0, 0][0], add_pair(halves[0, 0][1], sent))
        turns = [turn for turn in turns if turn in halves]
        received, operands = [], []
        for turn in turns:
            operand = halves[turn][1]
            if len(received) > 1:
                operand = after(operand, received[-2], operands[-1])
            operands.append(operand)
            received.append(over_members(operand, bit_level))
        for place, turn in enumerate(turns):
            arrived = after(received[place], *operands[place + 1 :][:1])
            if bit_level < bit_count - 1:
                current[turn] = add_pair(halves[turn][0], arrived)
            else:
                current[turn] = (halves[turn][0], arrived)
    blocks, operands = [None] * feat_count, []
    for place in reversed(range(len(groups))):
        total = sum(part.astype(jnp.float32) for part in current[place, 0])
        for k in range(1, layers):
            if place > 0:
                value = add_pair(*current[place, k])
                value = after(value, ahead) if place == 1 else value
                moved = to_layer(value, k, sub_count, real)
            else:
                moved = to_layer(after(joined[k], *operands[:1]), k, sub_count, real)
            total = total + moved.astype(jnp.float32)
        for spot, block in enumerate(groups[place]):
            if block == 0:
                rebuilt = total[0, spot]
            else:
                operands.append(total[0, spot].astype(jnp.bfloat16))
                blocks[block] = over_feat(operands[-1], block)
    for block in reversed(blocks[1:]):
        rebuilt = rebuilt + block.astype(jnp.float32)
    turned_features = turned(source, 1)[0]
    turned_tokens = [
        turned(after(tokens[rel], turned_features).reshape(1, tok, cols), 1) for rel in order
    ]
    recon_error = rebuilt - after(targets, turned_features, *turned_tokens).astype(jnp.float32)
    scaled = (loss_scale / tok * recon_error).astype(jnp.bfloat16)

    blocks = all_over_feat(scaled, 0)
    stages = [[0]]
    for level in range(bit_count - 1, 0, -1):
        known = [rel for stage in stages for rel in stage]
        stages.append([rel ^ 2**level for rel in known])
    spans = [[s] for s in range(min(2, feat_count))]
    spans += [list(range(2, feat_count))] if feat_count > 2 else []
    groups_of = {(0, k): [None] * len(spans) for k in range(layers)}
    early, last = [], len(spans) - 1
    for place, group in enumerate(spans):
        stacked = jnp.stack([blocks[s] for s in group], 0)
        groups_of[0, 0][place] = stacked
        for k in range(1, layers):
            groups_of[0, k][place] = from_layer(stacked, k, sub_count)
        known = [0]
        for level in range(bit_count - 1, 0, -1):
            for rel in known:
                other = rel ^ 2**level
                for k in range(layers):
                    if k == 0 or place < last:
                        part = over_members(groups_of[rel, k][place], level)
                    else:
                        part = from_layer(groups_of[other, 0][place], k, sub_count)
                    groups_of.setdefault((other, k), [None] * len(spans))[place] = part
            known += [rel ^ 2**level for rel in known]
        if place == last - 1:
            early = [part for parts in groups_of.values() for part in parts if part is not None]
            early.pop()

    feature_grad, dec_grad, squares = None, None, {}
    for k in range(layers):
        for rel in [rel for stage in stages for rel in stage]:
            parts = groups_of[rel, k]
            if feature_grad is None:
                parts = [after(parts[0], groups_of[2, 0][0], groups_of[0, 1][0], groups_of[2, 1][0], groups_of[2, 0][1], groups_of[0, 1][1])] + parts[1:]
            elif (rel > 0 and k == 0) or (rel > 0 and k > 0):
                parts = [after(part, feature_grad) for part in parts]
            feature_grad, dec_grad, squares[k, rel] = backward_pair(
                info,
                rel,
                k,
                parts,
                [over_members(part, 0) for part in parts],
                turned_features,
                dec_held,
                feature_grad,
                dec_grad,
            )
    scale = (tok / loss_scale) ** 2 / (layers * tok * depth)
    enc_grad, bias_grad, mean_square = encoder_grad(
        info,
        order,
        turned_tokens,
        features,
        feature_grad,
        [squares[key] for key in sorted(squares)],
        scale,
    )
    return (recon_error, mean_square[0, 0], enc_grad, bias_grad[0], dec_grad)


def solution(mesh):
    placed = (
        P("feat", "layer"),
        P("feat", "layer"),
        P(None, ("layer", "feat")),
        P(("layer", "feat")),
        P(None, ("layer", "feat"), None),
    )
    return jax.shard_map(
        on_device,
        mesh=mesh,
        in_specs=placed,
        out_specs=(
            P("feat", "layer"),
            P(),
            P(None, ("layer", "feat")),
            P(("layer", "feat")),
            P(None, ("layer", "feat"), None),
        ),
        check_vma=False,
    )
```

```python
import jax
import jax.numpy as jnp
from jax import lax
from jax.experimental import pallas as pl
from jax.experimental.pallas import tpu as pltpu
from jax.sharding import PartitionSpec as P

loss_scale = 64.0
tile = 512
in_vmem = pl.BlockSpec(memory_space=pltpu.VMEM)
in_smem = pl.BlockSpec(memory_space=pltpu.SMEM)
in_hbm = pl.BlockSpec(memory_space=pltpu.HBM)


def over_feat(value, mask):
    pairs = [(source, source ^ mask) for source in range(lax.axis_size("feat"))]
    return lax.ppermute(value, "feat", pairs)


def over_members(value, bit_level):
    mask = 2**bit_level
    pairs = [(source, source ^ mask) for source in range(lax.axis_size("layer"))]
    return lax.ppermute(value, "layer", pairs)


def to_layer(value, offset, sub_count, real):
    count = lax.axis_size("layer")
    pairs = [(p, (p + offset * sub_count) % count) for p in range(count)]
    moved = lax.ppermute(value, "layer", pairs)
    return jnp.where(real[offset], moved, jnp.zeros_like(moved))


def from_layer(value, offset, sub_count):
    count = lax.axis_size("layer")
    pairs = [(p, (p - offset * sub_count) % count) for p in range(count)]
    return lax.ppermute(value, "layer", pairs)


def after(value, *others):
    return lax.optimization_barrier((value, *others))[0]


def all_over_feat(value, turn=0):
    count = lax.axis_size("feat")
    blocks = [value] + [None] * (count - 1)
    for s in (range(1, count) if turn == 0 else reversed(range(1, count))):
        blocks[s] = over_feat(value, s)
    return blocks


def params(flops, bytes_accessed, scratch_mib):
    return dict(
        compiler_params=pltpu.CompilerParams(vmem_limit_bytes=scratch_mib * 1024 * 1024),
        cost_estimate=pl.CostEstimate(
            flops=flops, bytes_accessed=bytes_accessed, transcendentals=0
        ),
    )


def dot(left, right, contract):
    return lax.dot_general(
        left, right, ((contract[:1], contract[1:]), ((), ())), preferred_element_type=jnp.float32
    )


def span(index, size):
    return pl.ds(pl.multiple_of(index * size, size), size)


def fetch(*arrays):
    parts = [(number, start) for number, array in enumerate(arrays) for start in range(4)]

    def kernel(*refs):
        copies = []
        for place, (number, start) in enumerate(parts):
            source, target = refs[number], refs[len(arrays) + number]
            size = source.shape[-2] // 4
            here = (slice(None),) * (len(source.shape) - 2) + (pl.ds(start * size, size),)
            copies.append(
                pltpu.make_async_copy(source.at[here], target.at[here], refs[-1].at[place])
            )
        for copy in copies:
            copy.start()
        for copy in copies:
            copy.wait()

    total = sum(2 * array.size for array in arrays)
    return pl.pallas_call(
        kernel,
        in_specs=[in_hbm] * len(arrays),
        out_specs=[in_vmem] * len(arrays),
        out_shape=[jax.ShapeDtypeStruct(array.shape, array.dtype) for array in arrays],
        scratch_shapes=[pltpu.SemaphoreType.DMA((len(parts),))],
        name="fetch",
        **params(0, total, 14),
    )(*arrays)


def encode(info, rels, pieces, weights, partial, bias):
    feat_count, rows, cols = pieces[0].shape
    tok = feat_count * rows
    width = weights.shape[1]
    extra = [value for value in (partial, bias) if value is not None]

    def kernel(info_ref, *refs):
        piece_refs, weight_ref = refs[: len(pieces)], refs[len(pieces)]
        extra_refs, out_ref = refs[len(pieces) + 1 : -1], refs[-1]
        left = jnp.concatenate([ref[...].reshape(tok, cols) for ref in piece_refs], 1)
        for start in range(0, width, tile):
            here = slice(start, start + tile)
            right = jnp.concatenate(
                [weight_ref[span(info_ref[0] ^ rel, cols), here] for rel in rels], 0
            )
            total = dot(left, right, (1, 0))
            if partial is not None:
                total += extra_refs[0][:, here]
            if bias is None:
                out_ref[:, here] = total
            else:
                pre_act = total + extra_refs[-1][:, here]
                out_ref[0, :, here] = jnp.maximum(pre_act, 0.0).astype(jnp.bfloat16)
                out_ref[1, :, here] = jnp.where(pre_act > 0.0, 1.0, 0.0).astype(jnp.bfloat16)

    if bias is None:
        out_shape = jax.ShapeDtypeStruct((tok, width), jnp.float32)
    else:
        out_shape = jax.ShapeDtypeStruct((2, tok, width), jnp.bfloat16)
    return pl.pallas_call(
        kernel,
        in_specs=[in_smem] + [in_vmem] * (len(pieces) + 1 + len(extra)),
        out_specs=in_vmem,
        out_shape=out_shape,
        name="encode",
        **params(
            2 * len(pieces) * tok * cols * width, 2 * len(pieces) * cols * (tok + width), 4
        ),
    )(info, *pieces, weights, *extra)


def decode(info, features, weights, offset, groups, rows, cols):
    _, tok, width = features.shape
    count = weights.shape[2] // cols // 2

    def kernel(info_ref, feat_ref, weight_ref, *out_refs):
        left = feat_ref[0]
        even = info_ref[0] % 2 == 0
        step = min(tile, cols)
        for pair in range(count):
            piece = pair ^ (info_ref[0] // 2)
            for start in range(0, cols, step):
                low, high = (
                    dot(left, weight_ref[offset, :, base + start : base + start + step], (1, 0)).astype(
                        jnp.bfloat16
                    )
                    for base in (2 * pair * cols, (2 * pair + 1) * cols)
                )
                sides = (jnp.where(even, high, low), jnp.where(even, low, high))
                for side, product in enumerate(sides):
                    for number, group in enumerate(groups):
                        for place, block in enumerate(group):
                            out_refs[side * len(groups) + number][
                                piece, place, :, start : start + step
                            ] = product[block * rows : (block + 1) * rows]
    out_shape = [
        jax.ShapeDtypeStruct((count, len(group), rows, cols), jnp.bfloat16) for group in groups
    ] * 2
    result = pl.pallas_call(
        kernel,
        in_specs=[in_smem, in_vmem, in_vmem],
        out_specs=[in_vmem] * len(out_shape),
        out_shape=out_shape,
        name="decode",
        **params(4 * count * tok * cols * width, 4 * count * cols * width, 4),
    )(info, features, weights)
    return result[: len(groups)], result[len(groups) :]


def turned(value, count):
    _, tok, width = value.shape

    step = min(tile, width)

    def kernel(in_ref, out_ref):
        for piece in range(count):
            for start in range(0, width, step):
                out_ref[piece, start : start + step, :] = in_ref[
                    piece, :, start : start + step
                ].T

    return pl.pallas_call(
        kernel,
        in_specs=[in_vmem],
        out_specs=in_vmem,
        out_shape=jax.ShapeDtypeStruct((count, width, tok), value.dtype),
        name="turned",
        **params(0, 4 * count * tok * width, 4),
    )(value)


def tree_sum(values):
    while len(values) > 1:
        values = [values[i] + values[i + 1] for i in range(0, len(values), 2)]
    return values[0]


def backward_pair(info, rel, offset, own, other, turned_features, dec_weight, feature_grad, dec_grad):
    layers, width, depth = dec_weight.shape
    tok = turned_features.shape[1]
    cols = own[0].shape[2]
    first = feature_grad is None
    extra = [] if first else [feature_grad, dec_grad]
    inputs = [*own, *other]

    def kernel(info_ref, *refs):
        grad_refs = refs[: len(inputs)]
        feat_ref, weight_ref = refs[len(inputs) : len(inputs) + 2]
        out_ref, dec_ref, square_ref, held, sems = refs[-5:]
        columns = span((info_ref[0] ^ rel) // 2, 2 * cols)
        starts = range(0, width, tile)
        copies = [
            pltpu.make_async_copy(
                held.at[slice(start, start + tile)],
                dec_ref.at[offset, slice(start, start + tile), columns],
                sems.at[place],
            )
            for place, start in enumerate(starts)
        ]
        sides, sums = [], []
        for side in (grad_refs[: len(own)], grad_refs[len(own) :]):
            blocks = [ref[i] for ref in side for i in range(ref.shape[0])]
            totals = []
            for block in blocks:
                total = jnp.zeros((8, 128), jnp.float32)
                for row in range(0, block.shape[0], 8):
                    for col in range(0, cols, 128):
                        part = block[row : row + 8, col : col + 128].astype(jnp.float32)
                        total += part * part
                totals.append(total)
            sums.append(tree_sum(totals))
            sides.append(jnp.concatenate(blocks, 0))
        square_ref[...] = tree_sum(sums)

        def products():
            second = info_ref[0] % 2 > 0
            grad = jnp.concatenate(
                [jnp.where(second, sides[1], sides[0]), jnp.where(second, sides[0], sides[1])], 1
            )
            for copy, start in zip(copies, starts):
                here = slice(start, start + tile)
                held[here] = dot(feat_ref[here], grad, (1, 0)).astype(jnp.bfloat16)
                copy.start()
            for start in starts:
                here = slice(start, start + tile)
                product = dot(grad, weight_ref[offset, here, columns], (1, 1))
                if not first:
                    product += refs[len(inputs) + 2][:, here]
                out_ref[:, here] = product

        def nothing():
            held[...] = jnp.zeros_like(held)
            for copy in copies:
                copy.start()
            out_ref[...] = refs[len(inputs) + 2][...]

        if offset == 0:
            products()
        else:
            pl.when(info_ref[1] >= offset)(products)
            pl.when(info_ref[1] < offset)(nothing)
        for copy in copies:
            copy.wait()

    return pl.pallas_call(
        kernel,
        in_specs=[in_smem]
        + [in_vmem] * (len(inputs) + 2)
        + ([] if first else [in_vmem, in_hbm]),
        out_specs=[in_vmem, in_hbm, in_vmem],
        out_shape=[
            jax.ShapeDtypeStruct((tok, width), jnp.float32),
            jax.ShapeDtypeStruct((layers, width, depth), jnp.bfloat16),
            jax.ShapeDtypeStruct((8, 128), jnp.float32),
        ],
        scratch_shapes=[
            pltpu.VMEM((width, 2 * cols), jnp.bfloat16),
            pltpu.SemaphoreType.DMA((width // tile,)),
        ],
        input_output_aliases={} if first else {len(inputs) + 3: 0, len(inputs) + 4: 1},
        name="backward_pair",
        **params(tok * cols, tok * cols, 8),
    )(info, *inputs, turned_features, dec_weight, *extra)


def encoder_grad(info, rels, turned_tokens, features, feature_grad, squares, scale):
    count, cols, tok = turned_tokens[0].shape
    width = features.shape[2]
    pieces = len(turned_tokens) * count

    def kernel(info_ref, *refs):
        token_refs = refs[: len(turned_tokens)]
        mask_ref, grad_ref = refs[len(turned_tokens) : len(turned_tokens) + 2]
        square_refs = refs[len(turned_tokens) + 2 : -6]
        enc_ref, bias_ref, mean_ref, preact, held, sems = refs[-6:]
        mean_ref[...] = scale * jnp.sum(
            tree_sum([ref[...] for ref in square_refs]), (0, 1), keepdims=True
        )
        copies = []
        for start in range(0, width, 256):
            here = slice(start, start + 256)
            kept = jnp.where(mask_ref[1, :, here] > 0.0, grad_ref[:, here], 0.0).astype(jnp.bfloat16)
            preact[:, here] = kept
            held[0, :, here] = dot(token_refs[0][0], kept, (1, 0)).astype(jnp.bfloat16)
            bias_ref[:, here] = jnp.sum(kept.astype(jnp.float32), 0, keepdims=True)
        for piece in range(pieces):
            if piece > 0:
                held[piece] = dot(
                    token_refs[piece // count][piece % count], preact[...], (1, 0)
                ).astype(jnp.bfloat16)
            copy = pltpu.make_async_copy(
                held.at[piece], enc_ref.at[span(info_ref[0] ^ rels[piece], cols)], sems.at[piece]
            )
            copy.start()
            copies.append(copy)
        for copy in copies:
            copy.wait()

    return pl.pallas_call(
        kernel,
        in_specs=[in_smem] + [in_vmem] * (len(turned_tokens) + 2 + len(squares)),
        out_specs=[in_hbm, in_vmem, in_vmem],
        out_shape=[
            jax.ShapeDtypeStruct((pieces * cols, width), jnp.bfloat16),
            jax.ShapeDtypeStruct((1, width), jnp.float32),
            jax.ShapeDtypeStruct((1, 1), jnp.float32),
        ],
        scratch_shapes=[
            pltpu.VMEM((tok, width), jnp.bfloat16),
            pltpu.VMEM((pieces, cols, width), jnp.bfloat16),
            pltpu.SemaphoreType.DMA((pieces,)),
        ],
        name="encoder_grad",
        **params(
            2 * pieces * tok * cols * width, 2 * pieces * cols * (tok + width) + 6 * tok * width, 10
        ),
    )(info, *turned_tokens, features, feature_grad, *squares)


def add_pair(left, right):
    return (left.astype(jnp.float32) + right.astype(jnp.float32)).astype(jnp.bfloat16)


def on_device(tokens_in, targets, enc_weight, enc_bias, dec_weight):
    layers, width, depth = dec_weight.shape
    feat_count = lax.axis_size("feat")
    sub_count = lax.axis_size("layer") // layers
    position = lax.axis_index("layer")
    layer = position // sub_count
    rows, cols = tokens_in.shape
    tok = feat_count * rows
    bit_count = sub_count.bit_length() - 1
    groups = [list(range(feat_count // 2)), list(range(feat_count // 2, feat_count))]

    info = jnp.stack([position % sub_count, layers - 1 - layer]).astype(jnp.int32)
    real = [layer >= k for k in range(layers)]
    tokens_in, info, *real = lax.optimization_barrier((tokens_in, info, *real))
    enc_weight = pltpu.with_memory_space_constraint(enc_weight, pltpu.HBM)
    dec_weight = pltpu.with_memory_space_constraint(dec_weight, pltpu.HBM)

    order = [rel for pair in range(0, sub_count, 2) for rel in (pair, pair ^ 1)]
    held = {rel: [None] * feat_count for rel in order[::2]}
    held[0] = all_over_feat(tokens_in, 0)
    enc_held, dec_held = fetch(enc_weight, after(dec_weight, held[0][1]))
    for s in range(feat_count):
        known = [0]
        for bit_level in range(bit_count - 1, 0, -1):
            for rel in known:
                value = after(held[rel][s], dec_held) if s > 1 else held[rel][s]
                held[rel ^ 2**bit_level][s] = over_members(value, bit_level)
            known += [rel ^ 2**bit_level for rel in known]
    early = [
        held[rel][s] for rel in order[2::2] for s in range(feat_count) if 2 * s != feat_count
    ]
    tokens = {0: after(jnp.stack(held[0], 0), enc_held, *early)}
    tokens[1] = over_members(tokens[0], 0)
    partial = encode(info, [0, 1], [tokens[0], tokens[1]], enc_held, None, None)
    for rel in order[2::2]:
        tokens[rel] = jnp.stack([after(block, partial) for block in held[rel]], 0)
        tokens[rel ^ 1] = over_members(tokens[rel], 0)
    for rel in order[2:-1]:
        partial = encode(info, [rel], [tokens[rel]], enc_held, partial, None)
    features = encode(info, order[-1:], [tokens[order[-1]]], enc_held, partial, enc_bias[None])

    current, source = {}, features
    for k in reversed(range(layers)):
        sent, kept = decode(info, source, dec_held, k, groups, rows, cols)
        for place in reversed(range(len(groups))):
            current[place, k] = add_pair(kept[place], over_members(sent[place], 0))
        source = after(features, kept[-1])
    turns = sorted(current, reverse=True)
    joined = {}
    for bit_level in range(1, bit_count):
        halves = {}
        for turn, value in current.items():
            split = value.reshape((value.shape[0] // 2, 2) + value.shape[1:])
            halves[turn] = (split[:, 0], split[:, 1])
        if bit_level == bit_count - 1:
            for k in range(1, layers):
                joined[k], sent = halves.pop((0, k))
                sent = to_layer(sent, k, sub_count, real)
                ahead = sent
                halves[0, 0] = (halves[0, 0][0], add_pair(halves[0, 0][1], sent))
        turns = [turn for turn in turns if turn in halves]
        received, operands = [], []
        for turn in turns:
            operand = halves[turn][1]
            if len(received) > 1:
                operand = after(operand, received[-2], operands[-1])
            operands.append(operand)
            received.append(over_members(operand, bit_level))
        for place, turn in enumerate(turns):
            arrived = after(received[place], *operands[place + 1 :][:1])
            if bit_level < bit_count - 1:
                current[turn] = add_pair(halves[turn][0], arrived)
            else:
                current[turn] = (halves[turn][0], arrived)
    blocks, operands = [None] * feat_count, []
    for place in reversed(range(len(groups))):
        total = sum(part.astype(jnp.float32) for part in current[place, 0])
        for k in range(1, layers):
            if place > 0:
                value = add_pair(*current[place, k])
                value = after(value, ahead) if place == 1 else value
                moved = to_layer(value, k, sub_count, real)
            else:
                moved = to_layer(after(joined[k], *operands[:1]), k, sub_count, real)
            total = total + moved.astype(jnp.float32)
        for spot, block in enumerate(groups[place]):
            if block == 0:
                rebuilt = total[0, spot]
            else:
                operands.append(total[0, spot].astype(jnp.bfloat16))
                blocks[block] = over_feat(operands[-1], block)
    for block in reversed(blocks[1:]):
        rebuilt = rebuilt + block.astype(jnp.float32)
    turned_features = turned(source, 1)[0]
    turned_tokens = [
        turned(after(tokens[rel], turned_features).reshape(1, tok, cols), 1) for rel in order
    ]
    recon_error = rebuilt - after(targets, turned_features, *turned_tokens).astype(jnp.float32)
    scaled = (loss_scale / tok * recon_error).astype(jnp.bfloat16)

    blocks = all_over_feat(scaled, 0)
    stages = [[0]]
    for level in range(bit_count - 1, 0, -1):
        known = [rel for stage in stages for rel in stage]
        stages.append([rel ^ 2**level for rel in known])
    spans = [[s] for s in range(min(2, feat_count))]
    spans += [list(range(2, feat_count))] if feat_count > 2 else []
    groups_of = {(0, k): [None] * len(spans) for k in range(layers)}
    early, last = [], len(spans) - 1
    for place, group in enumerate(spans):
        stacked = jnp.stack([blocks[s] for s in group], 0)
        if place == last:
            stacked = after(stacked, groups_of[2, 0][1])
        groups_of[0, 0][place] = stacked
        for k in range(1, layers):
            groups_of[0, k][place] = from_layer(stacked, k, sub_count)
        known = [0]
        for level in range(bit_count - 1, 0, -1):
            for rel in known:
                other = rel ^ 2**level
                for k in range(layers):
                    if k == 0 or place < last:
                        part = over_members(groups_of[rel, k][place], level)
                    else:
                        part = from_layer(groups_of[other, 0][place], k, sub_count)
                    groups_of.setdefault((other, k), [None] * len(spans))[place] = part
            known += [rel ^ 2**level for rel in known]
        if place == last - 1:
            early = [part for parts in groups_of.values() for part in parts if part is not None]
            early.pop()

    feature_grad, dec_grad, squares = None, None, {}
    for k in range(layers):
        for rel in [rel for stage in stages for rel in stage]:
            parts = groups_of[rel, k]
            if feature_grad is None:
                parts = [after(parts[0], groups_of[2, 0][0], groups_of[0, 1][0], groups_of[2, 1][0], groups_of[0, 1][1])] + parts[1:]
            elif (rel > 0 and k == 0) or (rel > 0 and k > 0):
                parts = [after(part, feature_grad) for part in parts]
            if feature_grad is not None:
                if rel > 0 and k == 0:
                    feature_grad = after(feature_grad, groups_of[2, layers - 1][0], groups_of[2, layers - 1][1])
            feature_grad, dec_grad, squares[k, rel] = backward_pair(
                info,
                rel,
                k,
                parts,
                [over_members(part, 0) for part in parts],
                turned_features,
                dec_held,
                feature_grad,
                dec_grad,
            )
    scale = (tok / loss_scale) ** 2 / (layers * tok * depth)
    enc_grad, bias_grad, mean_square = encoder_grad(
        info,
        order,
        turned_tokens,
        features,
        feature_grad,
        [squares[key] for key in sorted(squares)],
        scale,
    )
    return (recon_error, mean_square[0, 0], enc_grad, bias_grad[0], dec_grad)


def solution(mesh):
    placed = (
        P("feat", "layer"),
        P("feat", "layer"),
        P(None, ("layer", "feat")),
        P(("layer", "feat")),
        P(None, ("layer", "feat"), None),
    )
    return jax.shard_map(
        on_device,
        mesh=mesh,
        in_specs=placed,
        out_specs=(
            P("feat", "layer"),
            P(),
            P(None, ("layer", "feat")),
            P(("layer", "feat")),
            P(None, ("layer", "feat"), None),
        ),
        check_vma=False,
    )
```

```python
import jax
import jax.numpy as jnp
from jax import lax
from jax.experimental import pallas as pl
from jax.experimental.pallas import tpu as pltpu
from jax.sharding import PartitionSpec as P

loss_scale = 64.0
tile = 512
in_vmem = pl.BlockSpec(memory_space=pltpu.VMEM)
in_smem = pl.BlockSpec(memory_space=pltpu.SMEM)
in_hbm = pl.BlockSpec(memory_space=pltpu.HBM)


def over_feat(value, mask):
    pairs = [(source, source ^ mask) for source in range(lax.axis_size("feat"))]
    return lax.ppermute(value, "feat", pairs)


def over_members(value, bit_level):
    mask = 2**bit_level
    pairs = [(source, source ^ mask) for source in range(lax.axis_size("layer"))]
    return lax.ppermute(value, "layer", pairs)


def to_layer(value, offset, sub_count, real):
    count = lax.axis_size("layer")
    pairs = [(p, (p + offset * sub_count) % count) for p in range(count)]
    moved = lax.ppermute(value, "layer", pairs)
    return jnp.where(real[offset], moved, jnp.zeros_like(moved))


def from_layer(value, offset, sub_count):
    count = lax.axis_size("layer")
    pairs = [(p, (p - offset * sub_count) % count) for p in range(count)]
    return lax.ppermute(value, "layer", pairs)


def after(value, *others):
    return lax.optimization_barrier((value, *others))[0]


def all_over_feat(value, turn=0):
    count = lax.axis_size("feat")
    blocks = [value] + [None] * (count - 1)
    for s in (range(1, count) if turn == 0 else reversed(range(1, count))):
        blocks[s] = over_feat(value, s)
    return blocks


def params(flops, bytes_accessed, scratch_mib):
    return dict(
        compiler_params=pltpu.CompilerParams(vmem_limit_bytes=scratch_mib * 1024 * 1024),
        cost_estimate=pl.CostEstimate(
            flops=flops, bytes_accessed=bytes_accessed, transcendentals=0
        ),
    )


def dot(left, right, contract):
    return lax.dot_general(
        left, right, ((contract[:1], contract[1:]), ((), ())), preferred_element_type=jnp.float32
    )


def span(index, size):
    return pl.ds(pl.multiple_of(index * size, size), size)


def fetch(*arrays):
    parts = [(number, start) for number, array in enumerate(arrays) for start in range(4)]

    def kernel(*refs):
        copies = []
        for place, (number, start) in enumerate(parts):
            source, target = refs[number], refs[len(arrays) + number]
            size = source.shape[-2] // 4
            here = (slice(None),) * (len(source.shape) - 2) + (pl.ds(start * size, size),)
            copies.append(
                pltpu.make_async_copy(source.at[here], target.at[here], refs[-1].at[place])
            )
        for copy in copies:
            copy.start()
        for copy in copies:
            copy.wait()

    total = sum(2 * array.size for array in arrays)
    return pl.pallas_call(
        kernel,
        in_specs=[in_hbm] * len(arrays),
        out_specs=[in_vmem] * len(arrays),
        out_shape=[jax.ShapeDtypeStruct(array.shape, array.dtype) for array in arrays],
        scratch_shapes=[pltpu.SemaphoreType.DMA((len(parts),))],
        name="fetch",
        **params(0, total, 14),
    )(*arrays)


def encode(info, rels, pieces, weights, partial, bias):
    feat_count, rows, cols = pieces[0].shape
    tok = feat_count * rows
    width = weights.shape[1]
    extra = [value for value in (partial, bias) if value is not None]

    def kernel(info_ref, *refs):
        piece_refs, weight_ref = refs[: len(pieces)], refs[len(pieces)]
        extra_refs, out_ref = refs[len(pieces) + 1 : -1], refs[-1]
        left = jnp.concatenate([ref[...].reshape(tok, cols) for ref in piece_refs], 1)
        for start in range(0, width, tile):
            here = slice(start, start + tile)
            right = jnp.concatenate(
                [weight_ref[span(info_ref[0] ^ rel, cols), here] for rel in rels], 0
            )
            total = dot(left, right, (1, 0))
            if partial is not None:
                total += extra_refs[0][:, here]
            if bias is None:
                out_ref[:, here] = total
            else:
                pre_act = total + extra_refs[-1][:, here]
                out_ref[0, :, here] = jnp.maximum(pre_act, 0.0).astype(jnp.bfloat16)
                out_ref[1, :, here] = jnp.where(pre_act > 0.0, 1.0, 0.0).astype(jnp.bfloat16)

    if bias is None:
        out_shape = jax.ShapeDtypeStruct((tok, width), jnp.float32)
    else:
        out_shape = jax.ShapeDtypeStruct((2, tok, width), jnp.bfloat16)
    return pl.pallas_call(
        kernel,
        in_specs=[in_smem] + [in_vmem] * (len(pieces) + 1 + len(extra)),
        out_specs=in_vmem,
        out_shape=out_shape,
        name="encode",
        **params(
            2 * len(pieces) * tok * cols * width, 2 * len(pieces) * cols * (tok + width), 4
        ),
    )(info, *pieces, weights, *extra)


def decode(info, features, weights, offset, groups, rows, cols):
    _, tok, width = features.shape
    count = weights.shape[2] // cols // 2

    def kernel(info_ref, feat_ref, weight_ref, *out_refs):
        left = feat_ref[0]
        even = info_ref[0] % 2 == 0
        step = min(tile, cols)
        for pair in range(count):
            piece = pair ^ (info_ref[0] // 2)
            for start in range(0, cols, step):
                low, high = (
                    dot(left, weight_ref[offset, :, base + start : base + start + step], (1, 0)).astype(
                        jnp.bfloat16
                    )
                    for base in (2 * pair * cols, (2 * pair + 1) * cols)
                )
                sides = (jnp.where(even, high, low), jnp.where(even, low, high))
                for side, product in enumerate(sides):
                    for number, group in enumerate(groups):
                        for place, block in enumerate(group):
                            out_refs[side * len(groups) + number][
                                piece, place, :, start : start + step
                            ] = product[block * rows : (block + 1) * rows]
    out_shape = [
        jax.ShapeDtypeStruct((count, len(group), rows, cols), jnp.bfloat16) for group in groups
    ] * 2
    result = pl.pallas_call(
        kernel,
        in_specs=[in_smem, in_vmem, in_vmem],
        out_specs=[in_vmem] * len(out_shape),
        out_shape=out_shape,
        name="decode",
        **params(4 * count * tok * cols * width, 4 * count * cols * width, 4),
    )(info, features, weights)
    return result[: len(groups)], result[len(groups) :]


def turned(value, count):
    _, tok, width = value.shape

    step = min(tile, width)

    def kernel(in_ref, out_ref):
        for piece in range(count):
            for start in range(0, width, step):
                out_ref[piece, start : start + step, :] = in_ref[
                    piece, :, start : start + step
                ].T

    return pl.pallas_call(
        kernel,
        in_specs=[in_vmem],
        out_specs=in_vmem,
        out_shape=jax.ShapeDtypeStruct((count, width, tok), value.dtype),
        name="turned",
        **params(0, 4 * count * tok * width, 4),
    )(value)


def tree_sum(values):
    while len(values) > 1:
        values = [values[i] + values[i + 1] for i in range(0, len(values), 2)]
    return values[0]


def backward_pair(info, rel, offset, own, other, turned_features, dec_weight, feature_grad, dec_grad):
    layers, width, depth = dec_weight.shape
    tok = turned_features.shape[1]
    cols = own[0].shape[2]
    first = feature_grad is None
    extra = [] if first else [feature_grad, dec_grad]
    inputs = [*own, *other]

    def kernel(info_ref, *refs):
        grad_refs = refs[: len(inputs)]
        feat_ref, weight_ref = refs[len(inputs) : len(inputs) + 2]
        out_ref, dec_ref, square_ref, held, sems = refs[-5:]
        columns = span((info_ref[0] ^ rel) // 2, 2 * cols)
        starts = range(0, width, tile)
        copies = [
            pltpu.make_async_copy(
                held.at[slice(start, start + tile)],
                dec_ref.at[offset, slice(start, start + tile), columns],
                sems.at[place],
            )
            for place, start in enumerate(starts)
        ]
        sides, sums = [], []
        for side in (grad_refs[: len(own)], grad_refs[len(own) :]):
            blocks = [ref[i] for ref in side for i in range(ref.shape[0])]
            totals = []
            for block in blocks:
                total = jnp.zeros((8, 128), jnp.float32)
                for row in range(0, block.shape[0], 8):
                    for col in range(0, cols, 128):
                        part = block[row : row + 8, col : col + 128].astype(jnp.float32)
                        total += part * part
                totals.append(total)
            sums.append(tree_sum(totals))
            sides.append(jnp.concatenate(blocks, 0))
        square_ref[...] = tree_sum(sums)

        def products():
            second = info_ref[0] % 2 > 0
            grad = jnp.concatenate(
                [jnp.where(second, sides[1], sides[0]), jnp.where(second, sides[0], sides[1])], 1
            )
            held[...] = dot(feat_ref[...], grad, (1, 0)).astype(jnp.bfloat16)
            for copy in copies:
                copy.start()
            for start in starts:
                here = slice(start, start + tile)
                product = dot(grad, weight_ref[offset, here, columns], (1, 1))
                if not first:
                    product += refs[len(inputs) + 2][:, here]
                out_ref[:, here] = product

        def nothing():
            held[...] = jnp.zeros_like(held)
            for copy in copies:
                copy.start()
            out_ref[...] = refs[len(inputs) + 2][...]

        if offset == 0:
            products()
        else:
            pl.when(info_ref[1] >= offset)(products)
            pl.when(info_ref[1] < offset)(nothing)
        for copy in copies:
            copy.wait()

    return pl.pallas_call(
        kernel,
        in_specs=[in_smem]
        + [in_vmem] * (len(inputs) + 2)
        + ([] if first else [in_vmem, in_hbm]),
        out_specs=[in_vmem, in_hbm, in_vmem],
        out_shape=[
            jax.ShapeDtypeStruct((tok, width), jnp.float32),
            jax.ShapeDtypeStruct((layers, width, depth), jnp.bfloat16),
            jax.ShapeDtypeStruct((8, 128), jnp.float32),
        ],
        scratch_shapes=[
            pltpu.VMEM((width, 2 * cols), jnp.bfloat16),
            pltpu.SemaphoreType.DMA((width // tile,)),
        ],
        input_output_aliases={} if first else {len(inputs) + 3: 0, len(inputs) + 4: 1},
        name="backward_pair",
        **params(tok * cols, tok * cols, 12),
    )(info, *inputs, turned_features, dec_weight, *extra)


def encoder_grad(info, rels, turned_tokens, features, feature_grad, squares, scale):
    count, cols, tok = turned_tokens[0].shape
    width = features.shape[2]
    pieces = len(turned_tokens) * count

    def kernel(info_ref, *refs):
        token_refs = refs[: len(turned_tokens)]
        mask_ref, grad_ref = refs[len(turned_tokens) : len(turned_tokens) + 2]
        square_refs = refs[len(turned_tokens) + 2 : -6]
        enc_ref, bias_ref, mean_ref, preact, held, sems = refs[-6:]
        mean_ref[...] = scale * jnp.sum(
            tree_sum([ref[...] for ref in square_refs]), (0, 1), keepdims=True
        )
        for start in range(0, width, tile):
            here = slice(start, start + tile)
            kept = jnp.where(mask_ref[1, :, here] > 0.0, grad_ref[:, here], 0.0).astype(jnp.bfloat16)
            preact[:, here] = kept
            bias_ref[:, here] = jnp.sum(kept.astype(jnp.float32), 0, keepdims=True)
        copies = []
        for first in range(0, pieces, 2):
            both = [token_refs[piece][0] for piece in range(first, first + 2)]
            product = dot(jnp.concatenate(both, 0), preact[...], (1, 0)).astype(jnp.bfloat16)
            for piece in range(first, first + 2):
                held[piece] = product[(piece - first) * cols : (piece - first + 1) * cols]
                size = cols // 4
                for part in range(4):
                    row = (info_ref[0] ^ rels[piece]) * 4 + part
                    copy = pltpu.make_async_copy(
                        held.at[piece, pl.ds(part * size, size)],
                        enc_ref.at[span(row, size)],
                        sems.at[4 * piece + part],
                    )
                    copy.start()
                    copies.append(copy)
        for copy in copies:
            copy.wait()

    return pl.pallas_call(
        kernel,
        in_specs=[in_smem] + [in_vmem] * (len(turned_tokens) + 2 + len(squares)),
        out_specs=[in_hbm, in_vmem, in_vmem],
        out_shape=[
            jax.ShapeDtypeStruct((pieces * cols, width), jnp.bfloat16),
            jax.ShapeDtypeStruct((1, width), jnp.float32),
            jax.ShapeDtypeStruct((1, 1), jnp.float32),
        ],
        scratch_shapes=[
            pltpu.VMEM((tok, width), jnp.bfloat16),
            pltpu.VMEM((pieces, cols, width), jnp.bfloat16),
            pltpu.SemaphoreType.DMA((4 * pieces,)),
        ],
        name="encoder_grad",
        **params(
            2 * pieces * tok * cols * width, 2 * pieces * cols * (tok + width) + 6 * tok * width, 14
        ),
    )(info, *turned_tokens, features, feature_grad, *squares)


def add_pair(left, right):
    return (left.astype(jnp.float32) + right.astype(jnp.float32)).astype(jnp.bfloat16)


def on_device(tokens_in, targets, enc_weight, enc_bias, dec_weight):
    layers, width, depth = dec_weight.shape
    feat_count = lax.axis_size("feat")
    sub_count = lax.axis_size("layer") // layers
    position = lax.axis_index("layer")
    layer = position // sub_count
    rows, cols = tokens_in.shape
    tok = feat_count * rows
    bit_count = sub_count.bit_length() - 1
    groups = [list(range(feat_count // 2)), list(range(feat_count // 2, feat_count))]

    info = jnp.stack([position % sub_count, layers - 1 - layer]).astype(jnp.int32)
    real = [layer >= k for k in range(layers)]
    tokens_in, info, *real = lax.optimization_barrier((tokens_in, info, *real))
    enc_weight = pltpu.with_memory_space_constraint(enc_weight, pltpu.HBM)
    dec_weight = pltpu.with_memory_space_constraint(dec_weight, pltpu.HBM)

    order = [rel for pair in range(0, sub_count, 2) for rel in (pair, pair ^ 1)]
    held = {rel: [None] * feat_count for rel in order[::2]}
    held[0] = all_over_feat(tokens_in, 0)
    enc_held, dec_held = fetch(enc_weight, after(dec_weight, held[0][1]))
    for s in range(feat_count):
        known = [0]
        for bit_level in range(bit_count - 1, 0, -1):
            for rel in known:
                value = after(held[rel][s], dec_held) if s > 1 else held[rel][s]
                held[rel ^ 2**bit_level][s] = over_members(value, bit_level)
            known += [rel ^ 2**bit_level for rel in known]
    early = [
        held[rel][s] for rel in order[2::2] for s in range(feat_count) if 2 * s != feat_count
    ]
    tokens = {0: after(jnp.stack(held[0], 0), enc_held, *early)}
    tokens[1] = over_members(tokens[0], 0)
    partial = encode(info, [0, 1], [tokens[0], tokens[1]], enc_held, None, None)
    for rel in order[2::2]:
        tokens[rel] = jnp.stack([after(block, partial) for block in held[rel]], 0)
        tokens[rel ^ 1] = over_members(tokens[rel], 0)
    for rel in order[2:-1]:
        partial = encode(info, [rel], [tokens[rel]], enc_held, partial, None)
    features = encode(info, order[-1:], [tokens[order[-1]]], enc_held, partial, enc_bias[None])

    current, source = {}, features
    for k in reversed(range(layers)):
        sent, kept = decode(info, source, dec_held, k, groups, rows, cols)
        for place in reversed(range(len(groups))):
            current[place, k] = add_pair(kept[place], over_members(sent[place], 0))
        source = after(features, kept[-1])
    turns = sorted(current, reverse=True)
    joined = {}
    for bit_level in range(1, bit_count):
        halves = {}
        for turn, value in current.items():
            split = value.reshape((value.shape[0] // 2, 2) + value.shape[1:])
            halves[turn] = (split[:, 0], split[:, 1])
        if bit_level == bit_count - 1:
            for k in range(1, layers):
                joined[k], sent = halves.pop((0, k))
                sent = to_layer(sent, k, sub_count, real)
                ahead = sent
                halves[0, 0] = (halves[0, 0][0], add_pair(halves[0, 0][1], sent))
        turns = [turn for turn in turns if turn in halves]
        received, operands = [], []
        for turn in turns:
            operand = halves[turn][1]
            if len(received) > 1:
                operand = after(operand, received[-2], operands[-1])
            operands.append(operand)
            received.append(over_members(operand, bit_level))
        for place, turn in enumerate(turns):
            arrived = after(received[place], *operands[place + 1 :][:1])
            if bit_level < bit_count - 1:
                current[turn] = add_pair(halves[turn][0], arrived)
            else:
                current[turn] = (halves[turn][0], arrived)
    blocks, operands = [None] * feat_count, []
    for place in reversed(range(len(groups))):
        total = sum(part.astype(jnp.float32) for part in current[place, 0])
        for k in range(1, layers):
            if place > 0:
                value = add_pair(*current[place, k])
                value = after(value, ahead) if place == 1 else value
                moved = to_layer(value, k, sub_count, real)
            else:
                moved = to_layer(after(joined[k], *operands[:1]), k, sub_count, real)
            total = total + moved.astype(jnp.float32)
        for spot, block in enumerate(groups[place]):
            if block == 0:
                rebuilt = total[0, spot]
            else:
                operands.append(total[0, spot].astype(jnp.bfloat16))
                blocks[block] = over_feat(operands[-1], block)
    for block in reversed(blocks[1:]):
        rebuilt = rebuilt + block.astype(jnp.float32)
    turned_features = turned(source, 1)[0]
    turned_tokens = [
        turned(after(tokens[rel], turned_features).reshape(1, tok, cols), 1) for rel in order
    ]
    recon_error = rebuilt - after(targets, turned_features, *turned_tokens).astype(jnp.float32)
    scaled = (loss_scale / tok * recon_error).astype(jnp.bfloat16)

    blocks = all_over_feat(scaled, 0)
    stages = [[0]]
    for level in range(bit_count - 1, 0, -1):
        known = [rel for stage in stages for rel in stage]
        stages.append([rel ^ 2**level for rel in known])
    spans = [[s] for s in range(min(2, feat_count))]
    spans += [list(range(2, feat_count))] if feat_count > 2 else []
    groups_of = {(0, k): [None] * len(spans) for k in range(layers)}
    early, last = [], len(spans) - 1
    for place, group in enumerate(spans):
        stacked = jnp.stack([blocks[s] for s in group], 0)
        groups_of[0, 0][place] = stacked
        for k in range(1, layers):
            groups_of[0, k][place] = from_layer(stacked, k, sub_count)
        known = [0]
        for level in range(bit_count - 1, 0, -1):
            for rel in known:
                other = rel ^ 2**level
                for k in range(layers):
                    if k == 0 or place < last:
                        part = over_members(groups_of[rel, k][place], level)
                    else:
                        part = from_layer(groups_of[other, 0][place], k, sub_count)
                    groups_of.setdefault((other, k), [None] * len(spans))[place] = part
            known += [rel ^ 2**level for rel in known]
        if place == last - 1:
            early = [part for parts in groups_of.values() for part in parts if part is not None]
            early.pop()

    feature_grad, dec_grad, squares = None, None, {}
    for k in range(layers):
        for rel in [rel for stage in stages for rel in stage]:
            parts = groups_of[rel, k]
            if feature_grad is None:
                parts = [after(parts[0], groups_of[2, 0][0], groups_of[0, 1][0], groups_of[2, 1][0], groups_of[2, 0][1], groups_of[0, 1][1])] + parts[1:]
            elif (rel > 0 and k == 0) or (rel > 0 and k > 0):
                parts = [after(part, feature_grad) for part in parts]
            feature_grad, dec_grad, squares[k, rel] = backward_pair(
                info,
                rel,
                k,
                parts,
                [over_members(part, 0) for part in parts],
                turned_features,
                dec_held,
                feature_grad,
                dec_grad,
            )
    scale = (tok / loss_scale) ** 2 / (layers * tok * depth)
    enc_grad, bias_grad, mean_square = encoder_grad(
        info,
        order,
        turned_tokens,
        features,
        feature_grad,
        [squares[key] for key in sorted(squares)],
        scale,
    )
    return (recon_error, mean_square[0, 0], enc_grad, bias_grad[0], dec_grad)


def solution(mesh):
    placed = (
        P("feat", "layer"),
        P("feat", "layer"),
        P(None, ("layer", "feat")),
        P(("layer", "feat")),
        P(None, ("layer", "feat"), None),
    )
    return jax.shard_map(
        on_device,
        mesh=mesh,
        in_specs=placed,
        out_specs=(
            P("feat", "layer"),
            P(),
            P(None, ("layer", "feat")),
            P(("layer", "feat")),
            P(None, ("layer", "feat"), None),
        ),
        check_vma=False,
    )
```

```python
import jax
import jax.numpy as jnp
from jax import lax
from jax.experimental import pallas as pl
from jax.experimental.pallas import tpu as pltpu
from jax.sharding import PartitionSpec as P

loss_scale = 64.0
tile = 512
in_vmem = pl.BlockSpec(memory_space=pltpu.VMEM)
in_smem = pl.BlockSpec(memory_space=pltpu.SMEM)
in_hbm = pl.BlockSpec(memory_space=pltpu.HBM)


def over_feat(value, mask):
    pairs = [(source, source ^ mask) for source in range(lax.axis_size("feat"))]
    return lax.ppermute(value, "feat", pairs)


def over_members(value, bit_level):
    mask = 2**bit_level
    pairs = [(source, source ^ mask) for source in range(lax.axis_size("layer"))]
    return lax.ppermute(value, "layer", pairs)


def to_layer(value, offset, sub_count, real):
    count = lax.axis_size("layer")
    pairs = [(p, (p + offset * sub_count) % count) for p in range(count)]
    moved = lax.ppermute(value, "layer", pairs)
    return jnp.where(real[offset], moved, jnp.zeros_like(moved))


def from_layer(value, offset, sub_count):
    count = lax.axis_size("layer")
    pairs = [(p, (p - offset * sub_count) % count) for p in range(count)]
    return lax.ppermute(value, "layer", pairs)


def after(value, *others):
    return lax.optimization_barrier((value, *others))[0]


def all_over_feat(value, turn=0):
    count = lax.axis_size("feat")
    blocks = [value] + [None] * (count - 1)
    for s in (range(1, count) if turn == 0 else reversed(range(1, count))):
        blocks[s] = over_feat(value, s)
    return blocks


def params(flops, bytes_accessed, scratch_mib):
    return dict(
        compiler_params=pltpu.CompilerParams(vmem_limit_bytes=scratch_mib * 1024 * 1024),
        cost_estimate=pl.CostEstimate(
            flops=flops, bytes_accessed=bytes_accessed, transcendentals=0
        ),
    )


def dot(left, right, contract):
    return lax.dot_general(
        left, right, ((contract[:1], contract[1:]), ((), ())), preferred_element_type=jnp.float32
    )


def span(index, size):
    return pl.ds(pl.multiple_of(index * size, size), size)


def fetch(*arrays):
    parts = [(number, start) for number, array in enumerate(arrays) for start in range(4)]

    def kernel(*refs):
        copies = []
        for place, (number, start) in enumerate(parts):
            source, target = refs[number], refs[len(arrays) + number]
            size = source.shape[-2] // 4
            here = (slice(None),) * (len(source.shape) - 2) + (pl.ds(start * size, size),)
            copies.append(
                pltpu.make_async_copy(source.at[here], target.at[here], refs[-1].at[place])
            )
        for copy in copies:
            copy.start()
        for copy in copies:
            copy.wait()

    total = sum(2 * array.size for array in arrays)
    return pl.pallas_call(
        kernel,
        in_specs=[in_hbm] * len(arrays),
        out_specs=[in_vmem] * len(arrays),
        out_shape=[jax.ShapeDtypeStruct(array.shape, array.dtype) for array in arrays],
        scratch_shapes=[pltpu.SemaphoreType.DMA((len(parts),))],
        name="fetch",
        **params(0, total, 14),
    )(*arrays)


def encode(info, rels, pieces, weights, partial, bias):
    feat_count, rows, cols = pieces[0].shape
    tok = feat_count * rows
    width = weights.shape[1]
    extra = [value for value in (partial, bias) if value is not None]

    def kernel(info_ref, *refs):
        piece_refs, weight_ref = refs[: len(pieces)], refs[len(pieces)]
        extra_refs, out_ref = refs[len(pieces) + 1 : -1], refs[-1]
        left = jnp.concatenate([ref[...].reshape(tok, cols) for ref in piece_refs], 1)
        for start in range(0, width, tile):
            here = slice(start, start + tile)
            right = jnp.concatenate(
                [weight_ref[span(info_ref[0] ^ rel, cols), here] for rel in rels], 0
            )
            total = dot(left, right, (1, 0))
            if partial is not None:
                total += extra_refs[0][:, here]
            if bias is None:
                out_ref[:, here] = total
            else:
                pre_act = total + extra_refs[-1][:, here]
                out_ref[0, :, here] = jnp.maximum(pre_act, 0.0).astype(jnp.bfloat16)
                out_ref[1, :, here] = jnp.where(pre_act > 0.0, 1.0, 0.0).astype(jnp.bfloat16)

    if bias is None:
        out_shape = jax.ShapeDtypeStruct((tok, width), jnp.float32)
    else:
        out_shape = jax.ShapeDtypeStruct((2, tok, width), jnp.bfloat16)
    return pl.pallas_call(
        kernel,
        in_specs=[in_smem] + [in_vmem] * (len(pieces) + 1 + len(extra)),
        out_specs=in_vmem,
        out_shape=out_shape,
        name="encode",
        **params(
            2 * len(pieces) * tok * cols * width, 2 * len(pieces) * cols * (tok + width), 4
        ),
    )(info, *pieces, weights, *extra)


def decode(info, features, weights, offset, groups, rows, cols):
    _, tok, width = features.shape
    count = weights.shape[2] // cols // 2

    def kernel(info_ref, feat_ref, weight_ref, *out_refs):
        left = feat_ref[0]
        even = info_ref[0] % 2 == 0
        step = min(tile, cols)
        for pair in range(count):
            piece = pair ^ (info_ref[0] // 2)
            for start in range(0, cols, step):
                low, high = (
                    dot(left, weight_ref[offset, :, base + start : base + start + step], (1, 0)).astype(
                        jnp.bfloat16
                    )
                    for base in (2 * pair * cols, (2 * pair + 1) * cols)
                )
                sides = (jnp.where(even, high, low), jnp.where(even, low, high))
                for side, product in enumerate(sides):
                    for number, group in enumerate(groups):
                        for place, block in enumerate(group):
                            out_refs[side * len(groups) + number][
                                piece, place, :, start : start + step
                            ] = product[block * rows : (block + 1) * rows]
    out_shape = [
        jax.ShapeDtypeStruct((count, len(group), rows, cols), jnp.bfloat16) for group in groups
    ] * 2
    result = pl.pallas_call(
        kernel,
        in_specs=[in_smem, in_vmem, in_vmem],
        out_specs=[in_vmem] * len(out_shape),
        out_shape=out_shape,
        name="decode",
        **params(4 * count * tok * cols * width, 4 * count * cols * width, 4),
    )(info, features, weights)
    return result[: len(groups)], result[len(groups) :]


def turned(value, count):
    _, tok, width = value.shape

    step = min(tile, width)

    def kernel(in_ref, out_ref):
        for piece in range(count):
            for start in range(0, width, step):
                out_ref[piece, start : start + step, :] = in_ref[
                    piece, :, start : start + step
                ].T

    return pl.pallas_call(
        kernel,
        in_specs=[in_vmem],
        out_specs=in_vmem,
        out_shape=jax.ShapeDtypeStruct((count, width, tok), value.dtype),
        name="turned",
        **params(0, 4 * count * tok * width, 4),
    )(value)


def tree_sum(values):
    while len(values) > 1:
        values = [values[i] + values[i + 1] for i in range(0, len(values), 2)]
    return values[0]


def backward_pair(info, rel, offset, own, other, turned_features, dec_weight, feature_grad, dec_grad):
    layers, width, depth = dec_weight.shape
    tok = turned_features.shape[1]
    cols = own[0].shape[2]
    first = feature_grad is None
    extra = [] if first else [feature_grad, dec_grad]
    inputs = [*own, *other]

    def kernel(info_ref, *refs):
        grad_refs = refs[: len(inputs)]
        feat_ref, weight_ref = refs[len(inputs) : len(inputs) + 2]
        out_ref, dec_ref, square_ref, held, sems = refs[-5:]
        columns = span((info_ref[0] ^ rel) // 2, 2 * cols)
        starts = range(0, width, tile)
        copies = [
            pltpu.make_async_copy(
                held.at[slice(start, start + tile)],
                dec_ref.at[offset, slice(start, start + tile), columns],
                sems.at[place],
            )
            for place, start in enumerate(starts)
        ]
        sides, sums = [], []
        for side in (grad_refs[: len(own)], grad_refs[len(own) :]):
            blocks = [ref[i] for ref in side for i in range(ref.shape[0])]
            totals = []
            for block in blocks:
                total = jnp.zeros((8, 128), jnp.float32)
                for row in range(0, block.shape[0], 8):
                    for col in range(0, cols, 128):
                        part = block[row : row + 8, col : col + 128].astype(jnp.float32)
                        total += part * part
                totals.append(total)
            sums.append(tree_sum(totals))
            sides.append(jnp.concatenate(blocks, 0))
        square_ref[...] = tree_sum(sums)

        def products():
            second = info_ref[0] % 2 > 0
            grad = jnp.concatenate(
                [jnp.where(second, sides[1], sides[0]), jnp.where(second, sides[0], sides[1])], 1
            )
            for copy, start in zip(copies, starts):
                here = slice(start, start + tile)
                held[here] = dot(feat_ref[here], grad, (1, 0)).astype(jnp.bfloat16)
                copy.start()
            for start in starts:
                here = slice(start, start + tile)
                product = dot(grad, weight_ref[offset, here, columns], (1, 1))
                if not first:
                    product += refs[len(inputs) + 2][:, here]
                out_ref[:, here] = product

        def nothing():
            held[...] = jnp.zeros_like(held)
            for copy in copies:
                copy.start()
            out_ref[...] = refs[len(inputs) + 2][...]

        if offset == 0:
            products()
        else:
            pl.when(info_ref[1] >= offset)(products)
            pl.when(info_ref[1] < offset)(nothing)
        for copy in copies:
            copy.wait()

    return pl.pallas_call(
        kernel,
        in_specs=[in_smem]
        + [in_vmem] * (len(inputs) + 2)
        + ([] if first else [in_vmem, in_hbm]),
        out_specs=[in_vmem, in_hbm, in_vmem],
        out_shape=[
            jax.ShapeDtypeStruct((tok, width), jnp.float32),
            jax.ShapeDtypeStruct((layers, width, depth), jnp.bfloat16),
            jax.ShapeDtypeStruct((8, 128), jnp.float32),
        ],
        scratch_shapes=[
            pltpu.VMEM((width, 2 * cols), jnp.bfloat16),
            pltpu.SemaphoreType.DMA((width // tile,)),
        ],
        input_output_aliases={} if first else {len(inputs) + 3: 0, len(inputs) + 4: 1},
        name="backward_pair",
        **params(tok * cols, tok * cols, 8),
    )(info, *inputs, turned_features, dec_weight, *extra)


def encoder_grad(info, rels, turned_tokens, features, feature_grad, squares, scale):
    count, cols, tok = turned_tokens[0].shape
    width = features.shape[2]
    pieces = len(turned_tokens) * count

    def kernel(info_ref, *refs):
        token_refs = refs[: len(turned_tokens)]
        mask_ref, grad_ref = refs[len(turned_tokens) : len(turned_tokens) + 2]
        square_refs = refs[len(turned_tokens) + 2 : -6]
        enc_ref, bias_ref, mean_ref, preact, held, sems = refs[-6:]
        mean_ref[...] = scale * jnp.sum(
            tree_sum([ref[...] for ref in square_refs]), (0, 1), keepdims=True
        )
        for start in range(0, width, tile):
            here = slice(start, start + tile)
            kept = jnp.where(mask_ref[1, :, here] > 0.0, grad_ref[:, here], 0.0).astype(jnp.bfloat16)
            preact[:, here] = kept
            bias_ref[:, here] = jnp.sum(kept.astype(jnp.float32), 0, keepdims=True)
        copies = []
        for piece in range(pieces):
            held[piece] = dot(
                token_refs[piece // count][piece % count], preact[...], (1, 0)
            ).astype(jnp.bfloat16)
            size = cols // 4
            for part in range(4):
                row = (info_ref[0] ^ rels[piece]) * 4 + part
                copy = pltpu.make_async_copy(
                    held.at[piece, pl.ds(part * size, size)],
                    enc_ref.at[span(row, size)],
                    sems.at[4 * piece + part],
                )
                copy.start()
                copies.append(copy)
        for copy in copies:
            copy.wait()

    return pl.pallas_call(
        kernel,
        in_specs=[in_smem] + [in_vmem] * (len(turned_tokens) + 2 + len(squares)),
        out_specs=[in_hbm, in_vmem, in_vmem],
        out_shape=[
            jax.ShapeDtypeStruct((pieces * cols, width), jnp.bfloat16),
            jax.ShapeDtypeStruct((1, width), jnp.float32),
            jax.ShapeDtypeStruct((1, 1), jnp.float32),
        ],
        scratch_shapes=[
            pltpu.VMEM((tok, width), jnp.bfloat16),
            pltpu.VMEM((pieces, cols, width), jnp.bfloat16),
            pltpu.SemaphoreType.DMA((4 * pieces,)),
        ],
        name="encoder_grad",
        **params(
            2 * pieces * tok * cols * width, 2 * pieces * cols * (tok + width) + 6 * tok * width, 10
        ),
    )(info, *turned_tokens, features, feature_grad, *squares)


def add_pair(left, right):
    return (left.astype(jnp.float32) + right.astype(jnp.float32)).astype(jnp.bfloat16)


def on_device(tokens_in, targets, enc_weight, enc_bias, dec_weight):
    layers, width, depth = dec_weight.shape
    feat_count = lax.axis_size("feat")
    sub_count = lax.axis_size("layer") // layers
    position = lax.axis_index("layer")
    layer = position // sub_count
    rows, cols = tokens_in.shape
    tok = feat_count * rows
    bit_count = sub_count.bit_length() - 1
    groups = [list(range(feat_count // 2)), list(range(feat_count // 2, feat_count))]

    info = jnp.stack([position % sub_count, layers - 1 - layer]).astype(jnp.int32)
    real = [layer >= k for k in range(layers)]
    tokens_in, info, *real = lax.optimization_barrier((tokens_in, info, *real))
    enc_weight = pltpu.with_memory_space_constraint(enc_weight, pltpu.HBM)
    dec_weight = pltpu.with_memory_space_constraint(dec_weight, pltpu.HBM)

    order = [rel for pair in range(0, sub_count, 2) for rel in (pair, pair ^ 1)]
    held = {rel: [None] * feat_count for rel in order[::2]}
    held[0] = all_over_feat(tokens_in, 0)
    enc_held, dec_held = fetch(enc_weight, after(dec_weight, held[0][1]))
    for s in range(feat_count):
        known = [0]
        for bit_level in range(bit_count - 1, 0, -1):
            for rel in known:
                value = held[rel][s]
                if s > 1:
                    value = after(value, dec_held, held[rel ^ 2**bit_level][1])
                held[rel ^ 2**bit_level][s] = over_members(value, bit_level)
            known += [rel ^ 2**bit_level for rel in known]
    early = [
        held[rel][s] for rel in order[2::2] for s in range(feat_count) if 2 * s != feat_count
    ]
    tokens = {0: after(jnp.stack(held[0], 0), enc_held, *early)}
    tokens[1] = over_members(tokens[0], 0)
    partial = encode(info, [0, 1], [tokens[0], tokens[1]], enc_held, None, None)
    for rel in order[2::2]:
        tokens[rel] = jnp.stack([after(block, partial) for block in held[rel]], 0)
        tokens[rel ^ 1] = over_members(tokens[rel], 0)
    for rel in order[2:-1]:
        partial = encode(info, [rel], [tokens[rel]], enc_held, partial, None)
    features = encode(info, order[-1:], [tokens[order[-1]]], enc_held, partial, enc_bias[None])

    current, source = {}, features
    for k in reversed(range(layers)):
        sent, kept = decode(info, source, dec_held, k, groups, rows, cols)
        for place in reversed(range(len(groups))):
            current[place, k] = add_pair(kept[place], over_members(sent[place], 0))
        source = after(features, kept[-1])
    turns = sorted(current, reverse=True)
    joined = {}
    for bit_level in range(1, bit_count):
        halves = {}
        for turn, value in current.items():
            split = value.reshape((value.shape[0] // 2, 2) + value.shape[1:])
            halves[turn] = (split[:, 0], split[:, 1])
        if bit_level == bit_count - 1:
            for k in range(1, layers):
                joined[k], sent = halves.pop((0, k))
                sent = to_layer(sent, k, sub_count, real)
                ahead = sent
                halves[0, 0] = (halves[0, 0][0], add_pair(halves[0, 0][1], sent))
        turns = [turn for turn in turns if turn in halves]
        received, operands = [], []
        for turn in turns:
            operand = halves[turn][1]
            if len(received) > 1:
                operand = after(operand, received[-2], operands[-1])
            operands.append(operand)
            received.append(over_members(operand, bit_level))
        for place, turn in enumerate(turns):
            arrived = after(received[place], *operands[place + 1 :][:1])
            if bit_level < bit_count - 1:
                current[turn] = add_pair(halves[turn][0], arrived)
            else:
                current[turn] = (halves[turn][0], arrived)
    blocks, operands = [None] * feat_count, []
    for place in reversed(range(len(groups))):
        total = sum(part.astype(jnp.float32) for part in current[place, 0])
        for k in range(1, layers):
            if place > 0:
                value = add_pair(*current[place, k])
                value = after(value, ahead) if place == 1 else value
                moved = to_layer(value, k, sub_count, real)
            else:
                moved = to_layer(after(joined[k], *operands[:1]), k, sub_count, real)
            total = total + moved.astype(jnp.float32)
        for spot, block in enumerate(groups[place]):
            if block == 0:
                rebuilt = total[0, spot]
            else:
                operands.append(total[0, spot].astype(jnp.bfloat16))
                blocks[block] = over_feat(operands[-1], block)
    for block in reversed(blocks[1:]):
        rebuilt = rebuilt + block.astype(jnp.float32)
    turned_features = turned(source, 1)[0]
    turned_tokens = [
        turned(after(tokens[rel], turned_features).reshape(1, tok, cols), 1) for rel in order
    ]
    recon_error = rebuilt - after(targets, turned_features, *turned_tokens).astype(jnp.float32)
    scaled = (loss_scale / tok * recon_error).astype(jnp.bfloat16)

    blocks = all_over_feat(scaled, 0)
    stages = [[0]]
    for level in range(bit_count - 1, 0, -1):
        known = [rel for stage in stages for rel in stage]
        stages.append([rel ^ 2**level for rel in known])
    spans = [[s] for s in range(min(2, feat_count))]
    spans += [list(range(2, feat_count))] if feat_count > 2 else []
    groups_of = {(0, k): [None] * len(spans) for k in range(layers)}
    early, last = [], len(spans) - 1
    for place, group in enumerate(spans):
        stacked = jnp.stack([blocks[s] for s in group], 0)
        groups_of[0, 0][place] = stacked
        for k in range(1, layers):
            groups_of[0, k][place] = from_layer(stacked, k, sub_count)
        known = [0]
        for level in range(bit_count - 1, 0, -1):
            for rel in known:
                other = rel ^ 2**level
                for k in range(layers):
                    if k == 0 or place < last:
                        part = over_members(groups_of[rel, k][place], level)
                    else:
                        part = from_layer(groups_of[other, 0][place], k, sub_count)
                    groups_of.setdefault((other, k), [None] * len(spans))[place] = part
            known += [rel ^ 2**level for rel in known]
        if place == last - 1:
            early = [part for parts in groups_of.values() for part in parts if part is not None]
            early.pop()

    feature_grad, dec_grad, squares = None, None, {}
    for k in range(layers):
        for rel in [rel for stage in stages for rel in stage]:
            parts = groups_of[rel, k]
            if feature_grad is None:
                parts = [after(parts[0], groups_of[2, 0][0], groups_of[0, 1][0], groups_of[2, 1][0], groups_of[2, 0][1], groups_of[0, 1][1])] + parts[1:]
            elif (rel > 0 and k == 0) or (rel > 0 and k > 0):
                parts = [after(part, feature_grad) for part in parts]
            feature_grad, dec_grad, squares[k, rel] = backward_pair(
                info,
                rel,
                k,
                parts,
                [over_members(part, 0) for part in parts],
                turned_features,
                dec_held,
                feature_grad,
                dec_grad,
            )
    scale = (tok / loss_scale) ** 2 / (layers * tok * depth)
    enc_grad, bias_grad, mean_square = encoder_grad(
        info,
        order,
        turned_tokens,
        features,
        feature_grad,
        [squares[key] for key in sorted(squares)],
        scale,
    )
    return (recon_error, mean_square[0, 0], enc_grad, bias_grad[0], dec_grad)


def solution(mesh):
    placed = (
        P("feat", "layer"),
        P("feat", "layer"),
        P(None, ("layer", "feat")),
        P(("layer", "feat")),
        P(None, ("layer", "feat"), None),
    )
    return jax.shard_map(
        on_device,
        mesh=mesh,
        in_specs=placed,
        out_specs=(
            P("feat", "layer"),
            P(),
            P(None, ("layer", "feat")),
            P(("layer", "feat")),
            P(None, ("layer", "feat"), None),
        ),
        check_vma=False,
    )
```
